128 devices in a mesh: gx: 8 (over x_lo, y), gy: 16 (over x_hi, z, core).
Axes of the slice: x: 4 (x_hi: 2, x_lo: 2; x = x_hi * 2 + x_lo), y: 4, z: 4, core: 2. Of those that a mesh axis runs over, the one named last changes fastest.
Arguments:
- adjoint: float32 [2, 16, 256, 2048], P(None, None, 'gx', 'gy'), may hold values from -6 to 6
- base_flow: bfloat16 [2, 16, 256, 2048], P(None, None, 'gx', 'gy'), may hold values from -3 to 3
- slot_cell: int32 [8, 16, 3, 8, 128], P('gx', 'gy'), may hold values from 0 to 3708, as said below
- slot_marker: int32 [8, 16, 3, 8, 128], P('gx', 'gy'), may hold values from 0 to 4095, as said below
- slot_count: int32 [8, 16, 3, 8], P('gx', 'gy'), may hold values from 0 to 128, as said below
- slot_weight: float32 [8, 16, 3, 8, 16, 128], P('gx', 'gy'), may hold values from 0.02 to 0.12
- marker_source: float32 [2, 16, 64, 512], P(None, 'gx', 'gy'), may hold values from -6 to 6
Outputs:
- adjoint_out: float32 [2, 16, 256, 2048], P(None, None, 'gx', 'gy')
- marker_force: float32 [2, 16, 64, 512], P(None, 'gx', 'gy')
The draws below stay inside these ranges and needn't reach their ends.
Inputs may be any that keep to these rules, and one draw needn't show every extreme that they name: `slot_cell`: i * 128 + j with i <= 28 and j <= 124; almost every cell lies near its marker's place on the section's circle. `slot_marker`: a marker row of the owner. `slot_count`: zero where b + g - 1 lies outside 0 to 15; every tile fills all 128 slots to some owner of its own column of owners.
All inputs are finite; a program needn't handle non-finite values.
Results may differ from the reference program's by a relative error of at most 0.002.
Values may be sent and summed in bfloat16 or wider, within the bound.
No kernel may reach another device: no remote copies, remote signals or barrier semaphores. Data moves between devices by JAX's collectives and lax.ppermute only.
A program may use at most 128 MiB of HBM per device.

```python
import jax
import jax.numpy as jnp

CX = 32
CY = 128
PLANES = 16
RISER_DEV = 4
MARKERS = 512
CAP = 128
SUBSTEPS = 3
SWEEPS = 8
RISERS = 64
NX = 256
NY = 2048
N_GX = 8
N_GY = 16


def single_slot(shape, slot_no):
    spot = jnp.zeros(shape, jnp.int32)
    spot = spot + jnp.arange(shape[0], dtype=jnp.int32)[:, None, None, None, None]
    spot = spot + jnp.arange(shape[1], dtype=jnp.int32)[None, :, None, None, None]
    spot = spot + jnp.abs(jnp.arange(3, dtype=jnp.int32) - 1)[None, None, :, None, None]
    spot = spot + jnp.arange(shape[3], dtype=jnp.int32)[None, None, None, :, None]
    spot = spot + jnp.abs(jnp.arange(shape[4], dtype=jnp.int32) - slot_no)[None, None, None, None, :]
    return spot == 0


def marker_parts(key):
    shape = (N_GX, N_GY, 3, N_GX, CAP)
    plane_key, riser_key, place_key = jax.random.split(key, 3)
    plane = jax.random.randint(plane_key, shape, 0, PLANES // N_GX)
    riser = jax.random.randint(riser_key, shape, 0, RISER_DEV)
    spread = jax.random.randint(place_key, shape, 0, MARKERS)
    side_no = jnp.arange(3, dtype=jnp.int32)[None, None, :, None, None]
    narrow = spread % (MARKERS // 4) - MARKERS // 8
    marker = jnp.where(side_no == 1, spread, jnp.where(side_no == 0, narrow % MARKERS, narrow + MARKERS // 2))
    top_slot = single_slot(shape, 1)
    plane = jnp.where(top_slot, PLANES // N_GX - 1, plane)
    riser = jnp.where(top_slot, RISER_DEV - 1, riser)
    marker = jnp.where(top_slot, MARKERS - 1, marker)
    return (plane.astype(jnp.int32), riser.astype(jnp.int32), marker.astype(jnp.int32), side_no)


def draw_slot_cell(key, part):
    plane, riser, marker, side_no = marker_parts(key)
    place = marker % MARKERS
    turned = (marker - MARKERS // 4) % MARKERS
    across = CY // 2 * (2 * jnp.abs(2 * place - MARKERS) - MARKERS) // MARKERS
    along = (CX // 2 - 2) * (2 * jnp.abs(2 * turned - MARKERS) - MARKERS) // MARKERS
    column = (side_no - 1) * CY + (2 * riser + 1) * CY // (2 * RISER_DEV) + across
    row = CX // 2 - 2 + along
    col_start = jnp.clip(column, 0, CY - 4)
    row_start = jnp.clip(row, 0, CX - 4)
    cells = row_start * CY + col_start
    corner_slot = single_slot(cells.shape, 0)
    cells = jnp.where(corner_slot, (CX - 4) * CY + CY - 4, cells)
    return cells.astype(jnp.int32)


def draw_slot_marker(key, part):
    plane, riser, marker, side_no = marker_parts(key)
    return (plane * (RISER_DEV * MARKERS) + riser * MARKERS + marker).astype(jnp.int32)


def draw_slot_count(key, part):
    key = jax.random.fold_in(key, 13)
    level_key, count_key, full_key = jax.random.split(key, 3)
    shape = (N_GX, N_GY, 3, N_GX)
    level = jax.random.randint(level_key, (N_GX, N_GY, 1, 1), 1, 9)
    lowest = CAP * level // 16
    highest = CAP * level // 8 + 1
    counts = jax.random.randint(count_key, shape, lowest, highest)
    full_owner = jax.random.randint(full_key, (N_GX, N_GY, 1, 1), 0, N_GX)
    side_no = jnp.arange(3, dtype=jnp.int32)[None, None, :, None]
    owners = jnp.arange(N_GX, dtype=jnp.int32)[None, None, None, :]
    tile_y = jnp.arange(N_GY, dtype=jnp.int32)[None, :, None, None]
    counts = jnp.where((side_no == 1) & (owners == full_owner), CAP, counts)
    neighbour = tile_y + side_no - 1
    valid = (neighbour >= 0) & (neighbour < N_GY)
    return jnp.where(valid, counts, 0).astype(jnp.int32)


def levels(rng, extent, cuts, low, largest):
    def one(position, blocks):
        heights = jax.random.uniform(jax.random.fold_in(jax.random.fold_in(rng, 6), position), (blocks,), jnp.float32, low / len(cuts), largest / len(cuts))
        return jnp.repeat(jnp.exp(heights), extent[position] // blocks).reshape((-1,) + (1,) * (len(extent) - position - 1))

    factor_of = one(*cuts[0])
    for cut in cuts[1:]:
        factor_of = factor_of * one(*cut)
    return factor_of


def centred(rng, shape, deviation, most, shards=(), kind=jnp.bfloat16):
    values = deviation * jax.random.normal(rng, shape, jnp.float32)
    if shards:
        values = values * levels(rng, shape, shards, -0.22, 0.18)
    return jnp.clip(values, -most, most).astype(kind)


def setup_inputs(seed: int = 0) -> dict:
    keys = jax.random.split(jax.random.key(seed), 8)
    return {
        "adjoint": centred(keys[0], (2, PLANES, NX, NY), 1.0, 6.0, ((2, 8), (3, 16)), jnp.float32),
        "base_flow": centred(keys[1], (2, PLANES, NX, NY), 0.5, 3.0, ((2, 8), (3, 16))),
        "slot_cell": draw_slot_cell(jax.random.fold_in(keys[7], 71), 0),
        "slot_marker": draw_slot_marker(jax.random.fold_in(keys[7], 71), 0),
        "slot_count": draw_slot_count(jax.random.fold_in(keys[7], 71), 0),
        "slot_weight": jnp.clip(0.02 + 0.09999999776482582 * jax.random.uniform(keys[5], (N_GX, N_GY, 3, N_GX, 16, CAP), jnp.float32) ** levels(keys[5], (N_GX, N_GY, 3, N_GX, 16, CAP), ((0, 8), (1, 16)), -0.2, 0.2), 0.02, 0.12),
        "marker_source": centred(keys[6], (2, PLANES, RISERS, MARKERS), 1.0, 6.0, ((1, 8), (2, 16)), jnp.float32),
    }


TIME_STEP = 0.5
VISCOSITY = 0.2
STIFFNESS = 2.0
BENDING = 0.25


def pad_one(field):
    return jnp.pad(field, [(0, 0)] * (field.ndim - 2) + [(1, 1), (1, 1)])


def base_gradients(padded):
    grad_ux = 0.5 * (padded[0, :, 2:, 1:-1] - padded[0, :, :-2, 1:-1])
    grad_vx = 0.5 * (padded[1, :, 2:, 1:-1] - padded[1, :, :-2, 1:-1])
    grad_uy = 0.5 * (padded[0, :, 1:-1, 2:] - padded[0, :, 1:-1, :-2])
    grad_vy = 0.5 * (padded[1, :, 1:-1, 2:] - padded[1, :, 1:-1, :-2])
    return (grad_ux, grad_vx, grad_uy, grad_vy)


def transport(padded, gradients, base_inner):
    centre = padded[..., 1:-1, 1:-1]
    east_cells = padded[..., 2:, 1:-1]
    west_cells = padded[..., :-2, 1:-1]
    north_cells = padded[..., 1:-1, 2:]
    south_cells = padded[..., 1:-1, :-2]
    laplace = east_cells + west_cells + north_cells + south_cells - 4.0 * centre
    along_x = 0.5 * (east_cells - west_cells)
    along_y = 0.5 * (north_cells - south_cells)
    stream_vel = base_inner[0]
    cross_vel = base_inner[1]
    first_comp = centre[0] + TIME_STEP * (stream_vel * along_x[0] + cross_vel * along_y[0] - gradients[0] * centre[0] - gradients[1] * centre[1] + VISCOSITY * laplace[0])
    second_comp = centre[1] + TIME_STEP * (stream_vel * along_x[1] + cross_vel * along_y[1] - gradients[2] * centre[0] - gradients[3] * centre[1] + VISCOSITY * laplace[1])
    return jnp.stack([first_comp, second_comp])


def divergence(padded):
    return 0.5 * (padded[0, :, 2:, 1:-1] - padded[0, :, :-2, 1:-1]) + 0.5 * (padded[1, :, 1:-1, 2:] - padded[1, :, 1:-1, :-2])


def relax_once(padded, div_source):
    return 0.25 * (padded[:, 2:, 1:-1] + padded[:, :-2, 1:-1] + padded[:, 1:-1, 2:] + padded[:, 1:-1, :-2] - div_source)


def correct(field, padded):
    slope_x = 0.5 * (padded[:, 2:, 1:-1] - padded[:, :-2, 1:-1])
    slope_y = 0.5 * (padded[:, 1:-1, 2:] - padded[:, 1:-1, :-2])
    return jnp.stack([field[0] - slope_x, field[1] - slope_y])


def marker_force_of(marker_sums, marker_source):
    bent = jnp.roll(marker_sums, 1, axis=-1) + jnp.roll(marker_sums, -1, axis=-1) - 2.0 * marker_sums
    return STIFFNESS * (marker_sums + marker_source - BENDING * bent)


def reference(adjoint, base_flow, slot_cell, slot_marker, slot_count, slot_weight, marker_source):
    planes = adjoint.shape[1]
    rows_all = adjoint.shape[2]
    cols_all = adjoint.shape[3]
    base_wide = pad_one(base_flow.astype(jnp.float32))
    gradients = base_gradients(base_wide)
    base_inner = base_flow.astype(jnp.float32)
    plane_block = planes // N_GX
    per_owner = RISER_DEV * MARKERS
    tile_x = jnp.arange(N_GX, dtype=jnp.int32)[:, None, None, None, None]
    tile_y = jnp.arange(N_GY, dtype=jnp.int32)[None, :, None, None, None]
    side_no = jnp.arange(3, dtype=jnp.int32)[None, None, :, None, None]
    owner_x = jnp.arange(N_GX, dtype=jnp.int32)[None, None, None, :, None]
    owner_y = jnp.clip(tile_y + side_no - 1, 0, N_GY - 1)
    local_plane = slot_marker // per_owner
    remainder = slot_marker % per_owner
    riser_row = owner_y * RISER_DEV + remainder // MARKERS
    plane_row = owner_x * plane_block + local_plane
    marker_index = ((plane_row * (RISER_DEV * N_GY) + riser_row) * MARKERS + remainder % MARKERS).reshape(-1).astype(jnp.int32)
    corner = ((plane_row * rows_all + tile_x * CX + slot_cell // CY) * cols_all + tile_y * CY + slot_cell % CY).reshape(-1).astype(jnp.int32)
    live_mask = (jnp.arange(CAP, dtype=jnp.int32)[None, None, None, None, :] < slot_count[..., None]).astype(jnp.float32).reshape(-1)
    count_markers = planes * RISER_DEV * N_GY * MARKERS
    forces = jnp.zeros(marker_source.shape, jnp.float32)
    for substep in range(SUBSTEPS):
        advected = transport(pad_one(adjoint), gradients, base_inner)
        flat_field = advected.reshape(2, -1)
        values = jnp.zeros((2, corner.shape[0]), jnp.float32)
        for corner_no in range(16):
            offset = (corner_no // 4) * cols_all + corner_no % 4
            weights = slot_weight[:, :, :, :, corner_no, :].reshape(-1)
            values = values + weights * flat_field[:, corner + offset]
        values = values * live_mask
        marker_sums = jnp.zeros((2, count_markers), jnp.float32).at[:, marker_index].add(values)
        forces = marker_force_of(marker_sums.reshape(marker_source.shape), marker_source)
        back_force = forces.reshape(2, -1)[:, marker_index] * live_mask
        for corner_no in range(16):
            offset = (corner_no // 4) * cols_all + corner_no % 4
            weights = slot_weight[:, :, :, :, corner_no, :].reshape(-1)
            flat_field = flat_field.at[:, corner + offset].add(TIME_STEP * weights * back_force)
        advected = flat_field.reshape(advected.shape)
        div_source = divergence(pad_one(advected))
        pressure = jnp.zeros_like(div_source)
        for sweep_no in range(SWEEPS):
            pressure = relax_once(pad_one(pressure), div_source)
        adjoint = correct(advected, pad_one(pressure))
    return adjoint, forces
```

```python
import functools

import jax
import jax.numpy as jnp
from jax import lax
from jax.experimental import pallas as pl
from jax.experimental.pallas import tpu as pltpu
from jax.sharding import PartitionSpec as P

SUBSTEPS = 3
SWEEPS = 8

TIME_STEP = 0.5
VISCOSITY = 0.2
STIFFNESS = 2.0
BENDING = 0.25

F32 = jnp.float32
BF16 = jnp.bfloat16
I32 = jnp.int32

GX = 8
ROWS = 32
NROW = GX * ROWS
COLS = 128
PL = 2
RIM = 16
THIN = 8
PACK = 312
PAIRS = 12
SPAN = 2 * COLS

NT = (((1,), (1,)), ((), ()))
NN = (((1,), (0,)), ((), ()))

PARAMS = pltpu.CompilerParams(vmem_limit_bytes=48 * 1024 * 1024)
VMEM = pl.BlockSpec(memory_space=pltpu.VMEM)
SMEM = pl.BlockSpec(memory_space=pltpu.SMEM)


def call(body, outs, ins, scratch=(), smem=()):
    return pl.pallas_call(
        body,
        out_shape=outs,
        in_specs=[SMEM if n in smem else VMEM for n in range(len(ins))],
        out_specs=jax.tree.map(lambda _: VMEM, outs),
        scratch_shapes=list(scratch),
        compiler_params=PARAMS,
    )(*ins)


def shape(*dims, dtype=F32):
    return jax.ShapeDtypeStruct(dims, dtype)


def moved_along(value, steps):
    count = lax.axis_size("gy")
    pairs = [(n, n + steps) for n in range(count) if 0 <= n + steps < count]
    return lax.ppermute(value, "gy", pairs)


def two_parts(value):
    high = value.astype(BF16)
    return high, (value - high.astype(F32)).astype(BF16)


def row_next(x):
    lane = lax.broadcasted_iota(I32, x.shape, 1)
    return jnp.where(lane == NROW - 1, 0.0, pltpu.roll(x, NROW - 1, 1))


def row_prev(x):
    lane = lax.broadcasted_iota(I32, x.shape, 1)
    return jnp.where(lane == 0, 0.0, pltpu.roll(x, 1, 1))


def col_next(x):
    return pltpu.roll(x, x.shape[0] - 1, 0)


def col_prev(x):
    return pltpu.roll(x, 1, 0)


def pack_kernel(count_ref, adj_ref, base_ref, cell_ref, mark_ref, weight_ref, out_ref):
    lane = lax.broadcasted_iota(I32, (16, COLS), 1)
    for e in range(GX):
        for c in range(2):
            for q in range(PL):
                at = (c * PL + q) * ROWS
                out_ref[e, at : at + ROWS, :] = adj_ref[c, e * PL + q]
                out_ref[e, 128 + at : 128 + at + ROWS, :] = base_ref[c, e * PL + q].astype(F32)
        for g in range(3):
            live = lane < count_ref[g, e]
            out_ref[e, 256 + 16 * g : 272 + 16 * g, :] = jnp.where(live, weight_ref[g, e], 0.0)
        ints = [cell_ref[g, e : e + 1, :] for g in range(3)]
        ints = ints + [mark_ref[g, e : e + 1, :] for g in range(3)]
        ints = ints + [jnp.zeros((2, COLS), I32)]
        out_ref[e, 304:312, :] = jnp.concatenate(ints, axis=0).astype(F32)


def unpack_kernel(got_ref, adj_ref, base_ref, ints_ref, weight_ref, low_ref, high_ref):
    for n in range(4):
        for ref, at in ((adj_ref, 0), (base_ref, 128)):
            at = at + n * ROWS
            block = jnp.concatenate([got_ref[a, at : at + ROWS, :] for a in range(GX)], axis=0)
            turned = block.T
            ref[n // 2, n % 2] = turned
            to = n // 2 if at < 128 else 2 + n // 2
            low_ref[to, n % 2] = turned[:THIN]
            high_ref[to, n % 2] = turned[COLS - THIN :]
    for g in range(3):
        for j in range(4):
            pair = g * 4 + j
            rows = []
            cell = []
            mark = []
            for a in (2 * j, 2 * j + 1):
                one = got_ref[a, 304:312, :].astype(I32)
                cell.append(one[g : g + 1])
                mark.append(one[3 + g : 4 + g])
                rows.append(
                    (mark[-1] >> 11) * COLS + (cell[-1] >> 7) + ROWS * (a % 4)
                )
                side = (a % 2) * COLS
                weight_ref[pair, :, side : side + COLS] = got_ref[
                    a, 256 + 16 * g : 272 + 16 * g, :
                ]
            cell = jnp.concatenate(cell, axis=1)
            mark = jnp.concatenate(mark, axis=1)
            ints_ref[pair, 0:1, :] = jnp.concatenate(rows, axis=1)
            ints_ref[pair, 1:2, :] = cell & 127
            ints_ref[pair, 2:3, :] = mark >> 7
            ints_ref[pair, 3:4, :] = mark & 127
            ints_ref[pair, 4:8, :] = jnp.zeros((4, SPAN), I32)


def one_hot(index, count):
    spot = lax.broadcasted_iota(I32, (count, SPAN), 0)
    return jnp.where(spot == index, 1.0, 0.0).astype(BF16)


def col_weights(first_col, weights, at, count):
    off = lax.broadcasted_iota(I32, (count, SPAN), 0) + at - first_col
    hits = [off == n for n in range(4)]
    tables = []
    for di in range(4):
        table = jnp.zeros((count, SPAN), F32)
        for dj in (3, 2, 1, 0):
            row = weights[4 * di + dj : 4 * di + dj + 1]
            table = jnp.where(hits[dj], row, table)
        tables.append(table)
    return tables


def projected(place, low_ref, mid_ref, high_ref, q):
    has_low = jnp.where(place == 0, 0.0, 1.0)
    has_high = jnp.where(place == 15, 0.0, 1.0)

    def inside(x):
        width = x.shape[0]
        return jnp.concatenate(
            [x[:RIM] * has_low, x[RIM : width - RIM], x[width - RIM :] * has_high], axis=0
        )

    wide = [
        jnp.concatenate(
            [low_ref[c, q].astype(F32), mid_ref[c, q], high_ref[c, q].astype(F32)], axis=0
        )
        for c in range(2)
    ]
    div = 0.5 * (row_next(wide[0]) - row_prev(wide[0])) + 0.5 * (
        col_next(wide[1]) - col_prev(wide[1])
    )
    pressure = inside(-0.25 * div)
    for sweep in range(SWEEPS - 1):
        pressure = inside(
            0.25
            * (
                row_next(pressure)
                + row_prev(pressure)
                + col_next(pressure)
                + col_prev(pressure)
                - div
            )
        )
    first = wide[0] - 0.5 * (row_next(pressure) - row_prev(pressure))
    second = wide[1] - 0.5 * (col_next(pressure) - col_prev(pressure))
    return inside(first), inside(second)


def transported(w, base):
    ux = 0.5 * (row_next(base[0]) - row_prev(base[0]))
    vx = 0.5 * (row_next(base[1]) - row_prev(base[1]))
    uy = 0.5 * (col_next(base[0]) - col_prev(base[0]))
    vy = 0.5 * (col_next(base[1]) - col_prev(base[1]))
    mixed = (ux * w[0] + vx * w[1], uy * w[0] + vy * w[1])
    out = []
    for c in range(2):
        east, west = row_next(w[c]), row_prev(w[c])
        north, south = col_next(w[c]), col_prev(w[c])
        laplace = east + west + north + south - 4.0 * w[c]
        value = w[c] + TIME_STEP * (
            base[0] * (0.5 * (east - west))
            + base[1] * (0.5 * (north - south))
            - mixed[c]
            + VISCOSITY * laplace
        )
        out.append(value[THIN : THIN + COLS])
    return out


def interpolate(moved_ref, ints_ref, weight_ref, part_refs, pick_hi, pick_lo, rows_ref, sum_ref):
    for c in range(2):
        for di in range(4):
            shifted = [moved_ref[c, q] for q in range(PL)]
            if di:
                shifted = [pltpu.roll(x, NROW - di, 1) for x in shifted]
            for half in range(2):
                both = jnp.concatenate(
                    [x[:, half * COLS : (half + 1) * COLS] for x in shifted], axis=1
                )
                at = (di * 2 + c) * COLS
                hi, lo = two_parts(both)
                pick_hi[half, at : at + COLS, :] = hi
                pick_lo[half, at : at + COLS, :] = lo
    sum_ref[...] = jnp.zeros(sum_ref.shape, F32)

    def block(pair, carry):
        g = pair // 4
        half = (pair % 4) // 2
        rows = one_hot(ints_ref[pair, 0:1, :], SPAN)
        rows_ref[...] = lax.dot_general(
            pick_hi[half], rows, NN, preferred_element_type=F32
        ) + lax.dot_general(pick_lo[half], rows, NN, preferred_element_type=F32)
        first_col = ints_ref[pair, 1:2, :]
        weights = weight_ref[pair]
        step = 16
        totals = [jnp.zeros((step, SPAN), F32) for c in range(2)]
        for at in range(0, COLS, step):
            tables = col_weights(first_col, weights, at, step)
            for di in range(4):
                for c in range(2):
                    start = (di * 2 + c) * COLS + at
                    totals[c] = totals[c] + tables[di] * rows_ref[start : start + step, :]
        high = lax.broadcasted_iota(I32, (32, SPAN), 0) == ints_ref[pair, 2:3, :]
        parts = [
            two_parts(jnp.where(high, jnp.sum(totals[c], axis=0, keepdims=True), 0.0))
            for c in range(2)
        ]
        stacked = jnp.concatenate([parts[0][0], parts[1][0], parts[0][1], parts[1][1]], axis=0)
        sums = lax.dot_general(
            stacked, one_hot(ints_ref[pair, 3:4, :], COLS), NT, preferred_element_type=F32
        )
        sum_ref[g] = sum_ref[g] + sums[:64] + sums[64:]
        return carry

    lax.fori_loop(0, PAIRS, block, 0)
    for g in range(3):
        part_refs[g][...] = sum_ref[g]


def advance_kernel(
    first, place_ref, low_ref, mid_ref, high_ref, base_low_ref, base_ref, base_high_ref,
    ints_ref, weight_ref, moved_ref, part0, part1, part2, pick_hi, pick_lo, rows_ref, sum_ref,
):
    for q in range(PL):
        base = [
            jnp.concatenate(
                [base_low_ref[2 + c, q], base_ref[c, q], base_high_ref[2 + c, q]], axis=0
            )
            for c in range(2)
        ]
        if first:
            w = [
                jnp.concatenate([low_ref[c, q], mid_ref[c, q], high_ref[c, q]], axis=0)
                for c in range(2)
            ]
        else:
            w = projected(place_ref[0], low_ref, mid_ref, high_ref, q)
            w = [x[RIM - THIN : RIM + COLS + THIN] for x in w]
        out = transported(w, base)
        for c in range(2):
            moved_ref[c, q] = out[c]
    interpolate(
        moved_ref, ints_ref, weight_ref, (part0, part1, part2), pick_hi, pick_lo, rows_ref, sum_ref
    )


def force_kernel(own_ref, low_ref, high_ref, source_ref, out_ref):
    sums = own_ref[...] + low_ref[...] + high_ref[...]
    row = lax.broadcasted_iota(I32, sums.shape, 0) & 3
    lane = lax.broadcasted_iota(I32, sums.shape, 1)
    count = sums.shape[0]
    up = jnp.where(row == 0, pltpu.roll(sums, count - 3, 0), pltpu.roll(sums, 1, 0))
    down = jnp.where(row == 3, pltpu.roll(sums, 3, 0), pltpu.roll(sums, count - 1, 0))
    before = jnp.where(lane == 0, pltpu.roll(up, 1, 1), pltpu.roll(sums, 1, 1))
    after = jnp.where(lane == 127, pltpu.roll(down, 127, 1), pltpu.roll(sums, 127, 1))
    bent = before + after - 2.0 * sums
    out_ref[...] = STIFFNESS * (sums + source_ref[...] - BENDING * bent)


def spread_kernel(
    low_ref, own_ref, high_ref, moved_ref, ints_ref, weight_ref,
    out_ref, edge_low, edge_high, force_ref, hi_ref, lo_ref, acc_ref,
):
    for g, ref in enumerate((low_ref, own_ref, high_ref)):
        hi, lo = two_parts(ref[...])
        force_ref[g, :64, :] = hi
        force_ref[g, 64:, :] = lo
    acc_ref[...] = jnp.zeros(acc_ref.shape, F32)

    def block(pair, carry):
        g = pair // 4
        half = (pair % 4) // 2
        picked = lax.dot_general(
            force_ref[g], one_hot(ints_ref[pair, 3:4, :], COLS), NN, preferred_element_type=F32
        )
        picked = picked[:64] + picked[64:]
        high = lax.broadcasted_iota(I32, (32, SPAN), 0) == ints_ref[pair, 2:3, :]
        forces = [
            TIME_STEP
            * jnp.sum(
                jnp.where(high, picked[32 * c : 32 * c + 32], 0.0), axis=0, keepdims=True
            )
            for c in range(2)
        ]
        first_col = ints_ref[pair, 1:2, :]
        weights = weight_ref[pair]
        step = 16
        for at in range(0, COLS, step):
            tables = col_weights(first_col, weights, at, step)
            for di in range(4):
                for c in range(2):
                    start = (di * 2 + c) * COLS + at
                    hi, lo = two_parts(tables[di] * forces[c])
                    hi_ref[start : start + step, :] = hi
                    lo_ref[start : start + step, :] = lo
        rows = one_hot(ints_ref[pair, 0:1, :], SPAN)
        acc_ref[half] = (
            acc_ref[half]
            + lax.dot_general(hi_ref[...], rows, NT, preferred_element_type=F32)
            + lax.dot_general(lo_ref[...], rows, NT, preferred_element_type=F32)
        )
        return carry

    lax.fori_loop(0, PAIRS, block, 0)
    for c in range(2):
        for q in range(PL):
            halves = []
            for half in range(2):
                total = moved_ref[c, q, :, half * COLS : (half + 1) * COLS]
                for di in range(4):
                    at = (di * 2 + c) * COLS
                    one = acc_ref[half, at : at + COLS, q * COLS : (q + 1) * COLS]
                    total = total + (pltpu.roll(one, di, 1) if di else one)
                halves.append(total)
            total = jnp.concatenate(halves, axis=1)
            out_ref[c, q] = total
            edge_low[c, q] = total[:RIM].astype(BF16)
            edge_high[c, q] = total[COLS - RIM :].astype(BF16)


def finish_kernel(place_ref, low_ref, mid_ref, high_ref, out_ref):
    for q in range(PL):
        w = projected(place_ref[0], low_ref, mid_ref, high_ref, q)
        for c in range(2):
            block = w[c][RIM : RIM + COLS].T
            for a in range(GX):
                out_ref[a, c, q] = block[a * ROWS : (a + 1) * ROWS]


def on_device(adjoint, base_flow, slot_cell, slot_marker, slot_count, slot_weight, marker_source):
    place = lax.axis_index("gy").astype(I32).reshape(1)
    field = shape(2, PL, COLS, NROW)
    packed = call(
        pack_kernel,
        shape(GX, PACK, COLS),
        (slot_count[0, 0], adjoint, base_flow, slot_cell[0, 0], slot_marker[0, 0], slot_weight[0, 0]),
        smem=(0,),
    )
    got = lax.all_to_all(packed, "gx", split_axis=0, concat_axis=0, tiled=True)
    thin = shape(4, PL, THIN, NROW)
    current, base, ints, weights, thin_low, thin_high = call(
        unpack_kernel,
        (field, field, shape(PAIRS, 8, SPAN, dtype=I32), shape(PAIRS, 16, SPAN), thin, thin),
        (got,),
    )
    base_low = moved_along(thin_high, 1)
    base_high = moved_along(thin_low, -1)
    low, high = base_low, base_high
    source = marker_source.reshape(64, COLS)
    marker = shape(64, COLS)
    rim = shape(2, PL, RIM, NROW, dtype=BF16)
    forces = source
    for substep in range(SUBSTEPS):
        moved, part0, part1, part2 = call(
            functools.partial(advance_kernel, substep == 0),
            (field, marker, marker, marker),
            (place, low, current, high, base_low, base, base_high, ints, weights),
            scratch=(
                pltpu.VMEM((2, 8 * COLS, SPAN), BF16),
                pltpu.VMEM((2, 8 * COLS, SPAN), BF16),
                pltpu.VMEM((8 * COLS, SPAN), F32),
                pltpu.VMEM((3, 64, COLS), F32),
            ),
            smem=(0,),
        )
        forces = call(
            force_kernel,
            marker,
            (part1, moved_along(part2, 1), moved_along(part0, -1), source),
        )
        current, edge_low, edge_high = call(
            spread_kernel,
            (field, rim, rim),
            (moved_along(forces, 1), forces, moved_along(forces, -1), moved, ints, weights),
            scratch=(
                pltpu.VMEM((3, 128, COLS), BF16),
                pltpu.VMEM((8 * COLS, SPAN), BF16),
                pltpu.VMEM((8 * COLS, SPAN), BF16),
                pltpu.VMEM((2, 8 * COLS, SPAN), F32),
            ),
        )
        low = moved_along(edge_high, 1)
        high = moved_along(edge_low, -1)
    done = call(
        finish_kernel,
        shape(GX, 2, PL, ROWS, COLS),
        (place, low, current, high),
        smem=(0,),
    )
    back = lax.all_to_all(done, "gx", split_axis=0, concat_axis=0, tiled=True)
    result = jnp.transpose(back, (1, 0, 2, 3, 4)).reshape(adjoint.shape)
    return (result, forces.reshape(marker_source.shape))


def solution(mesh):
    in_specs = (
        P(None, None, "gx", "gy"),
        P(None, None, "gx", "gy"),
        P("gx", "gy", None, None, None),
        P("gx", "gy", None, None, None),
        P("gx", "gy", None, None),
        P("gx", "gy", None, None, None, None),
        P(None, "gx", "gy", None),
    )
    out_specs = (P(None, None, "gx", "gy"), P(None, "gx", "gy", None))
    return jax.shard_map(
        on_device, mesh=mesh, in_specs=in_specs, out_specs=out_specs, check_vma=False
    )
```

```python
import functools

import jax
import jax.numpy as jnp
from jax import lax
from jax.experimental import pallas as pl
from jax.experimental.pallas import tpu as pltpu
from jax.sharding import Mesh, PartitionSpec as P

SUBSTEPS = 3
SWEEPS = 8

TIME_STEP = 0.5
VISCOSITY = 0.2
STIFFNESS = 2.0
BENDING = 0.25

F32 = jnp.float32
BF16 = jnp.bfloat16
I32 = jnp.int32

GX = 8
ROWS = 32
COLS = 128
NROW = GX * ROWS
NCOL = 2 * COLS
LAST = 7
RIM = 16
THIN = 8
PACK = 304
SPAN = 256
STREAMS = 4
DEPTH = 6
EMPTY = STREAMS * DEPTH
COUNT_AT = 31

NT = (((1,), (1,)), ((), ()))
NN = (((1,), (0,)), ((), ()))

PARAMS = pltpu.CompilerParams(vmem_limit_bytes=48 * 1024 * 1024)
ROOMY = pltpu.CompilerParams(vmem_limit_bytes=60 * 1024 * 1024)
VMEM = pl.BlockSpec(memory_space=pltpu.VMEM)
SMEM = pl.BlockSpec(memory_space=pltpu.SMEM)
HBM = pl.BlockSpec(memory_space=pltpu.HBM)


def call(body, outs, ins, scratch=(), spaces=(), out_specs=None, params=PARAMS):
    spaces = dict(spaces)
    return pl.pallas_call(
        body,
        out_shape=outs,
        in_specs=[spaces.get(n, VMEM) for n in range(len(ins))],
        out_specs=out_specs or jax.tree.map(lambda _: VMEM, outs),
        scratch_shapes=list(scratch),
        compiler_params=params,
    )(*ins)


def shape(*dims, dtype=F32):
    return jax.ShapeDtypeStruct(dims, dtype)


def moved_along(value, steps):
    count = lax.axis_size("gb")
    return lax.ppermute(value, "gb", [(n, (n + steps) % count) for n in range(count)])


def swapped(value):
    return lax.ppermute(value, "core", [(0, 1), (1, 0)])


def two_parts(value):
    high = value.astype(BF16)
    return high, (value - high.astype(F32)).astype(BF16)


def row_next(x):
    lane = lax.broadcasted_iota(I32, x.shape, 1)
    return jnp.where(lane == NROW - 1, 0.0, pltpu.roll(x, NROW - 1, 1))


def row_prev(x):
    lane = lax.broadcasted_iota(I32, x.shape, 1)
    return jnp.where(lane == 0, 0.0, pltpu.roll(x, 1, 1))


def col_next(x):
    return pltpu.roll(x, x.shape[0] - 1, 0)


def col_prev(x):
    return pltpu.roll(x, 1, 0)


def pack_kernel(
    count_ref, adj_hbm, base_hbm, cell_hbm, mark_hbm, weight_hbm, out_ref,
    adj_ref, base_ref, cell_ref, mark_ref, weight_ref, sems,
):
    copies = [
        pltpu.make_async_copy(src, dst, sems.at[n])
        for n, (src, dst) in enumerate(
            (
                (cell_hbm, cell_ref),
                (mark_hbm, mark_ref),
                (weight_hbm, weight_ref),
                (base_hbm, base_ref),
                (adj_hbm, adj_ref),
            )
        )
    ]
    for copy in copies:
        copy.start()
    copies[0].wait()
    copies[1].wait()
    lane = lax.broadcasted_iota(I32, (1, COLS), 1)
    none = jnp.zeros((4, COLS), F32)
    for e in range(GX):
        for q in range(2):
            rows = []
            for g in range(3):
                cell = cell_ref[g, e : e + 1, :]
                mark = mark_ref[g, e : e + 1, :]
                live = (lane < count_ref[g, e]) & ((mark >> 11) == q)
                rows += [cell >> 7, cell & 127, jnp.where(live, (mark >> 7) & 15, -1), mark & 127]
            ints = jnp.concatenate([r.astype(F32) for r in rows] + [none], axis=0)
            out_ref[2 * e + q, 288:304, :] = ints.astype(BF16)
    copies[2].wait()
    for e in range(GX):
        for g in range(3):
            hi, lo = two_parts(weight_ref[g, e])
            for q in range(2):
                out_ref[2 * e + q, 192 + 16 * g : 208 + 16 * g, :] = hi
                out_ref[2 * e + q, 240 + 16 * g : 256 + 16 * g, :] = lo
    copies[3].wait()
    for p in range(2 * GX):
        for c in range(2):
            out_ref[p, 128 + c * ROWS : 128 + (c + 1) * ROWS, :] = base_ref[c, p]
    copies[4].wait()
    for p in range(2 * GX):
        for c in range(2):
            hi, lo = two_parts(adj_ref[c, p])
            out_ref[p, c * ROWS : (c + 1) * ROWS, :] = hi
            out_ref[p, 64 + c * ROWS : 64 + (c + 1) * ROWS, :] = lo


def stacked_rows(rows):
    spot = lax.broadcasted_iota(I32, (8, COLS), 0)
    total = jnp.zeros((8, COLS), F32)
    for n, row in enumerate(rows):
        total = jnp.where(spot == n, row, total)
    return total


def closed_up(blocks):
    lane = lax.broadcasted_iota(I32, (1, COLS), 1)
    spot = lax.broadcasted_iota(I32, (24, COLS), 0)
    blank = jnp.where(spot == 20, -1.0, 0.0)
    for bit in range(11):
        step = 1 << bit
        goes = []
        stays = []
        for x in blocks:
            away = x[20:21].astype(I32)
            flag = (away >> bit) & 1
            goes.append(jnp.where((away >= 0) & (flag == 1), 1.0, 0.0))
            stays.append((away >= 0) & (flag == 0))

        def ahead(values, n):
            if step >= COLS:
                m = n + step // COLS
                return values[m] if m < len(values) else None
            here = pltpu.roll(values[n], COLS - step, 1)
            if n + 1 < len(values):
                there = pltpu.roll(values[n + 1], COLS - step, 1)
            else:
                there = jnp.zeros_like(here)
            return jnp.where(lane < COLS - step, here, there)

        result = []
        for n, x in enumerate(blocks):
            kept = jnp.where(stays[n], x, blank)
            coming = ahead(goes, n)
            if coming is None:
                result.append(kept)
            else:
                result.append(jnp.where(coming > 0.5, ahead(blocks, n), kept))
        blocks = result
    return blocks


def unpack_kernel(got_ref, source_ref, adj_ref, base_ref, low_ref, high_ref):
    for n in range(4):
        for side in range(2):
            parts = []
            for a in range(GX):
                d = 2 * a + side
                at = (n % 2) * ROWS
                if n < 2:
                    part = got_ref[d, at : at + ROWS, :].astype(F32)
                    part = part + got_ref[d, 64 + at : 64 + at + ROWS, :].astype(F32)
                else:
                    part = got_ref[d, 128 + at : 128 + at + ROWS, :].astype(F32)
                parts.append(part)
            turned = jnp.concatenate(parts, axis=0).T
            ref = adj_ref if n < 2 else base_ref
            ref[n % 2, side * COLS : (side + 1) * COLS, :] = turned
            if side == 0:
                low_ref[n] = turned[:THIN]
            else:
                high_ref[n] = turned[COLS - THIN :]
    for c in range(2):
        for ref, side in ((low_ref, 0), (high_ref, 1)):
            ref[4 + c] = jnp.concatenate(
                [source_ref[c, side, 0:8, :], source_ref[c, side, 8:16, :]], axis=1
            )


def slots_kernel(got_ref, ints_ref, weight_ref, table_ref):
    order = [
        (side, half, g, 4 * half + n)
        for side in range(2)
        for half in range(2)
        for g in range(3)
        for n in range(4)
    ]
    ints = {}
    for side in range(2):
        for a in range(GX):
            ints[side, a] = got_ref[2 * a + side, 288:304, :].astype(F32)
    high = [ints[side, a][4 * g + 2 : 4 * g + 3] for side, half, g, a in order]
    live = jnp.where(jnp.concatenate(high, axis=0) >= 0.0, 1.0, 0.0)
    count = len(order)
    across = lax.broadcasted_iota(I32, (COLS, COLS), 0) <= lax.broadcasted_iota(
        I32, (COLS, COLS), 1
    )
    bits = live.astype(BF16)
    within = lax.dot_general(
        bits, jnp.where(across, 1.0, 0.0).astype(BF16), NN, preferred_element_type=F32
    )
    whole = lax.dot_general(bits, jnp.ones((COLS, COLS), BF16), NN, preferred_element_type=F32)
    row = lax.broadcasted_iota(I32, (count, COLS), 0)
    before = []
    for stream in range(STREAMS):
        total = jnp.zeros((1, COLS), F32)
        for n in range(12):
            at = stream * 12 + n
            before.append(total)
            total = total + whole[at : at + 1]
    rank = within + jnp.concatenate(before, axis=0)
    spot = ((row % 12) * COLS + lax.broadcasted_iota(I32, (count, COLS), 1)).astype(F32)
    away = jnp.where(live > 0.5, spot - rank + 1.0, -1.0)
    filled = jnp.int32(0)
    for stream in range(STREAMS):
        blocks = []
        for n in range(12):
            at = stream * 12 + n
            side, half, g, a = order[at]
            one = ints[side, a]
            weights = got_ref[2 * a + side, 192 + 16 * g : 208 + 16 * g, :].astype(F32)
            weights = weights + got_ref[2 * a + side, 240 + 16 * g : 256 + 16 * g, :].astype(F32)
            rest = stacked_rows(
                [
                    one[4 * g : 4 * g + 1] + float(ROWS * (a % 4)),
                    one[4 * g + 1 : 4 * g + 2],
                    one[4 * g + 2 : 4 * g + 3] + float(16 * (side + g)),
                    one[4 * g + 3 : 4 * g + 4],
                    away[at : at + 1],
                ]
            )
            blocks.append(jnp.concatenate([weights, rest], axis=0))
        blocks = closed_up(blocks)
        for n, block in enumerate(blocks):
            at = (n % 2) * COLS
            weight_ref[stream * DEPTH + n // 2, :, at : at + COLS] = block[:16]
            ints_ref[stream * DEPTH + n // 2, :, at : at + COLS] = block[16:].astype(I32)
        slots = jnp.max(rank[stream * 12 : stream * 12 + 12]).astype(I32)
        here = (slots + SPAN - 1) // SPAN
        for n in range(DEPTH):

            @pl.when(n < here)
            def _():
                table_ref[filled + n] = stream * DEPTH + n

        filled = filled + here
    table_ref[filled] = EMPTY
    table_ref[COUNT_AT] = filled
    weight_ref[EMPTY] = jnp.zeros((16, SPAN), F32)
    ints_ref[EMPTY] = jnp.zeros((8, SPAN), I32)


def one_hot(index, count):
    spot = lax.broadcasted_iota(I32, (count, SPAN), 0)
    return jnp.where(spot == index, 1.0, 0.0).astype(BF16)


def col_weights(first_col, weights, at, count):
    off = lax.broadcasted_iota(I32, (count, SPAN), 0) + at - first_col
    hits = [off == n for n in range(4)]
    tables = []
    for di in range(4):
        table = jnp.zeros((count, SPAN), F32)
        for dj in (3, 2, 1, 0):
            row = weights[4 * di + dj : 4 * di + dj + 1]
            table = jnp.where(hits[dj], row, table)
        tables.append(table)
    return tables


def neighbours(place):
    return jnp.where(place == 0, 0.0, 1.0), jnp.where(place == LAST, 0.0, 1.0)


def projected(place, low_ref, mid_ref, high_ref):
    has_low, has_high = neighbours(place)

    def inside(x):
        width = x.shape[0]
        return jnp.concatenate(
            [x[:RIM] * has_low, x[RIM : width - RIM], x[width - RIM :] * has_high], axis=0
        )

    wide = [
        inside(
            jnp.concatenate([low_ref[c].astype(F32), mid_ref[c], high_ref[c].astype(F32)], axis=0)
        )
        for c in range(2)
    ]
    div = 0.5 * (row_next(wide[0]) - row_prev(wide[0])) + 0.5 * (
        col_next(wide[1]) - col_prev(wide[1])
    )
    pressure = inside(-0.25 * div)
    for sweep in range(SWEEPS - 1):
        pressure = inside(
            0.25
            * (
                row_next(pressure)
                + row_prev(pressure)
                + col_next(pressure)
                + col_prev(pressure)
                - div
            )
        )
    first = wide[0] - 0.5 * (row_next(pressure) - row_prev(pressure))
    second = wide[1] - 0.5 * (col_next(pressure) - col_prev(pressure))
    return inside(first), inside(second)


def transported(w, base):
    ux = 0.5 * (row_next(base[0]) - row_prev(base[0]))
    vx = 0.5 * (row_next(base[1]) - row_prev(base[1]))
    uy = 0.5 * (col_next(base[0]) - col_prev(base[0]))
    vy = 0.5 * (col_next(base[1]) - col_prev(base[1]))
    mixed = (ux * w[0] + vx * w[1], uy * w[0] + vy * w[1])
    out = []
    for c in range(2):
        east, west = row_next(w[c]), row_prev(w[c])
        north, south = col_next(w[c]), col_prev(w[c])
        laplace = east + west + north + south - 4.0 * w[c]
        value = w[c] + TIME_STEP * (
            base[0] * (0.5 * (east - west))
            + base[1] * (0.5 * (north - south))
            - mixed[c]
            + VISCOSITY * laplace
        )
        out.append(value[THIN : THIN + NCOL])
    return out


def interpolate(moved_ref, table_ref, ints_ref, weight_ref, pick_ref, rows_refs, sum_ref):
    for c in range(2):
        for di in range(4):
            shifted = moved_ref[c]
            if di:
                shifted = pltpu.roll(shifted, NROW - di, 1)
            hi, lo = two_parts(shifted)
            at = (di * 2 + c) * COLS
            for stream in range(STREAMS):
                side, half = stream // 2, stream % 2
                pick_ref[stream, at : at + COLS, :] = jnp.concatenate(
                    [
                        x[side * COLS : (side + 1) * COLS, half * COLS : (half + 1) * COLS]
                        for x in (hi, lo)
                    ],
                    axis=1,
                )
    sum_ref[...] = jnp.zeros(sum_ref.shape, F32)

    def blocks(n, carry):
        ids = [table_ref[2 * n], table_ref[2 * n + 1]]
        for block, rows_ref in zip(ids, rows_refs):
            rows = one_hot(ints_ref[block, 0:1, :], COLS)
            rows_ref[...] = lax.dot_general(
                pick_ref[jnp.minimum(block // DEPTH, STREAMS - 1)],
                jnp.concatenate([rows, rows], axis=0),
                NN,
                preferred_element_type=F32,
            )
        sums = []
        for block, rows_ref in zip(ids, rows_refs):
            first_col = ints_ref[block, 1:2, :]
            weights = weight_ref[block]
            step = 16
            totals = [jnp.zeros((step, SPAN), F32) for c in range(2)]
            for at in range(0, COLS, step):
                tables = col_weights(first_col, weights, at, step)
                for di in range(4):
                    for c in range(2):
                        start = (di * 2 + c) * COLS + at
                        totals[c] = totals[c] + tables[di] * rows_ref[start : start + step, :]
            high = lax.broadcasted_iota(I32, (64, SPAN), 0) == ints_ref[block, 2:3, :]
            parts = [
                two_parts(jnp.where(high, jnp.sum(totals[c], axis=0, keepdims=True), 0.0))
                for c in range(2)
            ]
            stacked = jnp.concatenate(
                [parts[0][0], parts[1][0], parts[0][1], parts[1][1]], axis=0
            )
            both = lax.dot_general(
                stacked, one_hot(ints_ref[block, 3:4, :], COLS), NT, preferred_element_type=F32
            )
            sums.append(both[:128] + both[128:])
        sum_ref[...] = sum_ref[...] + (sums[0] + sums[1])
        return carry

    lax.fori_loop(0, (table_ref[COUNT_AT] + 1) // 2, blocks, 0)


def advance_kernel(
    first, place_ref, table_ref, low_ref, mid_ref, high_ref, base_low_ref, base_ref,
    base_high_ref, ints_ref, weight_ref, moved_ref, part_low, part_high, pick_ref, rows_a, rows_b,
    sum_ref,
):
    has_low, has_high = neighbours(place_ref[0])

    def widened(low, mid, high):
        return jnp.concatenate([low * has_low, mid, high * has_high], axis=0)

    base = [widened(base_low_ref[2 + c], base_ref[c], base_high_ref[2 + c]) for c in range(2)]
    if first:
        w = [widened(low_ref[c], mid_ref[c], high_ref[c]) for c in range(2)]
    else:
        w = projected(place_ref[0], low_ref, mid_ref, high_ref)
        w = [x[RIM - THIN : RIM + NCOL + THIN] for x in w]
    out = transported(w, base)
    for c in range(2):
        moved_ref[c] = out[c]
    interpolate(moved_ref, table_ref, ints_ref, weight_ref, pick_ref, (rows_a, rows_b), sum_ref)
    for c in range(2):
        part_low[c] = sum_ref[64 * c : 64 * c + 32, :]
        part_high[c] = sum_ref[64 * c + 32 : 64 * c + 64, :]


def force_of(sums, source):
    row = lax.broadcasted_iota(I32, sums.shape, 0) & 3
    lane = lax.broadcasted_iota(I32, sums.shape, 1)
    count = sums.shape[0]
    up = jnp.where(row == 0, pltpu.roll(sums, count - 3, 0), pltpu.roll(sums, 1, 0))
    down = jnp.where(row == 3, pltpu.roll(sums, 3, 0), pltpu.roll(sums, count - 1, 0))
    before = jnp.where(lane == 0, pltpu.roll(up, 1, 1), pltpu.roll(sums, 1, 1))
    after = jnp.where(lane == 127, pltpu.roll(down, 127, 1), pltpu.roll(sums, 127, 1))
    bent = before + after - 2.0 * sums
    return STIFFNESS * (sums + source - BENDING * bent)


def spread_kernel(
    place_ref, table_ref, part_low, part_high, from_low, from_high, thin_low, source_ref, thin_high,
    moved_ref, ints_ref, weight_ref, out_ref, edge_low, edge_high, own_ref,
    force_ref, left_a, left_b, acc_ref,
):
    has_low, has_high = neighbours(place_ref[0])
    for c in range(2):
        outer = [
            jnp.concatenate([ref[4 + c, :, :COLS], ref[4 + c, :, COLS:]], axis=0)
            for ref in (thin_low, thin_high)
        ]
        source = jnp.concatenate(
            [outer[0], source_ref[c, 0], source_ref[c, 1], outer[1]], axis=0
        )
        sums = jnp.concatenate(
            [part_low[c] + from_low[c] * has_low, part_high[c] + from_high[c] * has_high], axis=0
        )
        force = force_of(sums, source)
        own_ref[c, 0] = force[16:32]
        own_ref[c, 1] = force[32:48]
        hi, lo = two_parts(force)
        force_ref[64 * c : 64 * c + 64, :] = hi
        force_ref[128 + 64 * c : 192 + 64 * c, :] = lo
    acc_ref[...] = jnp.zeros(acc_ref.shape, F32)

    def blocks(n, carry):
        ids = [table_ref[2 * n], table_ref[2 * n + 1]]
        for block, left_ref in zip(ids, (left_a, left_b)):
            picked = lax.dot_general(
                force_ref[...], one_hot(ints_ref[block, 3:4, :], COLS), NN,
                preferred_element_type=F32,
            )
            picked = picked[:128] + picked[128:]
            high = lax.broadcasted_iota(I32, (64, SPAN), 0) == ints_ref[block, 2:3, :]
            forces = [
                TIME_STEP
                * jnp.sum(
                    jnp.where(high, picked[64 * c : 64 * c + 64], 0.0), axis=0, keepdims=True
                )
                for c in range(2)
            ]
            first_col = ints_ref[block, 1:2, :]
            weights = weight_ref[block]
            step = 16
            for at in range(0, COLS, step):
                tables = col_weights(first_col, weights, at, step)
                for di in range(4):
                    for c in range(2):
                        start = (di * 2 + c) * COLS + at
                        hi, lo = two_parts(tables[di] * forces[c])
                        left_ref[start : start + step, :SPAN] = hi
                        left_ref[start : start + step, SPAN:] = lo
        for block, left_ref in zip(ids, (left_a, left_b)):
            rows = one_hot(ints_ref[block, 0:1, :], COLS)
            stream = jnp.minimum(block // DEPTH, STREAMS - 1)
            acc_ref[stream] = acc_ref[stream] + lax.dot_general(
                left_ref[...],
                jnp.concatenate([rows, rows], axis=1),
                NT,
                preferred_element_type=F32,
            )
        return carry

    lax.fori_loop(0, (table_ref[COUNT_AT] + 1) // 2, blocks, 0)
    for c in range(2):
        for side in range(2):
            halves = []
            for half in range(2):
                total = moved_ref[
                    c, side * COLS : (side + 1) * COLS, half * COLS : (half + 1) * COLS
                ]
                for di in range(4):
                    at = (di * 2 + c) * COLS
                    one = acc_ref[side * 2 + half, at : at + COLS, :]
                    total = total + (pltpu.roll(one, di, 1) if di else one)
                halves.append(total)
            total = jnp.concatenate(halves, axis=1)
            out_ref[c, side * COLS : (side + 1) * COLS, :] = total
            if side == 0:
                edge_low[c] = total[:RIM].astype(BF16)
            else:
                edge_high[c] = total[COLS - RIM :].astype(BF16)


def finish_kernel(place_ref, low_ref, mid_ref, high_ref, out_ref):
    w = projected(place_ref[0], low_ref, mid_ref, high_ref)
    for c in range(2):
        for side in range(2):
            at = RIM + side * COLS
            block = w[c][at : at + COLS].T
            for a in range(GX):
                out_ref[2 * a + side, c] = block[a * ROWS : (a + 1) * ROWS]


def on_device(adjoint, base_flow, slot_cell, slot_marker, slot_count, slot_weight, marker_source):
    place = lax.axis_index("gb").astype(I32).reshape(1)
    core = lax.axis_index("core")
    whole = ("gx", "core")
    tiles = marker_source.reshape(2, 2, 16, COLS)
    kept = lax.dynamic_index_in_dim(tiles, core, axis=1, keepdims=False)
    other = swapped(lax.dynamic_index_in_dim(tiles, 1 - core, axis=1, keepdims=False))
    source = jnp.where(
        core == 0, jnp.stack([kept, other], axis=1), jnp.stack([other, kept], axis=1)
    )
    packed = call(
        pack_kernel,
        shape(2 * GX, PACK, COLS, dtype=BF16),
        (slot_count[0, 0], adjoint, base_flow, slot_cell[0, 0], slot_marker[0, 0], slot_weight[0, 0]),
        scratch=(
            pltpu.VMEM(adjoint.shape, F32),
            pltpu.VMEM(base_flow.shape, BF16),
            pltpu.VMEM((3, GX, COLS), I32),
            pltpu.VMEM((3, GX, COLS), I32),
            pltpu.VMEM((3, GX, 16, COLS), F32),
            pltpu.SemaphoreType.DMA((5,)),
        ),
        spaces={0: SMEM, 1: HBM, 2: HBM, 3: HBM, 4: HBM, 5: HBM},
        params=ROOMY,
    )
    got = lax.all_to_all(packed, whole, split_axis=0, concat_axis=0, tiled=True)
    field = shape(2, NCOL, NROW)
    thin = shape(6, THIN, NROW)
    current, base, thin_low, thin_high = call(
        unpack_kernel, (field, field, thin, thin), (got, source)
    )
    base_low = moved_along(thin_high, 1)
    base_high = moved_along(thin_low, -1)
    ints, weights, table = call(
        slots_kernel,
        (
            shape(EMPTY + 1, 8, SPAN, dtype=I32),
            shape(EMPTY + 1, 16, SPAN),
            shape(32, dtype=I32),
        ),
        (got,),
        out_specs=(VMEM, VMEM, SMEM),
    )
    low, high = base_low, base_high
    part = shape(2, 32, COLS)
    rim = shape(2, RIM, NROW, dtype=BF16)
    forces = source
    for substep in range(SUBSTEPS):
        moved, part_low, part_high = call(
            functools.partial(advance_kernel, substep == 0),
            (field, part, part),
            (place, table, low, current, high, base_low, base, base_high, ints, weights),
            scratch=(
                pltpu.VMEM((STREAMS, 8 * COLS, SPAN), BF16),
                pltpu.VMEM((8 * COLS, SPAN), F32),
                pltpu.VMEM((8 * COLS, SPAN), F32),
                pltpu.VMEM((128, COLS), F32),
            ),
            spaces={0: SMEM, 1: SMEM},
        )
        from_low = moved_along(part_high, 1)
        from_high = moved_along(part_low, -1)
        current, edge_low, edge_high, forces = call(
            spread_kernel,
            (field, rim, rim, shape(2, 2, 16, COLS)),
            (
                place, table, part_low, part_high, from_low, from_high, base_low, source,
                base_high, moved, ints, weights,
            ),
            scratch=(
                pltpu.VMEM((256, COLS), BF16),
                pltpu.VMEM((8 * COLS, 2 * SPAN), BF16),
                pltpu.VMEM((8 * COLS, 2 * SPAN), BF16),
                pltpu.VMEM((STREAMS, 8 * COLS, COLS), F32),
            ),
            spaces={0: SMEM, 1: SMEM},
        )
        low = moved_along(edge_high, 1)
        high = moved_along(edge_low, -1)
    done = call(
        finish_kernel,
        shape(2 * GX, 2, ROWS, COLS),
        (place, low, current, high),
        spaces={0: SMEM},
    )
    back = lax.all_to_all(done, whole, split_axis=0, concat_axis=0, tiled=True)
    result = jnp.transpose(back, (1, 0, 2, 3))
    mine = lax.dynamic_index_in_dim(forces, core, axis=1, keepdims=False)
    theirs = swapped(lax.dynamic_index_in_dim(forces, 1 - core, axis=1, keepdims=False))
    planes = jnp.where(
        core == 0, jnp.stack([mine, theirs], axis=1), jnp.stack([theirs, mine], axis=1)
    )
    return (result, planes.reshape(marker_source.shape))


def solution(mesh):
    split = Mesh(mesh.devices.reshape(8, 8, 2), ("gx", "gb", "core"))
    gy = ("gb", "core")
    in_specs = (
        P(None, None, "gx", gy),
        P(None, None, "gx", gy),
        P("gx", gy, None, None, None),
        P("gx", gy, None, None, None),
        P("gx", gy, None, None),
        P("gx", gy, None, None, None, None),
        P(None, "gx", gy, None),
    )
    out_specs = (P(None, None, "gx", gy), P(None, "gx", gy, None))
    return jax.shard_map(
        on_device, mesh=split, in_specs=in_specs, out_specs=out_specs, check_vma=False
    )
```

```python
import functools

import jax
import jax.numpy as jnp
from jax import lax
from jax.experimental import pallas as pl
from jax.experimental.pallas import tpu as pltpu
from jax.sharding import Mesh, PartitionSpec as P

SUBSTEPS = 3
SWEEPS = 8

TIME_STEP = 0.5
VISCOSITY = 0.2
STIFFNESS = 2.0
BENDING = 0.25

F32 = jnp.float32
BF16 = jnp.bfloat16
I32 = jnp.int32

GX = 8
ROWS = 32
COLS = 128
NROW = GX * ROWS
NCOL = 2 * COLS
LAST = 7
RIM = 16
STRIP = 3 * RIM
THIN = 8
PACK = 304
SPAN = 128
TILES = 2 * GX
DEPTH = 3
EMPTY = TILES * DEPTH
COUNT_AT = 63
GROUP = 12

NT = (((1,), (1,)), ((), ()))
NN = (((1,), (0,)), ((), ()))

PARAMS = pltpu.CompilerParams(vmem_limit_bytes=24 * 1024 * 1024)
ROOMY = pltpu.CompilerParams(vmem_limit_bytes=60 * 1024 * 1024)
VMEM = pl.BlockSpec(memory_space=pltpu.VMEM)
SMEM = pl.BlockSpec(memory_space=pltpu.SMEM)
HBM = pl.BlockSpec(memory_space=pltpu.HBM)


def call(body, outs, ins, scratch=(), spaces=(), out_specs=None, params=PARAMS):
    spaces = dict(spaces)
    return pl.pallas_call(
        body,
        out_shape=outs,
        in_specs=[spaces.get(n, VMEM) for n in range(len(ins))],
        out_specs=out_specs or jax.tree.map(lambda _: VMEM, outs),
        scratch_shapes=list(scratch),
        compiler_params=params,
    )(*ins)


OUTER_SCRATCH = (
    pltpu.VMEM((TILES, 8 * ROWS, 2 * COLS), BF16),
    pltpu.VMEM((128, COLS), F32),
) + tuple(pltpu.VMEM((8 * ROWS, SPAN), F32) for _ in range(GROUP))
SPREAD_SCRATCH = (
    pltpu.VMEM((128, 2 * COLS), BF16),
    pltpu.VMEM((TILES, 4 * ROWS, 2 * COLS), F32),
)


def shape(*dims, dtype=F32):
    return jax.ShapeDtypeStruct(dims, dtype)


def exchanged(far, near):
    count = lax.axis_size("gb")
    ups = [(n, (n + 1) % count) for n in range(count)]
    results = []
    for value, parity in ((far, 1), (near, 0)):
        pairs = [pair for pair in ups if pair[0] % 2 == parity]
        pairs = pairs + [(target, source) for source, target in pairs]
        results.append(lax.ppermute(value, "gb", pairs))
    return results


def swapped(value):
    return lax.ppermute(value, "core", [(0, 1), (1, 0)])


def two_parts(value):
    high = value.astype(BF16)
    return high, (value - high.astype(F32)).astype(BF16)


def row_next(x):
    lane = lax.broadcasted_iota(I32, x.shape, 1)
    return jnp.where(lane == NROW - 1, 0.0, pltpu.roll(x, NROW - 1, 1))


def row_prev(x):
    lane = lax.broadcasted_iota(I32, x.shape, 1)
    return jnp.where(lane == 0, 0.0, pltpu.roll(x, 1, 1))


def col_next(x):
    return pltpu.roll(x, x.shape[0] - 1, 0)


def col_prev(x):
    return pltpu.roll(x, 1, 0)


def pack_kernel(
    count_hbm, adj_hbm, base_hbm, cell_hbm, mark_hbm, weight_hbm, out_ref,
    count_ref, adj_ref, base_ref, cell_ref, mark_ref, weight_ref, sems,
):
    copies = [
        pltpu.make_async_copy(src, dst, sems.at[n])
        for n, (src, dst) in enumerate(
            (
                (cell_hbm, cell_ref),
                (mark_hbm, mark_ref),
                (weight_hbm, weight_ref),
                (base_hbm, base_ref),
                (adj_hbm, adj_ref),
                (count_hbm, count_ref),
            )
        )
    ]
    for copy in copies:
        copy.start()
    copies[5].wait()
    copies[0].wait()
    copies[1].wait()
    lane = lax.broadcasted_iota(I32, (1, COLS), 1)
    none = jnp.zeros((4, COLS), F32)
    for e in range(GX):
        for q in range(2):
            rows = []
            for g in range(3):
                cell = cell_ref[g, e : e + 1, :]
                mark = mark_ref[g, e : e + 1, :]
                live = (lane < count_ref[0, 0, g, e]) & ((mark >> 11) == q)
                rows += [cell >> 7, cell & 127, jnp.where(live, (mark >> 7) & 15, -1), mark & 127]
            ints = jnp.concatenate([r.astype(F32) for r in rows] + [none], axis=0)
            out_ref[2 * e + q, 288:304, :] = ints.astype(BF16)
    copies[2].wait()
    for e in range(GX):
        for g in range(3):
            hi, lo = two_parts(weight_ref[g, e])
            for q in range(2):
                out_ref[2 * e + q, 192 + 16 * g : 208 + 16 * g, :] = hi
                out_ref[2 * e + q, 240 + 16 * g : 256 + 16 * g, :] = lo
    copies[3].wait()
    for p in range(2 * GX):
        for c in range(2):
            out_ref[p, 128 + c * ROWS : 128 + (c + 1) * ROWS, :] = base_ref[c, p]
    copies[4].wait()
    for p in range(2 * GX):
        for c in range(2):
            hi, lo = two_parts(adj_ref[c, p])
            out_ref[p, c * ROWS : (c + 1) * ROWS, :] = hi
            out_ref[p, 64 + c * ROWS : 64 + (c + 1) * ROWS, :] = lo


def closed_up(blocks):
    lane = lax.broadcasted_iota(I32, (1, 1, SPAN), 2)
    spot = lax.broadcasted_iota(I32, (1, 24, SPAN), 1)
    blank = jnp.where(spot == 20, -1.0, 0.0)
    for bit in range(9):
        step = 1 << bit
        goes = []
        stays = []
        for x in blocks:
            away = x[:, 20:21, :].astype(I32)
            flag = (away >> bit) & 1
            goes.append(jnp.where((away >= 0) & (flag == 1), 1.0, 0.0))
            stays.append((away >= 0) & (flag == 0))

        def ahead(values, n):
            if step >= SPAN:
                m = n + step // SPAN
                return values[m] if m < len(values) else None
            here = pltpu.roll(values[n], SPAN - step, 2)
            if n + 1 < len(values):
                there = pltpu.roll(values[n + 1], SPAN - step, 2)
            else:
                there = jnp.zeros_like(here)
            return jnp.where(lane < SPAN - step, here, there)

        result = []
        for n, x in enumerate(blocks):
            kept = jnp.where(stays[n], x, blank)
            coming = ahead(goes, n)
            if coming is None:
                result.append(kept)
            else:
                result.append(jnp.where(coming > 0.5, ahead(blocks, n), kept))
        blocks = result
    return blocks


def unpack_kernel(place_ref, got_ref, source_ref, adj_ref, base_ref, far_ref, near_ref):
    place = place_ref[0]
    for n in range(4):
        edges = []
        for side in range(2):
            parts = []
            for a in range(GX):
                d = 2 * a + side
                at = (n % 2) * ROWS
                if n < 2:
                    part = got_ref[d, at : at + ROWS, :].astype(F32)
                    part = part + got_ref[d, 64 + at : 64 + at + ROWS, :].astype(F32)
                else:
                    part = got_ref[d, 128 + at : 128 + at + ROWS, :].astype(F32)
                parts.append(part)
            turned = jnp.concatenate(parts, axis=0).T
            ref = adj_ref if n < 2 else base_ref
            ref[n % 2, side * COLS : (side + 1) * COLS, :] = turned
            edges.append(turned[:THIN] if side == 0 else turned[COLS - THIN :])
        far_ref[n], near_ref[n] = turned_round(place, *edges)
    for c in range(2):
        edges = [
            jnp.concatenate([source_ref[c, side, 0:8, :], source_ref[c, side, 8:16, :]], axis=1)
            for side in range(2)
        ]
        far_ref[4 + c], near_ref[4 + c] = turned_round(place, *edges)


def slots_kernel(got_ref, ints_ref, weight_ref, table_ref):
    ints = got_ref[:, 288:304, :].astype(F32)
    across = lax.broadcasted_iota(I32, (SPAN, SPAN), 0) <= lax.broadcasted_iota(
        I32, (SPAN, SPAN), 1
    )
    across = jnp.where(across, 1.0, 0.0).astype(BF16)
    live = []
    ranks = []
    total = jnp.zeros((TILES, SPAN), F32)
    for g in range(3):
        alive = jnp.where(ints[:, 4 * g + 2, :] >= 0.0, 1.0, 0.0)
        bits = alive.astype(BF16)
        live.append(alive)
        ranks.append(
            total + lax.dot_general(bits, across, NN, preferred_element_type=F32)
        )
        total = total + lax.dot_general(
            bits, jnp.ones((SPAN, SPAN), BF16), NN, preferred_element_type=F32
        )
    filled = jnp.int32(0)
    here = [
        (jnp.max(total[d : d + 1]).astype(I32) + SPAN - 1) // SPAN for d in range(TILES)
    ]
    for d in range(TILES):
        for n in range(DEPTH):

            @pl.when(n < here[d])
            def _():
                table_ref[filled + n] = d * DEPTH + n

        filled = filled + here[d]
    for n in range(GROUP):
        table_ref[filled + n] = EMPTY
    table_ref[COUNT_AT] = filled
    lane = lax.broadcasted_iota(I32, (TILES, SPAN), 1).astype(F32)
    spot = lax.broadcasted_iota(I32, (TILES, 8, SPAN), 1)
    side = (lax.broadcasted_iota(I32, (TILES, 1, SPAN), 0) & 1).astype(F32)
    blocks = []
    for g in range(3):
        away = jnp.where(live[g] > 0.5, lane + float(g * SPAN + 1) - ranks[g], -1.0)
        weights = got_ref[:, 192 + 16 * g : 208 + 16 * g, :].astype(F32)
        weights = weights + got_ref[:, 240 + 16 * g : 256 + 16 * g, :].astype(F32)
        rows = [ints[:, 4 * g + n : 4 * g + n + 1, :] for n in range(4)]
        rows[2] = rows[2] + 16.0 * (side + float(g))
        rest = jnp.zeros((TILES, 8, SPAN), F32)
        for n, row in enumerate(rows + [away[:, None, :]]):
            rest = jnp.where(spot == n, row, rest)
        blocks.append(jnp.concatenate([weights, rest], axis=1))
    for n, block in enumerate(closed_up(blocks)):
        for d in range(TILES):
            weight_ref[d * DEPTH + n] = block[d, :16]
            ints_ref[d * DEPTH + n] = block[d, 16:].astype(I32)
    weight_ref[EMPTY] = jnp.zeros((16, SPAN), F32)
    ints_ref[EMPTY] = jnp.zeros((8, SPAN), I32)


def one_hot(index, count):
    spot = lax.broadcasted_iota(I32, (count, index.shape[1]), 0)
    return jnp.where(spot == index, 1.0, 0.0).astype(BF16)


def row_weights(first_row, weights):
    off = lax.broadcasted_iota(I32, (ROWS, SPAN), 0) - first_row
    hits = [off == n for n in range(4)]
    tables = []
    for dj in range(4):
        table = jnp.zeros((ROWS, SPAN), F32)
        for di in (3, 2, 1, 0):
            row = weights[4 * di + dj : 4 * di + dj + 1]
            table = jnp.where(hits[di], row, table)
        tables.append(table)
    return tables


def group_of(table_ref, n):
    ids = [table_ref[GROUP * n + m] for m in range(GROUP)]
    return ids, [jnp.minimum(block // DEPTH, TILES - 1) for block in ids]


def groups(table_ref):
    return (table_ref[COUNT_AT] + GROUP - 1) // GROUP


def joined(ref, ids, row):
    return jnp.concatenate([ref[block, row : row + 1, :] for block in ids], axis=1)


def turned_round(place, one, other):
    odd = (place & 1) == 1
    return jnp.where(odd, other, one), jnp.where(odd, one, other)


def neighbours(place):
    return jnp.where(place == 0, 0.0, 1.0), jnp.where(place == LAST, 0.0, 1.0)


def masked(place):
    has_low, has_high = neighbours(place)

    def inside(x):
        width = x.shape[0]
        return jnp.concatenate(
            [x[:RIM] * has_low, x[RIM : width - RIM], x[width - RIM :] * has_high], axis=0
        )

    return inside


def projected(wide, inside=lambda x: x):
    div = 0.5 * (row_next(wide[0]) - row_prev(wide[0])) + 0.5 * (
        col_next(wide[1]) - col_prev(wide[1])
    )
    pressure = inside(-0.25 * div)
    for sweep in range(SWEEPS - 1):
        pressure = inside(
            0.25
            * (
                row_next(pressure)
                + row_prev(pressure)
                + col_next(pressure)
                + col_prev(pressure)
                - div
            )
        )
    first = wide[0] - 0.5 * (row_next(pressure) - row_prev(pressure))
    second = wide[1] - 0.5 * (col_next(pressure) - col_prev(pressure))
    return inside(first), inside(second)


def strips(low, mid_ref, high, c):
    return jnp.concatenate(
        [low, mid_ref[c, : 2 * RIM, :], mid_ref[c, NCOL - 2 * RIM :, :], high], axis=0
    )


def rim_strips(place, far_ref, mid_ref, near_ref, inside):
    result = []
    for c in range(2):
        low, high = turned_round(place, far_ref[c].astype(F32), near_ref[c].astype(F32))
        result.append(inside(strips(low, mid_ref, high, c)))
    return result


def outer_columns(x):
    return x[RIM : 2 * RIM], x[2 * STRIP - 2 * RIM : 2 * STRIP - RIM]


def transported(w, base):
    ux = 0.5 * (row_next(base[0]) - row_prev(base[0]))
    vx = 0.5 * (row_next(base[1]) - row_prev(base[1]))
    uy = 0.5 * (col_next(base[0]) - col_prev(base[0]))
    vy = 0.5 * (col_next(base[1]) - col_prev(base[1]))
    mixed = (ux * w[0] + vx * w[1], uy * w[0] + vy * w[1])
    out = []
    for c in range(2):
        east, west = row_next(w[c]), row_prev(w[c])
        north, south = col_next(w[c]), col_prev(w[c])
        laplace = east + west + north + south - 4.0 * w[c]
        value = w[c] + TIME_STEP * (
            base[0] * (0.5 * (east - west))
            + base[1] * (0.5 * (north - south))
            - mixed[c]
            + VISCOSITY * laplace
        )
        out.append(value)
    return out


def interpolate(table_ref, ints_ref, weight_ref, pick_ref, got_refs, sum_ref):
    def blocks(n, carry):
        ids, tiles = group_of(table_ref, n)
        for block, tile, got_ref in zip(ids, tiles, got_refs):
            cols = one_hot(ints_ref[block, 1:2, :], COLS)
            got_ref[...] = lax.dot_general(
                pick_ref[tile],
                jnp.concatenate([cols, cols], axis=0),
                NN,
                preferred_element_type=F32,
            )
        values = []
        for block, got_ref in zip(ids, got_refs):
            tables = row_weights(ints_ref[block, 0:1, :], weight_ref[block])
            both = []
            for c in range(2):
                total = jnp.zeros((ROWS, SPAN), F32)
                for dj in range(4):
                    at = (dj * 2 + c) * ROWS
                    total = total + tables[dj] * got_ref[at : at + ROWS, :]
                both.append(jnp.sum(total, axis=0, keepdims=True))
            values.append(both)
        high = lax.broadcasted_iota(I32, (64, GROUP * SPAN), 0) == joined(ints_ref, ids, 2)
        parts = [
            two_parts(jnp.where(high, jnp.concatenate([v[c] for v in values], axis=1), 0.0))
            for c in range(2)
        ]
        stacked = jnp.concatenate([parts[0][0], parts[1][0], parts[0][1], parts[1][1]], axis=0)
        both = lax.dot_general(
            one_hot(joined(ints_ref, ids, 3), COLS), stacked, NT, preferred_element_type=F32
        )
        sum_ref[...] = sum_ref[...] + (both[:, :128] + both[:, 128:])
        return carry

    sum_ref[...] = jnp.zeros(sum_ref.shape, F32)
    lax.fori_loop(0, groups(table_ref), blocks, 0)


def pick(field, c, side, pick_ref):
    for dj in range(4):
        shifted = pltpu.roll(field, COLS - dj, 1) if dj else field
        both = jnp.concatenate(two_parts(shifted), axis=1)
        at = (dj * 2 + c) * ROWS
        for a in range(GX):
            pick_ref[2 * a + side, at : at + ROWS, :] = both[a * ROWS : (a + 1) * ROWS]


def inner_kernel(first, mid_ref, base_ref, moved_ref):
    w = [mid_ref[c] for c in range(2)]
    if not first:
        w = projected(w)
    out = transported(w, [base_ref[c] for c in range(2)])
    for c in range(2):
        moved_ref[c] = out[c]


def outer_kernel(
    first, place_ref, table_ref, far_ref, mid_ref, near_ref, base_far_ref, base_ref,
    base_near_ref, ints_ref, weight_ref, inner_ref, moved_ref, part_far, part_near,
    pick_ref, sum_ref, *got_refs,
):
    place = place_ref[0]
    inside = masked(place)
    blank = jnp.zeros((RIM - THIN, NROW), F32)

    def thin_strips(far, mid, near, c, at):
        low, high = turned_round(place, far[at + c], near[at + c])
        return inside(
            strips(
                jnp.concatenate([blank, low], axis=0),
                mid,
                jnp.concatenate([high, blank], axis=0),
                c,
            )
        )

    base = [thin_strips(base_far_ref, base_ref, base_near_ref, c, 2) for c in range(2)]
    if first:
        w = [thin_strips(far_ref, mid_ref, near_ref, c, 0) for c in range(2)]
    else:
        w = projected(rim_strips(place, far_ref, mid_ref, near_ref, inside), inside)
    out = transported(w, base)
    for c in range(2):
        low, high = outer_columns(out[c])
        moved = [
            jnp.concatenate([low, inner_ref[c, RIM:COLS, :]], axis=0),
            jnp.concatenate([inner_ref[c, COLS : NCOL - RIM, :], high], axis=0),
        ]
        for side in range(2):
            moved_ref[c, side * COLS : (side + 1) * COLS, :] = moved[side]
            pick(moved[side].T, c, side, pick_ref)
    interpolate(table_ref, ints_ref, weight_ref, pick_ref, got_refs, sum_ref)
    sums = sum_ref[...].T
    for c in range(2):
        part_far[c], part_near[c] = turned_round(
            place, sums[64 * c : 64 * c + 32, :], sums[64 * c + 32 : 64 * c + 64, :]
        )


def tables_kernel(table_ref, ints_ref, weight_ref, out_ref):
    def block(n, carry):
        ids, _ = group_of(table_ref, n)
        for block in ids:
            tables = row_weights(ints_ref[block, 0:1, :], weight_ref[block])
            out_ref[block] = jnp.concatenate(
                two_parts(jnp.concatenate(tables, axis=0)), axis=1
            )
        return carry

    out_ref[EMPTY] = jnp.zeros((4 * ROWS, 2 * SPAN), BF16)
    lax.fori_loop(0, groups(table_ref), block, 0)


def force_of(sums, source):
    row = lax.broadcasted_iota(I32, sums.shape, 0) & 3
    lane = lax.broadcasted_iota(I32, sums.shape, 1)
    count = sums.shape[0]
    up = jnp.where(row == 0, pltpu.roll(sums, count - 3, 0), pltpu.roll(sums, 1, 0))
    down = jnp.where(row == 3, pltpu.roll(sums, 3, 0), pltpu.roll(sums, count - 1, 0))
    before = jnp.where(lane == 0, pltpu.roll(up, 1, 1), pltpu.roll(sums, 1, 1))
    after = jnp.where(lane == 127, pltpu.roll(down, 127, 1), pltpu.roll(sums, 127, 1))
    bent = before + after - 2.0 * sums
    return STIFFNESS * (sums + source - BENDING * bent)


def spread_kernel(
    place_ref, table_ref, part_far, part_near, from_far, from_near, thin_far, source_ref, thin_near,
    moved_ref, ints_ref, row_ref, out_ref, edge_far, edge_near, own_ref,
    force_ref, acc_ref,
):
    place = place_ref[0]
    has_low, has_high = neighbours(place)
    has_far, has_near = turned_round(place, has_low, has_high)
    for c in range(2):
        outer = turned_round(
            place,
            *[
                jnp.concatenate([ref[4 + c, :, :COLS], ref[4 + c, :, COLS:]], axis=0)
                for ref in (thin_far, thin_near)
            ],
        )
        source = jnp.concatenate(
            [outer[0], source_ref[c, 0], source_ref[c, 1], outer[1]], axis=0
        )
        sums = jnp.concatenate(
            turned_round(
                place,
                part_far[c] + from_far[c] * has_far,
                part_near[c] + from_near[c] * has_near,
            ),
            axis=0,
        )
        force = force_of(sums, source)
        own_ref[c, 0] = force[16:32]
        own_ref[c, 1] = force[32:48]
        hi, lo = two_parts(force)
        force_ref[64 * c : 64 * c + 64, :] = jnp.concatenate([hi, lo], axis=1)
    acc_ref[...] = jnp.zeros(acc_ref.shape, F32)

    def blocks(n, carry):
        ids, tiles = group_of(table_ref, n)
        spots = one_hot(joined(ints_ref, ids, 3), COLS)
        picked = lax.dot_general(
            force_ref[...], jnp.concatenate([spots, spots], axis=0), NN,
            preferred_element_type=F32,
        )
        high = lax.broadcasted_iota(I32, (64, GROUP * SPAN), 0) == joined(ints_ref, ids, 2)
        parts = []
        for c in range(2):
            force = TIME_STEP * jnp.sum(
                jnp.where(high, picked[64 * c : 64 * c + 64], 0.0), axis=0, keepdims=True
            )
            parts.append([x.astype(F32) for x in two_parts(force)])
        sums = []
        for m, block in enumerate(ids):
            lanes = slice(m * SPAN, (m + 1) * SPAN)
            cols = lax.broadcasted_iota(I32, (COLS, SPAN), 0) == ints_ref[block, 1:2, :]
            hi, lo = (
                jnp.concatenate(
                    [jnp.where(cols, parts[c][k][:, lanes], 0.0).astype(BF16) for c in range(2)],
                    axis=0,
                )
                for k in range(2)
            )
            sums.append(
                lax.dot_general(
                    row_ref[block],
                    jnp.concatenate([hi, hi], axis=1),
                    NT,
                    preferred_element_type=F32,
                )
                + lax.dot_general(row_ref[block, :, :SPAN], lo, NT, preferred_element_type=F32)
            )
        for tile, one in zip(tiles, sums):
            acc_ref[tile] = acc_ref[tile] + one
        return carry

    lax.fori_loop(0, groups(table_ref), blocks, 0)
    for c in range(2):
        edges = []
        for side in range(2):
            rows = []
            for a in range(GX):
                total = jnp.zeros((ROWS, COLS), F32)
                for dj in range(4):
                    one = acc_ref[
                        2 * a + side, dj * ROWS : (dj + 1) * ROWS, c * COLS : (c + 1) * COLS
                    ]
                    total = total + (pltpu.roll(one, dj, 1) if dj else one)
                rows.append(total)
            cols = slice(side * COLS, (side + 1) * COLS)
            total = moved_ref[c, cols, :] + jnp.concatenate(rows, axis=0).T
            out_ref[c, cols, :] = total
            edges.append(total[:RIM] if side == 0 else total[COLS - RIM :])
        far, near = turned_round(place, *edges)
        edge_far[c] = far.astype(BF16)
        edge_near[c] = near.astype(BF16)


def finish_inner_kernel(mid_ref, out_ref):
    w = projected([mid_ref[c] for c in range(2)])
    for c in range(2):
        for side in range(2):
            block = w[c][side * COLS : (side + 1) * COLS].T
            for a in range(GX):
                out_ref[2 * a + side, c] = block[a * ROWS : (a + 1) * ROWS]


def finish_outer_kernel(place_ref, far_ref, mid_ref, near_ref, inner_ref, out_ref):
    place = place_ref[0]
    inside = masked(place)
    w = projected(rim_strips(place, far_ref, mid_ref, near_ref, inside), inside)
    blank = jnp.zeros((COLS - 2 * RIM, NROW), F32)
    lane = lax.broadcasted_iota(I32, (ROWS, COLS), 1)
    for c in range(2):
        low, high = outer_columns(w[c])
        both = jnp.concatenate([low, blank, high], axis=0).T
        for a in range(GX):
            rows = both[a * ROWS : (a + 1) * ROWS]
            out_ref[2 * a, c] = jnp.where(lane < RIM, rows, inner_ref[2 * a, c])
            out_ref[2 * a + 1, c] = jnp.where(lane >= COLS - RIM, rows, inner_ref[2 * a + 1, c])


def on_device(adjoint, base_flow, slot_cell, slot_marker, slot_count, slot_weight, marker_source):
    place = lax.axis_index("gb").astype(I32).reshape(1)
    core = lax.axis_index("core")
    whole = ("gx", "core")
    tiles = marker_source.reshape(2, 2, 16, COLS)
    kept = lax.dynamic_index_in_dim(tiles, core, axis=1, keepdims=False)
    other = swapped(lax.dynamic_index_in_dim(tiles, 1 - core, axis=1, keepdims=False))
    source = jnp.where(
        core == 0, jnp.stack([kept, other], axis=1), jnp.stack([other, kept], axis=1)
    )
    packed = call(
        pack_kernel,
        shape(2 * GX, PACK, COLS, dtype=BF16),
        (slot_count, adjoint, base_flow, slot_cell[0, 0], slot_marker[0, 0], slot_weight[0, 0]),
        scratch=(
            pltpu.SMEM((1, 1, 3, GX), I32),
            pltpu.VMEM(adjoint.shape, F32),
            pltpu.VMEM(base_flow.shape, BF16),
            pltpu.VMEM((3, GX, COLS), I32),
            pltpu.VMEM((3, GX, COLS), I32),
            pltpu.VMEM((3, GX, 16, COLS), F32),
            pltpu.SemaphoreType.DMA((6,)),
        ),
        spaces={n: HBM for n in range(6)},
        params=ROOMY,
    )
    got = lax.all_to_all(packed, whole, split_axis=0, concat_axis=0, tiled=True)
    field = shape(2, NCOL, NROW)
    thin = shape(6, THIN, NROW)
    current, base, thin_far, thin_near = call(
        unpack_kernel, (field, field, thin, thin), (place, got, source), spaces={0: SMEM}
    )
    base_far, base_near = exchanged(thin_far, thin_near)
    ints, weights, table = call(
        slots_kernel,
        (
            shape(EMPTY + 1, 8, SPAN, dtype=I32),
            shape(EMPTY + 1, 16, SPAN),
            shape(64, dtype=I32),
        ),
        (got,),
        out_specs=(VMEM, VMEM, SMEM),
    )
    far, near = base_far, base_near
    part = shape(2, 32, COLS)
    rim = shape(2, RIM, NROW, dtype=BF16)
    forces = source
    tables = None
    for substep in range(SUBSTEPS):
        inner = call(
            functools.partial(inner_kernel, substep == 0), field, (current, base)
        )
        moved, part_far, part_near = call(
            functools.partial(outer_kernel, substep == 0),
            (field, part, part),
            (place, table, far, current, near, base_far, base, base_near, ints, weights, inner),
            scratch=OUTER_SCRATCH,
            spaces={0: SMEM, 1: SMEM},
        )
        from_far, from_near = exchanged(part_far, part_near)
        if substep == 0:
            tables = call(
                tables_kernel,
                shape(EMPTY + 1, 4 * ROWS, 2 * SPAN, dtype=BF16),
                (table, ints, weights),
                spaces={0: SMEM},
            )
        current, edge_far, edge_near, forces = call(
            spread_kernel,
            (field, rim, rim, shape(2, 2, 16, COLS)),
            (
                place, table, part_far, part_near, from_far, from_near, base_far, source,
                base_near, moved, ints, tables,
            ),
            scratch=SPREAD_SCRATCH,
            spaces={0: SMEM, 1: SMEM},
        )
        far, near = exchanged(edge_far, edge_near)
    tiles_out = shape(2 * GX, 2, ROWS, COLS)
    inner = call(finish_inner_kernel, tiles_out, (current,))
    done = call(
        finish_outer_kernel, tiles_out, (place, far, current, near, inner), spaces={0: SMEM}
    )
    back = lax.all_to_all(done, whole, split_axis=0, concat_axis=0, tiled=True)
    result = jnp.transpose(back, (1, 0, 2, 3))
    mine = lax.dynamic_index_in_dim(forces, core, axis=1, keepdims=False)
    theirs = swapped(lax.dynamic_index_in_dim(forces, 1 - core, axis=1, keepdims=False))
    planes = jnp.where(
        core == 0, jnp.stack([mine, theirs], axis=1), jnp.stack([theirs, mine], axis=1)
    )
    return (result, planes.reshape(marker_source.shape))


def solution(mesh):
    split = Mesh(mesh.devices.reshape(8, 8, 2), ("gx", "gb", "core"))
    gy = ("gb", "core")
    in_specs = (
        P(None, None, "gx", gy),
        P(None, None, "gx", gy),
        P("gx", gy, None, None, None),
        P("gx", gy, None, None, None),
        P("gx", gy, None, None),
        P("gx", gy, None, None, None, None),
        P(None, "gx", gy, None),
    )
    out_specs = (P(None, None, "gx", gy), P(None, "gx", gy, None))
    return jax.shard_map(
        on_device, mesh=split, in_specs=in_specs, out_specs=out_specs, check_vma=False
    )
```

```python
import functools

import jax
import jax.numpy as jnp
from jax import lax
from jax.experimental import pallas as pl
from jax.experimental.pallas import tpu as pltpu
from jax.sharding import Mesh, PartitionSpec as P

SUBSTEPS = 3
SWEEPS = 8

TIME_STEP = 0.5
VISCOSITY = 0.2
STIFFNESS = 2.0
BENDING = 0.25

F32 = jnp.float32
BF16 = jnp.bfloat16
I32 = jnp.int32

GX = 8
ROWS = 32
COLS = 128
NROW = GX * ROWS
NCOL = 2 * COLS
LAST = 7
RIM = 16
STRIP = 2 * RIM
THIN = 8
KEPT = 192
PACK = 304
SPAN = 128
TILES = 2 * GX
DEPTH = 3
EMPTY = TILES * DEPTH
COUNT_AT = 127
GROUP = 24

NT = (((1,), (1,)), ((), ()))
NN = (((1,), (0,)), ((), ()))

PARAMS = pltpu.CompilerParams(vmem_limit_bytes=24 * 1024 * 1024)
ROOMY = pltpu.CompilerParams(vmem_limit_bytes=60 * 1024 * 1024)
VMEM = pl.BlockSpec(memory_space=pltpu.VMEM)
SMEM = pl.BlockSpec(memory_space=pltpu.SMEM)
HBM = pl.BlockSpec(memory_space=pltpu.HBM)


def call(body, outs, ins, scratch=(), spaces=(), out_specs=None, params=PARAMS):
    spaces = dict(spaces)
    return pl.pallas_call(
        body,
        out_shape=outs,
        in_specs=[spaces.get(n, VMEM) for n in range(len(ins))],
        out_specs=out_specs or jax.tree.map(lambda _: VMEM, outs),
        scratch_shapes=list(scratch),
        compiler_params=params,
    )(*ins)


OUTER_SCRATCH = (
    pltpu.VMEM((TILES, 8 * ROWS, 2 * COLS), BF16),
    pltpu.VMEM((COLS, 2 * KEPT), F32),
) + tuple(pltpu.VMEM((8 * ROWS, SPAN), F32) for _ in range(GROUP))
SPREAD_SCRATCH = (
    pltpu.VMEM((KEPT, 2 * COLS), BF16),
    pltpu.VMEM((TILES, 4 * ROWS, 2 * COLS), F32),
)


def shape(*dims, dtype=F32):
    return jax.ShapeDtypeStruct(dims, dtype)


def exchanged(far, near, step=1):
    count = lax.axis_size("zc")
    ups = [(n, (n + step) % count) for n in range(count)]
    results = []
    for value, parity in ((far, 1), (near, 0)):
        pairs = [pair for pair in ups if (pair[0] // step) % 2 == parity]
        pairs = pairs + [(target, source) for source, target in pairs]
        results.append(lax.ppermute(value, "zc", pairs))
    return results


def swapped(value):
    return lax.ppermute(value, "xh", [(0, 1), (1, 0)])


def two_parts(value):
    high = value.astype(BF16)
    return high, (value - high.astype(F32)).astype(BF16)


def row_next(x):
    lane = lax.broadcasted_iota(I32, x.shape, 1)
    return jnp.where(lane == NROW - 1, 0.0, pltpu.roll(x, NROW - 1, 1))


def row_prev(x):
    lane = lax.broadcasted_iota(I32, x.shape, 1)
    return jnp.where(lane == 0, 0.0, pltpu.roll(x, 1, 1))


def col_next(x):
    return pltpu.roll(x, x.shape[0] - 1, 0)


def col_prev(x):
    return pltpu.roll(x, 1, 0)


def pack_kernel(
    count_hbm, adj_hbm, base_hbm, cell_hbm, mark_hbm, weight_hbm, out_ref,
    count_ref, adj_ref, base_ref, cell_ref, mark_ref, weight_ref, sems,
):
    copies = [
        pltpu.make_async_copy(src, dst, sems.at[n])
        for n, (src, dst) in enumerate(
            (
                (cell_hbm, cell_ref),
                (mark_hbm, mark_ref),
                (weight_hbm, weight_ref),
                (base_hbm, base_ref),
                (adj_hbm, adj_ref),
                (count_hbm, count_ref),
            )
        )
    ]
    for copy in copies:
        copy.start()
    copies[5].wait()
    copies[0].wait()
    copies[1].wait()
    lane = lax.broadcasted_iota(I32, (1, COLS), 1)
    none = jnp.zeros((4, COLS), F32)
    for e in range(GX):
        for q in range(2):
            rows = []
            for g in range(3):
                cell = cell_ref[g, e : e + 1, :]
                mark = mark_ref[g, e : e + 1, :]
                live = (lane < count_ref[0, 0, g, e]) & ((mark >> 11) == q)
                rows += [cell >> 7, cell & 127, jnp.where(live, (mark >> 7) & 15, -1), mark & 127]
            ints = jnp.concatenate([r.astype(F32) for r in rows] + [none], axis=0)
            out_ref[2 * e + q, 288:304, :] = ints.astype(BF16)
    copies[2].wait()
    for e in range(GX):
        for g in range(3):
            hi, lo = two_parts(weight_ref[g, e])
            for q in range(2):
                out_ref[2 * e + q, 192 + 16 * g : 208 + 16 * g, :] = hi
                out_ref[2 * e + q, 240 + 16 * g : 256 + 16 * g, :] = lo
    copies[3].wait()
    for p in range(2 * GX):
        for c in range(2):
            out_ref[p, 128 + c * ROWS : 128 + (c + 1) * ROWS, :] = base_ref[c, p]
    copies[4].wait()
    for p in range(2 * GX):
        for c in range(2):
            hi, lo = two_parts(adj_ref[c, p])
            out_ref[p, c * ROWS : (c + 1) * ROWS, :] = hi
            out_ref[p, 64 + c * ROWS : 64 + (c + 1) * ROWS, :] = lo


def closed_up(blocks):
    lane = lax.broadcasted_iota(I32, (1, 1, SPAN), 2)
    spot = lax.broadcasted_iota(I32, (1, 24, SPAN), 1)
    blank = jnp.where(spot == 20, -1.0, 0.0)
    for bit in range(9):
        step = 1 << bit
        goes = []
        stays = []
        for x in blocks:
            away = x[:, 20:21, :].astype(I32)
            flag = (away >> bit) & 1
            goes.append(jnp.where((away >= 0) & (flag == 1), 1.0, 0.0))
            stays.append((away >= 0) & (flag == 0))

        def ahead(values, n):
            if step >= SPAN:
                m = n + step // SPAN
                return values[m] if m < len(values) else None
            here = pltpu.roll(values[n], SPAN - step, 2)
            if n + 1 < len(values):
                there = pltpu.roll(values[n + 1], SPAN - step, 2)
            else:
                there = jnp.zeros_like(here)
            return jnp.where(lane < SPAN - step, here, there)

        result = []
        for n, x in enumerate(blocks):
            kept = jnp.where(stays[n], x, blank)
            coming = ahead(goes, n)
            if coming is None:
                result.append(kept)
            else:
                result.append(jnp.where(coming > 0.5, ahead(blocks, n), kept))
        blocks = result
    return blocks


def unpack_kernel(place_ref, got_ref, source_ref, adj_ref, base_ref, far_ref, near_ref):
    place = place_ref[0]
    for n in range(4):
        for side in range(2):
            parts = []
            for a in range(GX):
                d = 2 * a + side
                at = (n % 2) * ROWS
                if n < 2:
                    part = got_ref[d, at : at + ROWS, :].astype(F32)
                    part = part + got_ref[d, 64 + at : 64 + at + ROWS, :].astype(F32)
                else:
                    part = got_ref[d, 128 + at : 128 + at + ROWS, :].astype(F32)
                parts.append(part)
            turned = jnp.concatenate(parts, axis=0).T
            ref = adj_ref if n < 2 else base_ref
            ref[n % 2, side * COLS : (side + 1) * COLS, :] = turned
            far_ref[side, n], near_ref[side, n] = turned_round(
                place, turned[:THIN], turned[COLS - THIN :]
            )
    for c in range(2):
        for side in range(2):
            both = jnp.concatenate(
                [source_ref[c, side, 0:8, :], source_ref[c, side, 8:16, :]], axis=1
            )
            far_ref[side, 4 + c] = both
            near_ref[side, 4 + c] = both


def slots_kernel(got_ref, ints_ref, weight_ref, table_ref):
    ints = got_ref[:, 288:304, :].astype(F32)
    across = lax.broadcasted_iota(I32, (SPAN, SPAN), 0) <= lax.broadcasted_iota(
        I32, (SPAN, SPAN), 1
    )
    across = jnp.where(across, 1.0, 0.0).astype(BF16)
    live = []
    ranks = []
    total = jnp.zeros((TILES, SPAN), F32)
    for g in range(3):
        alive = jnp.where(ints[:, 4 * g + 2, :] >= 0.0, 1.0, 0.0)
        bits = alive.astype(BF16)
        live.append(alive)
        ranks.append(
            total + lax.dot_general(bits, across, NN, preferred_element_type=F32)
        )
        total = total + lax.dot_general(
            bits, jnp.ones((SPAN, SPAN), BF16), NN, preferred_element_type=F32
        )
    filled = jnp.int32(0)
    here = [
        (jnp.max(total[d : d + 1]).astype(I32) + SPAN - 1) // SPAN for d in range(TILES)
    ]
    for d in range(TILES):
        for n in range(DEPTH):

            @pl.when(n < here[d])
            def _():
                table_ref[filled + n] = d * DEPTH + n

        filled = filled + here[d]
    for n in range(GROUP):
        table_ref[filled + n] = EMPTY
    table_ref[COUNT_AT] = filled
    lane = lax.broadcasted_iota(I32, (TILES, SPAN), 1).astype(F32)
    spot = lax.broadcasted_iota(I32, (TILES, 8, SPAN), 1)
    side = (lax.broadcasted_iota(I32, (TILES, 1, SPAN), 0) & 1).astype(F32)
    blocks = []
    for g in range(3):
        away = jnp.where(live[g] > 0.5, lane + float(g * SPAN + 1) - ranks[g], -1.0)
        weights = got_ref[:, 192 + 16 * g : 208 + 16 * g, :].astype(F32)
        weights = weights + got_ref[:, 240 + 16 * g : 256 + 16 * g, :].astype(F32)
        rows = [ints[:, 4 * g + n : 4 * g + n + 1, :] for n in range(4)]
        rows[2] = rows[2] + 48.0 * side + float(16 * g)
        rest = jnp.zeros((TILES, 8, SPAN), F32)
        for n, row in enumerate(rows + [away[:, None, :]]):
            rest = jnp.where(spot == n, row, rest)
        blocks.append(jnp.concatenate([weights, rest], axis=1))
    for n, block in enumerate(closed_up(blocks)):
        for d in range(TILES):
            weight_ref[d * DEPTH + n] = block[d, :16]
            ints_ref[d * DEPTH + n] = block[d, 16:].astype(I32)
    weight_ref[EMPTY] = jnp.zeros((16, SPAN), F32)
    ints_ref[EMPTY] = jnp.zeros((8, SPAN), I32)


def one_hot(index, count):
    spot = lax.broadcasted_iota(I32, (count, index.shape[1]), 0)
    return jnp.where(spot == index, 1.0, 0.0).astype(BF16)


def row_weights(first_row, weights):
    off = lax.broadcasted_iota(I32, (ROWS, SPAN), 0) - first_row
    hits = [off == n for n in range(4)]
    tables = []
    for dj in range(4):
        table = jnp.zeros((ROWS, SPAN), F32)
        for di in (3, 2, 1, 0):
            row = weights[4 * di + dj : 4 * di + dj + 1]
            table = jnp.where(hits[di], row, table)
        tables.append(table)
    return tables


def group_of(table_ref, n):
    ids = [table_ref[GROUP * n + m] for m in range(GROUP)]
    return ids, [jnp.minimum(block // DEPTH, TILES - 1) for block in ids]


def groups(table_ref):
    return (table_ref[COUNT_AT] + GROUP - 1) // GROUP


def joined(ref, ids, row):
    return jnp.concatenate([ref[block, row : row + 1, :] for block in ids], axis=1)


def turned_round(place, one, other):
    odd = (place & 1) == 1
    return jnp.where(odd, other, one), jnp.where(odd, one, other)


def neighbours(place):
    return jnp.where(place == 0, 0.0, 1.0), jnp.where(place == LAST, 0.0, 1.0)


def meeting(place, low, high, reach=1):
    start = place < reach
    end = place > LAST - reach
    has_low = jnp.where(start, 0.0, 1.0)
    has_high = jnp.where(end, 0.0, 1.0)
    lows = (low[0] * has_low, jnp.where(start, low[0], low[1]))
    highs = (jnp.where(end, high[1], high[0]), high[1] * has_high)
    return lows, highs


def masked(place):
    has_low, has_high = neighbours(place)

    def inside(x):
        width = x.shape[0]
        return jnp.concatenate(
            [x[:RIM] * has_low, x[RIM : width - RIM], x[width - RIM :] * has_high], axis=0
        )

    return inside


def projected(wide, inside=lambda x: x):
    div = 0.5 * (row_next(wide[0]) - row_prev(wide[0])) + 0.5 * (
        col_next(wide[1]) - col_prev(wide[1])
    )
    pressure = inside(-0.25 * div)
    for sweep in range(SWEEPS - 1):
        pressure = inside(
            0.25
            * (
                row_next(pressure)
                + row_prev(pressure)
                + col_next(pressure)
                + col_prev(pressure)
                - div
            )
        )
    first = wide[0] - 0.5 * (row_next(pressure) - row_prev(pressure))
    second = wide[1] - 0.5 * (col_next(pressure) - col_prev(pressure))
    return inside(first), inside(second)


def strips(lows, highs, mid_ref, c):
    parts = []
    for side in range(2):
        at = side * COLS
        if mid_ref is None:
            inner = [jnp.zeros((RIM, NROW), F32)] * 2
        else:
            inner = [
                mid_ref[c, at : at + RIM, :],
                mid_ref[c, at + COLS - RIM : at + COLS, :],
            ]
        parts += [lows[side], inner[0], inner[1], highs[side]]
    return jnp.concatenate(parts, axis=0)


def rim_strips(place, far_ref, near_ref):
    result = []
    for c in range(2):
        pairs = [
            turned_round(place, far_ref[side, c].astype(F32), near_ref[side, c].astype(F32))
            for side in range(2)
        ]
        result.append(strips(*meeting(place, *zip(*pairs)), None, c))
    return result


def thin_rims(place, far, near, at):
    pairs = [turned_round(place, far[side, at], near[side, at]) for side in range(2)]
    return meeting(place, *zip(*pairs))


def outer_columns(x, side):
    at = side * 2 * STRIP
    return x[at + RIM : at + 2 * RIM], x[at + STRIP : at + STRIP + RIM]


def widened(mid_ref, c, lows, highs):
    parts = []
    for side in range(2):
        parts += [lows[side], mid_ref[c, side * COLS : (side + 1) * COLS, :], highs[side]]
    return jnp.concatenate(parts, axis=0)


def wide_projected(place, mid_ref):
    blank = (jnp.zeros((RIM, NROW), F32),) * 2
    return projected([widened(mid_ref, c, blank, blank) for c in range(2)], masked(place))


def transported(w, base):
    ux = 0.5 * (row_next(base[0]) - row_prev(base[0]))
    vx = 0.5 * (row_next(base[1]) - row_prev(base[1]))
    uy = 0.5 * (col_next(base[0]) - col_prev(base[0]))
    vy = 0.5 * (col_next(base[1]) - col_prev(base[1]))
    mixed = (ux * w[0] + vx * w[1], uy * w[0] + vy * w[1])
    out = []
    for c in range(2):
        east, west = row_next(w[c]), row_prev(w[c])
        north, south = col_next(w[c]), col_prev(w[c])
        laplace = east + west + north + south - 4.0 * w[c]
        value = w[c] + TIME_STEP * (
            base[0] * (0.5 * (east - west))
            + base[1] * (0.5 * (north - south))
            - mixed[c]
            + VISCOSITY * laplace
        )
        out.append(value)
    return out


def interpolate(table_ref, ints_ref, weight_ref, pick_ref, got_refs, sum_ref):
    def blocks(n, carry):
        ids, tiles = group_of(table_ref, n)
        for block, tile, got_ref in zip(ids, tiles, got_refs):
            cols = one_hot(ints_ref[block, 1:2, :], COLS)
            got_ref[...] = lax.dot_general(
                pick_ref[tile],
                jnp.concatenate([cols, cols], axis=0),
                NN,
                preferred_element_type=F32,
            )
        values = []
        for block, got_ref in zip(ids, got_refs):
            tables = row_weights(ints_ref[block, 0:1, :], weight_ref[block])
            both = []
            for c in range(2):
                total = jnp.zeros((ROWS, SPAN), F32)
                for dj in range(4):
                    at = (dj * 2 + c) * ROWS
                    total = total + tables[dj] * got_ref[at : at + ROWS, :]
                both.append(jnp.sum(total, axis=0, keepdims=True))
            values.append(both)
        high = lax.broadcasted_iota(I32, (96, GROUP * SPAN), 0) == joined(ints_ref, ids, 2)
        parts = [two_parts(jnp.concatenate([v[c] for v in values], axis=1)) for c in range(2)]
        stacked = jnp.concatenate(
            [
                jnp.where(high, parts[c][k].astype(F32), 0.0).astype(BF16)
                for k in range(2)
                for c in range(2)
            ],
            axis=0,
        )
        both = lax.dot_general(
            one_hot(joined(ints_ref, ids, 3), COLS), stacked, NT, preferred_element_type=F32
        )
        sum_ref[...] = sum_ref[...] + both
        return carry

    sum_ref[...] = jnp.zeros(sum_ref.shape, F32)
    lax.fori_loop(0, groups(table_ref), blocks, 0)


def pick(field, c, side, pick_ref):
    for dj in range(4):
        shifted = pltpu.roll(field, COLS - dj, 1) if dj else field
        both = jnp.concatenate(two_parts(shifted), axis=1)
        at = (dj * 2 + c) * ROWS
        for a in range(GX):
            pick_ref[2 * a + side, at : at + ROWS, :] = both[a * ROWS : (a + 1) * ROWS]


def first_inner_kernel(mid_ref, base_ref, moved_ref):
    w = [mid_ref[c] for c in range(2)]
    out = transported(w, [base_ref[c] for c in range(2)])
    for c in range(2):
        moved_ref[c] = out[c]


def inner_kernel(place_ref, mid_ref, base_far_ref, base_ref, base_near_ref, moved_ref):
    place = place_ref[0]
    extra = RIM - THIN
    length = COLS + 2 * RIM
    w = [
        jnp.concatenate([x[extra : length - extra], x[length + extra : 2 * length - extra]], axis=0)
        for x in wide_projected(place, mid_ref)
    ]
    base = [
        widened(base_ref, c, *thin_rims(place, base_far_ref, base_near_ref, 2 + c))
        for c in range(2)
    ]
    out = transported(w, base)
    for c in range(2):
        for side in range(2):
            at = side * (COLS + 2 * THIN) + THIN
            moved_ref[c, side * COLS : (side + 1) * COLS, :] = out[c][at : at + COLS]


def outer_kernel(
    first, place_ref, table_ref, far_ref, mid_ref, near_ref, base_far_ref, base_ref,
    base_near_ref, ints_ref, weight_ref, inner_ref, moved_ref, own_ref, part_far, part_near,
    next_far, next_near, pick_ref, sum_ref, *got_refs,
):
    place = place_ref[0]
    blank = jnp.zeros((RIM - THIN, NROW), F32)

    def thin_strips(far, mid, near, c, at):
        lows, highs = thin_rims(place, far, near, at + c)
        return strips(
            [jnp.concatenate([blank, x], axis=0) for x in lows],
            [jnp.concatenate([x, blank], axis=0) for x in highs],
            mid,
            c,
        )

    base = [thin_strips(base_far_ref, base_ref, base_near_ref, c, 2) for c in range(2)]
    if first:
        w = [thin_strips(far_ref, mid_ref, near_ref, c, 0) for c in range(2)]
    else:
        w = projected(rim_strips(place, far_ref, near_ref), masked(place))
    out = transported(w, base)
    spot = lax.broadcasted_iota(I32, (RIM, NROW), 0)
    for c in range(2):
        for side in range(2):
            low, high = outer_columns(out[c], side)
            at = side * COLS
            old_low = inner_ref[c, at : at + RIM, :]
            old_high = inner_ref[c, at + COLS - RIM : at + COLS, :]
            if first:
                low = jnp.where(spot == 0, low, old_low)
                high = jnp.where(spot == RIM - 1, high, old_high)
            else:
                low = old_low + low
                high = old_high + high
            moved = jnp.concatenate(
                [low, inner_ref[c, at + RIM : at + COLS - RIM, :], high], axis=0
            )
            moved_ref[c, at : at + COLS, :] = moved
            pick(moved.T, c, side, pick_ref)
    interpolate(table_ref, ints_ref, weight_ref, pick_ref, got_refs, sum_ref)
    sums = sum_ref[...].T
    sums = sums[:KEPT] + sums[KEPT:]
    for c in range(2):
        for side in range(2):
            at = (2 * c + side) * 48
            one = sums[at : at + 48]
            own_ref[c, side] = one
            part_far[side, c], part_near[side, c] = turned_round(place, one[:32], one[16:])
            next_far[side, c], next_near[side, c] = turned_round(place >> 1, one[:16], one[32:])


def tables_kernel(table_ref, ints_ref, weight_ref, out_ref):
    def block(n, carry):
        ids, _ = group_of(table_ref, n)
        for block in ids:
            tables = row_weights(ints_ref[block, 0:1, :], weight_ref[block])
            out_ref[block] = jnp.concatenate(
                two_parts(jnp.concatenate(tables, axis=0)), axis=1
            )
        return carry

    out_ref[EMPTY] = jnp.zeros((4 * ROWS, 2 * SPAN), BF16)
    lax.fori_loop(0, groups(table_ref), block, 0)


def force_of(sums, source):
    row = lax.broadcasted_iota(I32, sums.shape, 0) & 3
    lane = lax.broadcasted_iota(I32, sums.shape, 1)
    count = sums.shape[0]
    up = jnp.where(row == 0, pltpu.roll(sums, count - 3, 0), pltpu.roll(sums, 1, 0))
    down = jnp.where(row == 3, pltpu.roll(sums, 3, 0), pltpu.roll(sums, count - 1, 0))
    before = jnp.where(lane == 0, pltpu.roll(up, 1, 1), pltpu.roll(sums, 1, 1))
    after = jnp.where(lane == 127, pltpu.roll(down, 127, 1), pltpu.roll(sums, 127, 1))
    bent = before + after - 2.0 * sums
    return STIFFNESS * (sums + source - BENDING * bent)


def spread_kernel(
    place_ref, table_ref, sums_ref, from_far, from_near, beyond_far, beyond_near, thin_far,
    source_ref, thin_near, moved_ref, ints_ref, row_ref, out_ref, edge_far, edge_near, own_ref,
    force_ref, acc_ref,
):
    place = place_ref[0]

    def unfolded(ref, side, c):
        return jnp.concatenate([ref[side, 4 + c, :, :COLS], ref[side, 4 + c, :, COLS:]], axis=0)

    for c in range(2):
        pairs = [turned_round(place, from_far[s, c], from_near[s, c]) for s in range(2)]
        lows, highs = meeting(place, *zip(*pairs))
        pairs = [turned_round(place >> 1, beyond_far[s, c], beyond_near[s, c]) for s in range(2)]
        lows2, highs2 = meeting(place, *zip(*pairs), reach=2)
        pairs = [
            turned_round(place, unfolded(thin_far, s, c), unfolded(thin_near, s, c))
            for s in range(2)
        ]
        source_lows, source_highs = meeting(place, *zip(*pairs))
        for side in range(2):
            sums = sums_ref[c, side] + jnp.concatenate(
                [
                    lows[side][:16] + lows2[side],
                    lows[side][16:] + highs[side][:16],
                    highs[side][16:] + highs2[side],
                ],
                axis=0,
            )
            source = jnp.concatenate(
                [source_lows[side], source_ref[c, side], source_highs[side]], axis=0
            )
            force = force_of(sums, source)
            own_ref[c, side] = force[16:32]
            at = (2 * c + side) * 48
            force_ref[at : at + 48, :] = jnp.concatenate(two_parts(force), axis=1)
    acc_ref[...] = jnp.zeros(acc_ref.shape, F32)

    def blocks(n, carry):
        ids, tiles = group_of(table_ref, n)
        spots = one_hot(joined(ints_ref, ids, 3), COLS)
        picked = lax.dot_general(
            force_ref[...], jnp.concatenate([spots, spots], axis=0), NN,
            preferred_element_type=F32,
        )
        high = lax.broadcasted_iota(I32, (96, GROUP * SPAN), 0) == joined(ints_ref, ids, 2)
        parts = []
        for c in range(2):
            force = TIME_STEP * jnp.sum(
                jnp.where(high, picked[96 * c : 96 * c + 96], 0.0), axis=0, keepdims=True
            )
            parts.append([x.astype(F32) for x in two_parts(force)])
        sums = []
        for m, block in enumerate(ids):
            lanes = slice(m * SPAN, (m + 1) * SPAN)
            cols = lax.broadcasted_iota(I32, (COLS, SPAN), 0) == ints_ref[block, 1:2, :]
            hi, lo = (
                jnp.concatenate(
                    [jnp.where(cols, parts[c][k][:, lanes], 0.0).astype(BF16) for c in range(2)],
                    axis=0,
                )
                for k in range(2)
            )
            sums.append(
                lax.dot_general(
                    row_ref[block],
                    jnp.concatenate([hi, hi], axis=1),
                    NT,
                    preferred_element_type=F32,
                )
                + lax.dot_general(row_ref[block, :, :SPAN], lo, NT, preferred_element_type=F32)
            )
        for tile, one in zip(tiles, sums):
            acc_ref[tile] = acc_ref[tile] + one
        return carry

    lax.fori_loop(0, groups(table_ref), blocks, 0)
    for c in range(2):
        for side in range(2):
            rows = []
            for a in range(GX):
                total = jnp.zeros((ROWS, COLS), F32)
                for dj in range(4):
                    one = acc_ref[
                        2 * a + side, dj * ROWS : (dj + 1) * ROWS, c * COLS : (c + 1) * COLS
                    ]
                    total = total + (pltpu.roll(one, dj, 1) if dj else one)
                rows.append(total)
            cols = slice(side * COLS, (side + 1) * COLS)
            total = moved_ref[c, cols, :] + jnp.concatenate(rows, axis=0).T
            out_ref[c, cols, :] = total
            far, near = turned_round(place, total[:RIM], total[COLS - RIM :])
            edge_far[side, c] = far.astype(BF16)
            edge_near[side, c] = near.astype(BF16)


def finish_inner_kernel(place_ref, mid_ref, out_ref):
    w = wide_projected(place_ref[0], mid_ref)
    for c in range(2):
        for side in range(2):
            at = side * (COLS + 2 * RIM) + RIM
            block = w[c][at : at + COLS].T
            for a in range(GX):
                out_ref[2 * a + side, c] = block[a * ROWS : (a + 1) * ROWS]


def finish_outer_kernel(place_ref, far_ref, near_ref, inner_ref, out_ref):
    place = place_ref[0]
    w = projected(rim_strips(place, far_ref, near_ref), masked(place))
    blank = jnp.zeros((COLS - 2 * RIM, NROW), F32)
    for c in range(2):
        for side in range(2):
            low, high = outer_columns(w[c], side)
            both = jnp.concatenate([low, blank, high], axis=0).T
            for a in range(GX):
                out_ref[2 * a + side, c] = (
                    inner_ref[2 * a + side, c] + both[a * ROWS : (a + 1) * ROWS]
                )


def on_device(adjoint, base_flow, slot_cell, slot_marker, slot_count, slot_weight, marker_source):
    place = lax.axis_index("zc").astype(I32).reshape(1)
    half = lax.axis_index("xh")
    whole = ("gx", "xh")
    tiles = marker_source.reshape(2, 2, 16, COLS)
    kept = lax.dynamic_index_in_dim(tiles, half, axis=1, keepdims=False)
    other = swapped(lax.dynamic_index_in_dim(tiles, 1 - half, axis=1, keepdims=False))
    source = jnp.where(
        half == 0, jnp.stack([kept, other], axis=1), jnp.stack([other, kept], axis=1)
    )
    packed = call(
        pack_kernel,
        shape(2 * GX, PACK, COLS, dtype=BF16),
        (slot_count, adjoint, base_flow, slot_cell[0, 0], slot_marker[0, 0], slot_weight[0, 0]),
        scratch=(
            pltpu.SMEM((1, 1, 3, GX), I32),
            pltpu.VMEM(adjoint.shape, F32),
            pltpu.VMEM(base_flow.shape, BF16),
            pltpu.VMEM((3, GX, COLS), I32),
            pltpu.VMEM((3, GX, COLS), I32),
            pltpu.VMEM((3, GX, 16, COLS), F32),
            pltpu.SemaphoreType.DMA((6,)),
        ),
        spaces={n: HBM for n in range(6)},
        params=ROOMY,
    )
    got = lax.all_to_all(packed, whole, split_axis=0, concat_axis=0, tiled=True)
    field = shape(2, NCOL, NROW)
    thin = shape(2, 6, THIN, NROW)
    current, base, thin_far, thin_near = call(
        unpack_kernel, (field, field, thin, thin), (place, got, source), spaces={0: SMEM}
    )
    base_far, base_near = exchanged(thin_far, thin_near)
    ints, weights, table = call(
        slots_kernel,
        (
            shape(EMPTY + 1, 8, SPAN, dtype=I32),
            shape(EMPTY + 1, 16, SPAN),
            shape(128, dtype=I32),
        ),
        (got,),
        out_specs=(VMEM, VMEM, SMEM),
    )
    far, near = base_far, base_near
    part = shape(2, 2, 32, COLS)
    beyond = shape(2, 2, 16, COLS)
    rim = shape(2, 2, RIM, NROW, dtype=BF16)
    forces = source
    tables = None
    for substep in range(SUBSTEPS):
        if substep == 0:
            inner = call(first_inner_kernel, field, (current, base))
        else:
            inner = call(
                inner_kernel,
                field,
                (place, current, base_far, base, base_near),
                spaces={0: SMEM},
            )
        moved, sums, part_far, part_near, next_far, next_near = call(
            functools.partial(outer_kernel, substep == 0),
            (field, shape(2, 2, 48, COLS), part, part, beyond, beyond),
            (place, table, far, current, near, base_far, base, base_near, ints, weights, inner),
            scratch=OUTER_SCRATCH,
            spaces={0: SMEM, 1: SMEM},
        )
        beyond_far, beyond_near = exchanged(next_far, next_near, 2)
        from_far, from_near = exchanged(part_far, part_near)
        if substep == 0:
            tables = call(
                tables_kernel,
                shape(EMPTY + 1, 4 * ROWS, 2 * SPAN, dtype=BF16),
                (table, ints, weights),
                spaces={0: SMEM},
            )
        current, edge_far, edge_near, forces = call(
            spread_kernel,
            (field, rim, rim, shape(2, 2, 16, COLS)),
            (
                place, table, sums, from_far, from_near, beyond_far, beyond_near, base_far,
                source, base_near, moved, ints, tables,
            ),
            scratch=SPREAD_SCRATCH,
            spaces={0: SMEM, 1: SMEM},
        )
        far, near = exchanged(edge_far, edge_near)
    tiles_out = shape(2 * GX, 2, ROWS, COLS)
    inner = call(finish_inner_kernel, tiles_out, (place, current), spaces={0: SMEM})
    done = call(finish_outer_kernel, tiles_out, (place, far, near, inner), spaces={0: SMEM})
    back = lax.all_to_all(done, whole, split_axis=0, concat_axis=0, tiled=True)
    result = jnp.transpose(back, (1, 0, 2, 3))
    mine = lax.dynamic_index_in_dim(forces, half, axis=1, keepdims=False)
    theirs = swapped(lax.dynamic_index_in_dim(forces, 1 - half, axis=1, keepdims=False))
    planes = jnp.where(
        half == 0, jnp.stack([mine, theirs], axis=1), jnp.stack([theirs, mine], axis=1)
    )
    return (result, planes.reshape(marker_source.shape))


def solution(mesh):
    split = Mesh(mesh.devices.reshape(8, 2, 8), ("gx", "xh", "zc"))
    gy = ("xh", "zc")
    in_specs = (
        P(None, None, "gx", gy),
        P(None, None, "gx", gy),
        P("gx", gy, None, None, None),
        P("gx", gy, None, None, None),
        P("gx", gy, None, None),
        P("gx", gy, None, None, None, None),
        P(None, "gx", gy, None),
    )
    out_specs = (P(None, None, "gx", gy), P(None, "gx", gy, None))
    return jax.shard_map(
        on_device, mesh=split, in_specs=in_specs, out_specs=out_specs, check_vma=False
    )
```

```python
import functools

import jax
import jax.numpy as jnp
from jax import lax
from jax.experimental import pallas as pl
from jax.experimental.pallas import tpu as pltpu
from jax.sharding import Mesh, PartitionSpec as P

SUBSTEPS = 3
SWEEPS = 8

TIME_STEP = 0.5
VISCOSITY = 0.2
STIFFNESS = 2.0
BENDING = 0.25

F32 = jnp.float32
BF16 = jnp.bfloat16
I32 = jnp.int32

GX = 8
ROWS = 32
COLS = 128
NROW = GX * ROWS
NCOL = 2 * COLS
LAST = 7
RIM = 16
STRIP = 2 * RIM
THIN = 8
KEPT = 192
PACK = 304
SPAN = 128
TILES = 2 * GX
DEPTH = 3
EMPTY = TILES * DEPTH
COUNT_AT = 127
GROUP = 24
FEW = 8

NT = (((1,), (1,)), ((), ()))
NN = (((1,), (0,)), ((), ()))

PARAMS = pltpu.CompilerParams(vmem_limit_bytes=24 * 1024 * 1024)
ROOMY = pltpu.CompilerParams(vmem_limit_bytes=60 * 1024 * 1024)
VMEM = pl.BlockSpec(memory_space=pltpu.VMEM)
SMEM = pl.BlockSpec(memory_space=pltpu.SMEM)
HBM = pl.BlockSpec(memory_space=pltpu.HBM)


def call(body, outs, ins, scratch=(), spaces=(), out_specs=None, params=PARAMS):
    spaces = dict(spaces)
    return pl.pallas_call(
        body,
        out_shape=outs,
        in_specs=[spaces.get(n, VMEM) for n in range(len(ins))],
        out_specs=out_specs or jax.tree.map(lambda _: VMEM, outs),
        scratch_shapes=list(scratch),
        compiler_params=params,
    )(*ins)


OUTER_SCRATCH = (
    pltpu.VMEM((TILES, 8 * ROWS, 2 * COLS), BF16),
    pltpu.VMEM((COLS, 2 * KEPT), F32),
) + tuple(pltpu.VMEM((8 * ROWS, SPAN), F32) for _ in range(GROUP))
SPREAD_SCRATCH = (
    pltpu.VMEM((KEPT, 2 * COLS), BF16),
    pltpu.VMEM((TILES, 8 * ROWS, COLS), F32),
)


def shape(*dims, dtype=F32):
    return jax.ShapeDtypeStruct(dims, dtype)


def exchanged(far, near, step=1):
    count = lax.axis_size("zc")
    ups = [(n, (n + step) % count) for n in range(count)]
    results = []
    for value, parity in ((far, 1), (near, 0)):
        pairs = [pair for pair in ups if (pair[0] // step) % 2 == parity]
        pairs = pairs + [(target, source) for source, target in pairs]
        results.append(lax.ppermute(value, "zc", pairs))
    return results


def swapped(value):
    return lax.ppermute(value, "xh", [(0, 1), (1, 0)])


def two_parts(value):
    high = value.astype(BF16)
    return high, (value - high.astype(F32)).astype(BF16)


def row_next(x):
    lane = lax.broadcasted_iota(I32, x.shape, 1)
    return jnp.where(lane == NROW - 1, 0.0, pltpu.roll(x, NROW - 1, 1))


def row_prev(x):
    lane = lax.broadcasted_iota(I32, x.shape, 1)
    return jnp.where(lane == 0, 0.0, pltpu.roll(x, 1, 1))


def col_next(x):
    return pltpu.roll(x, x.shape[0] - 1, 0)


def col_prev(x):
    return pltpu.roll(x, 1, 0)


def pack_kernel(
    count_hbm, adj_hbm, base_hbm, cell_hbm, mark_hbm, weight_hbm, out_ref,
    count_ref, adj_ref, base_ref, cell_ref, mark_ref, weight_ref, sems,
):
    copies = [
        pltpu.make_async_copy(src, dst, sems.at[n])
        for n, (src, dst) in enumerate(
            (
                (cell_hbm, cell_ref),
                (mark_hbm, mark_ref),
                (weight_hbm, weight_ref),
                (base_hbm, base_ref),
                (adj_hbm, adj_ref),
                (count_hbm, count_ref),
            )
        )
    ]
    for copy in copies:
        copy.start()
    copies[5].wait()
    copies[0].wait()
    copies[1].wait()
    lane = lax.broadcasted_iota(I32, (1, COLS), 1)
    none = jnp.zeros((4, COLS), F32)
    for e in range(GX):
        for q in range(2):
            rows = []
            for g in range(3):
                cell = cell_ref[g, e : e + 1, :]
                mark = mark_ref[g, e : e + 1, :]
                live = (lane < count_ref[0, 0, g, e]) & ((mark >> 11) == q)
                rows += [cell >> 7, cell & 127, jnp.where(live, (mark >> 7) & 15, -1), mark & 127]
            ints = jnp.concatenate([r.astype(F32) for r in rows] + [none], axis=0)
            out_ref[2 * e + q, 288:304, :] = ints.astype(BF16)
    copies[2].wait()
    for e in range(GX):
        for g in range(3):
            hi, lo = two_parts(weight_ref[g, e])
            for q in range(2):
                out_ref[2 * e + q, 192 + 16 * g : 208 + 16 * g, :] = hi
                out_ref[2 * e + q, 240 + 16 * g : 256 + 16 * g, :] = lo
    copies[3].wait()
    for p in range(2 * GX):
        for c in range(2):
            out_ref[p, 128 + c * ROWS : 128 + (c + 1) * ROWS, :] = base_ref[c, p]
    copies[4].wait()
    for p in range(2 * GX):
        for c in range(2):
            hi, lo = two_parts(adj_ref[c, p])
            out_ref[p, c * ROWS : (c + 1) * ROWS, :] = hi
            out_ref[p, 64 + c * ROWS : 64 + (c + 1) * ROWS, :] = lo


def closed_up(blocks):
    lane = lax.broadcasted_iota(I32, (1, 1, SPAN), 2)
    spot = lax.broadcasted_iota(I32, (1, 24, SPAN), 1)
    blank = jnp.where(spot == 20, -1.0, 0.0)
    for bit in range(9):
        step = 1 << bit
        goes = []
        stays = []
        for x in blocks:
            away = x[:, 20:21, :].astype(I32)
            flag = (away >> bit) & 1
            goes.append(jnp.where((away >= 0) & (flag == 1), 1.0, 0.0))
            stays.append((away >= 0) & (flag == 0))

        def ahead(values, n):
            if step >= SPAN:
                m = n + step // SPAN
                return values[m] if m < len(values) else None
            here = pltpu.roll(values[n], SPAN - step, 2)
            if n + 1 < len(values):
                there = pltpu.roll(values[n + 1], SPAN - step, 2)
            else:
                there = jnp.zeros_like(here)
            return jnp.where(lane < SPAN - step, here, there)

        result = []
        for n, x in enumerate(blocks):
            kept = jnp.where(stays[n], x, blank)
            coming = ahead(goes, n)
            if coming is None:
                result.append(kept)
            else:
                result.append(jnp.where(coming > 0.5, ahead(blocks, n), kept))
        blocks = result
    return blocks


def unpack_kernel(place_ref, got_ref, source_ref, adj_ref, base_ref, far_ref, near_ref):
    place = place_ref[0]
    for n in range(4):
        for side in range(2):
            parts = []
            for a in range(GX):
                d = 2 * a + side
                at = (n % 2) * ROWS
                if n < 2:
                    part = got_ref[d, at : at + ROWS, :].astype(F32)
                    part = part + got_ref[d, 64 + at : 64 + at + ROWS, :].astype(F32)
                else:
                    part = got_ref[d, 128 + at : 128 + at + ROWS, :].astype(F32)
                parts.append(part)
            turned = jnp.concatenate(parts, axis=0).T
            ref = adj_ref if n < 2 else base_ref
            ref[n % 2, side * COLS : (side + 1) * COLS, :] = turned
            far_ref[side, n], near_ref[side, n] = turned_round(
                place, turned[:THIN], turned[COLS - THIN :]
            )
    for c in range(2):
        for side in range(2):
            both = jnp.concatenate(
                [source_ref[c, side, 0:8, :], source_ref[c, side, 8:16, :]], axis=1
            )
            far_ref[side, 4 + c] = both
            near_ref[side, 4 + c] = both


def slots_kernel(got_ref, ints_ref, weight_ref, table_ref):
    ints = got_ref[:, 288:304, :].astype(F32)
    across = lax.broadcasted_iota(I32, (SPAN, SPAN), 0) <= lax.broadcasted_iota(
        I32, (SPAN, SPAN), 1
    )
    across = jnp.where(across, 1.0, 0.0).astype(BF16)
    live = []
    ranks = []
    total = jnp.zeros((TILES, SPAN), F32)
    for g in range(3):
        alive = jnp.where(ints[:, 4 * g + 2, :] >= 0.0, 1.0, 0.0)
        bits = alive.astype(BF16)
        live.append(alive)
        ranks.append(
            total + lax.dot_general(bits, across, NN, preferred_element_type=F32)
        )
        total = total + lax.dot_general(
            bits, jnp.ones((SPAN, SPAN), BF16), NN, preferred_element_type=F32
        )
    filled = jnp.int32(0)
    here = [
        (jnp.max(total[d : d + 1]).astype(I32) + SPAN - 1) // SPAN for d in range(TILES)
    ]
    for d in range(TILES):
        for n in range(DEPTH):

            @pl.when(n < here[d])
            def _():
                table_ref[filled + n] = d * DEPTH + n

        filled = filled + here[d]
    for n in range(GROUP):
        table_ref[filled + n] = EMPTY
    table_ref[COUNT_AT] = filled
    lane = lax.broadcasted_iota(I32, (TILES, SPAN), 1).astype(F32)
    spot = lax.broadcasted_iota(I32, (TILES, 8, SPAN), 1)
    side = (lax.broadcasted_iota(I32, (TILES, 1, SPAN), 0) & 1).astype(F32)
    blocks = []
    for g in range(3):
        away = jnp.where(live[g] > 0.5, lane + float(g * SPAN + 1) - ranks[g], -1.0)
        weights = got_ref[:, 192 + 16 * g : 208 + 16 * g, :].astype(F32)
        weights = weights + got_ref[:, 240 + 16 * g : 256 + 16 * g, :].astype(F32)
        rows = [ints[:, 4 * g + n : 4 * g + n + 1, :] for n in range(4)]
        rows[2] = rows[2] + 48.0 * side + float(16 * g)
        rest = jnp.zeros((TILES, 8, SPAN), F32)
        for n, row in enumerate(rows + [away[:, None, :]]):
            rest = jnp.where(spot == n, row, rest)
        blocks.append(jnp.concatenate([weights, rest], axis=1))
    for n, block in enumerate(closed_up(blocks)):
        for d in range(TILES):
            weight_ref[d * DEPTH + n] = block[d, :16]
            ints_ref[d * DEPTH + n] = block[d, 16:].astype(I32)
    weight_ref[EMPTY] = jnp.zeros((16, SPAN), F32)
    ints_ref[EMPTY] = jnp.zeros((8, SPAN), I32)


def one_hot(index, count):
    spot = lax.broadcasted_iota(I32, (count, index.shape[1]), 0)
    return jnp.where(spot == index, 1.0, 0.0).astype(BF16)


def row_weights(first_row, weights):
    off = lax.broadcasted_iota(I32, (ROWS, SPAN), 0) - first_row
    hits = [off == n for n in range(4)]
    tables = []
    for dj in range(4):
        table = jnp.zeros((ROWS, SPAN), F32)
        for di in (3, 2, 1, 0):
            row = weights[4 * di + dj : 4 * di + dj + 1]
            table = jnp.where(hits[di], row, table)
        tables.append(table)
    return tables


def over_blocks(table_ref, body):
    def step(size, start):
        def run(n, carry):
            ids = [table_ref[start + size * n + m] for m in range(size)]
            body(ids, [jnp.minimum(block // DEPTH, TILES - 1) for block in ids])
            return carry

        return run

    steps = (table_ref[COUNT_AT] + FEW - 1) // FEW
    full = steps // (GROUP // FEW)
    lax.fori_loop(0, full, step(GROUP, 0), 0)
    lax.fori_loop(0, steps - full * (GROUP // FEW), step(FEW, full * GROUP), 0)


def joined(ref, ids, row):
    return jnp.concatenate([ref[block, row : row + 1, :] for block in ids], axis=1)


def turned_round(place, one, other):
    odd = (place & 1) == 1
    return jnp.where(odd, other, one), jnp.where(odd, one, other)


def neighbours(place):
    return jnp.where(place == 0, 0.0, 1.0), jnp.where(place == LAST, 0.0, 1.0)


def meeting(place, low, high, reach=1):
    start = place < reach
    end = place > LAST - reach
    has_low = jnp.where(start, 0.0, 1.0)
    has_high = jnp.where(end, 0.0, 1.0)
    lows = (low[0] * has_low, jnp.where(start, low[0], low[1]))
    highs = (jnp.where(end, high[1], high[0]), high[1] * has_high)
    return lows, highs


def masked(place):
    has_low, has_high = neighbours(place)

    def inside(x):
        width = x.shape[0]
        return jnp.concatenate(
            [x[:RIM] * has_low, x[RIM : width - RIM], x[width - RIM :] * has_high], axis=0
        )

    return inside


def projected(wide, inside=lambda x: x):
    div = 0.5 * (row_next(wide[0]) - row_prev(wide[0])) + 0.5 * (
        col_next(wide[1]) - col_prev(wide[1])
    )
    pressure = inside(-0.25 * div)
    for sweep in range(SWEEPS - 1):
        pressure = inside(
            0.25
            * (
                row_next(pressure)
                + row_prev(pressure)
                + col_next(pressure)
                + col_prev(pressure)
                - div
            )
        )
    first = wide[0] - 0.5 * (row_next(pressure) - row_prev(pressure))
    second = wide[1] - 0.5 * (col_next(pressure) - col_prev(pressure))
    return inside(first), inside(second)


def strips(lows, highs, mid_ref, c):
    parts = []
    for side in range(2):
        at = side * COLS
        if mid_ref is None:
            inner = [jnp.zeros((RIM, NROW), F32)] * 2
        else:
            inner = [
                mid_ref[c, at : at + RIM, :],
                mid_ref[c, at + COLS - RIM : at + COLS, :],
            ]
        parts += [lows[side], inner[0], inner[1], highs[side]]
    return jnp.concatenate(parts, axis=0)


def rim_strips(place, far_ref, near_ref):
    result = []
    for c in range(2):
        pairs = [
            turned_round(place, far_ref[side, c].astype(F32), near_ref[side, c].astype(F32))
            for side in range(2)
        ]
        result.append(strips(*meeting(place, *zip(*pairs)), None, c))
    return result


def thin_rims(place, far, near, at):
    pairs = [turned_round(place, far[side, at], near[side, at]) for side in range(2)]
    return meeting(place, *zip(*pairs))


def outer_columns(x, side):
    at = side * 2 * STRIP
    return x[at + RIM : at + 2 * RIM], x[at + STRIP : at + STRIP + RIM]


def widened(mid_ref, c, lows, highs):
    parts = []
    for side in range(2):
        parts += [lows[side], mid_ref[c, side * COLS : (side + 1) * COLS, :], highs[side]]
    return jnp.concatenate(parts, axis=0)


def wide_projected(place, mid_ref):
    blank = (jnp.zeros((RIM, NROW), F32),) * 2
    return projected([widened(mid_ref, c, blank, blank) for c in range(2)], masked(place))


def transported(w, base):
    ux = 0.5 * (row_next(base[0]) - row_prev(base[0]))
    vx = 0.5 * (row_next(base[1]) - row_prev(base[1]))
    uy = 0.5 * (col_next(base[0]) - col_prev(base[0]))
    vy = 0.5 * (col_next(base[1]) - col_prev(base[1]))
    mixed = (ux * w[0] + vx * w[1], uy * w[0] + vy * w[1])
    out = []
    for c in range(2):
        east, west = row_next(w[c]), row_prev(w[c])
        north, south = col_next(w[c]), col_prev(w[c])
        laplace = east + west + north + south - 4.0 * w[c]
        value = w[c] + TIME_STEP * (
            base[0] * (0.5 * (east - west))
            + base[1] * (0.5 * (north - south))
            - mixed[c]
            + VISCOSITY * laplace
        )
        out.append(value)
    return out


def interpolate(table_ref, ints_ref, weight_ref, pick_ref, got_refs, sum_ref):
    def blocks(ids, tiles):
        for block, tile, got_ref in zip(ids, tiles, got_refs):
            cols = one_hot(ints_ref[block, 1:2, :], COLS)
            got_ref[...] = lax.dot_general(
                pick_ref[tile],
                jnp.concatenate([cols, cols], axis=0),
                NN,
                preferred_element_type=F32,
            )
        values = []
        for block, got_ref in zip(ids, got_refs):
            tables = row_weights(ints_ref[block, 0:1, :], weight_ref[block])
            both = []
            for c in range(2):
                total = jnp.zeros((ROWS, SPAN), F32)
                for dj in range(4):
                    at = (dj * 2 + c) * ROWS
                    total = total + tables[dj] * got_ref[at : at + ROWS, :]
                both.append(jnp.sum(total, axis=0, keepdims=True))
            values.append(both)
        high = lax.broadcasted_iota(I32, (96, len(ids) * SPAN), 0) == joined(ints_ref, ids, 2)
        parts = [two_parts(jnp.concatenate([v[c] for v in values], axis=1)) for c in range(2)]
        stacked = jnp.concatenate(
            [
                jnp.where(high, parts[c][k].astype(F32), 0.0).astype(BF16)
                for k in range(2)
                for c in range(2)
            ],
            axis=0,
        )
        both = lax.dot_general(
            one_hot(joined(ints_ref, ids, 3), COLS), stacked, NT, preferred_element_type=F32
        )
        sum_ref[...] = sum_ref[...] + both

    sum_ref[...] = jnp.zeros(sum_ref.shape, F32)
    over_blocks(table_ref, blocks)


def pick(field, c, side, pick_ref):
    for dj in range(4):
        shifted = pltpu.roll(field, COLS - dj, 1) if dj else field
        both = jnp.concatenate(two_parts(shifted), axis=1)
        at = (dj * 2 + c) * ROWS
        for a in range(GX):
            pick_ref[2 * a + side, at : at + ROWS, :] = both[a * ROWS : (a + 1) * ROWS]


def first_inner_kernel(mid_ref, base_ref, moved_ref):
    w = [mid_ref[c] for c in range(2)]
    out = transported(w, [base_ref[c] for c in range(2)])
    for c in range(2):
        moved_ref[c] = out[c]


def inner_kernel(place_ref, mid_ref, base_far_ref, base_ref, base_near_ref, moved_ref):
    place = place_ref[0]
    extra = RIM - THIN
    length = COLS + 2 * RIM
    w = [
        jnp.concatenate([x[extra : length - extra], x[length + extra : 2 * length - extra]], axis=0)
        for x in wide_projected(place, mid_ref)
    ]
    base = [
        widened(base_ref, c, *thin_rims(place, base_far_ref, base_near_ref, 2 + c))
        for c in range(2)
    ]
    out = transported(w, base)
    for c in range(2):
        for side in range(2):
            at = side * (COLS + 2 * THIN) + THIN
            moved_ref[c, side * COLS : (side + 1) * COLS, :] = out[c][at : at + COLS]


def outer_kernel(
    first, place_ref, table_ref, far_ref, mid_ref, near_ref, base_far_ref, base_ref,
    base_near_ref, ints_ref, weight_ref, inner_ref, moved_ref, own_ref, part_far, part_near,
    next_far, next_near, pick_ref, sum_ref, *got_refs,
):
    place = place_ref[0]
    blank = jnp.zeros((RIM - THIN, NROW), F32)

    def thin_strips(far, mid, near, c, at):
        lows, highs = thin_rims(place, far, near, at + c)
        return strips(
            [jnp.concatenate([blank, x], axis=0) for x in lows],
            [jnp.concatenate([x, blank], axis=0) for x in highs],
            mid,
            c,
        )

    base = [thin_strips(base_far_ref, base_ref, base_near_ref, c, 2) for c in range(2)]
    if first:
        w = [thin_strips(far_ref, mid_ref, near_ref, c, 0) for c in range(2)]
    else:
        w = projected(rim_strips(place, far_ref, near_ref), masked(place))
    out = transported(w, base)
    spot = lax.broadcasted_iota(I32, (RIM, NROW), 0)
    for c in range(2):
        for side in range(2):
            low, high = outer_columns(out[c], side)
            at = side * COLS
            old_low = inner_ref[c, at : at + RIM, :]
            old_high = inner_ref[c, at + COLS - RIM : at + COLS, :]
            if first:
                low = jnp.where(spot == 0, low, old_low)
                high = jnp.where(spot == RIM - 1, high, old_high)
            else:
                low = old_low + low
                high = old_high + high
            moved = jnp.concatenate(
                [low, inner_ref[c, at + RIM : at + COLS - RIM, :], high], axis=0
            )
            moved_ref[c, at : at + COLS, :] = moved
            pick(moved.T, c, side, pick_ref)
    interpolate(table_ref, ints_ref, weight_ref, pick_ref, got_refs, sum_ref)
    sums = sum_ref[...].T
    sums = sums[:KEPT] + sums[KEPT:]
    for c in range(2):
        for side in range(2):
            at = (2 * c + side) * 48
            one = sums[at : at + 48]
            own_ref[c, side] = one
            part_far[side, c], part_near[side, c] = turned_round(place, one[:32], one[16:])
            next_far[side, c], next_near[side, c] = turned_round(place >> 1, one[:16], one[32:])


def tables_kernel(table_ref, ints_ref, weight_ref, rows_ref, cols_ref):
    def blocks(ids, tiles):
        for block in ids:
            rows_ref[block] = jnp.concatenate(
                row_weights(ints_ref[block, 0:1, :], weight_ref[block]), axis=0
            )
            spot = lax.broadcasted_iota(I32, (COLS, SPAN), 0)
            hits = jnp.where(spot == ints_ref[block, 1:2, :], 1.0, 0.0).T.astype(BF16)
            cols_ref[block] = jnp.concatenate([hits, hits], axis=0)

    rows_ref[EMPTY] = jnp.zeros((4 * ROWS, SPAN), F32)
    cols_ref[EMPTY] = jnp.zeros((2 * SPAN, COLS), BF16)
    over_blocks(table_ref, blocks)


def force_of(sums, source):
    row = lax.broadcasted_iota(I32, sums.shape, 0) & 3
    lane = lax.broadcasted_iota(I32, sums.shape, 1)
    count = sums.shape[0]
    up = jnp.where(row == 0, pltpu.roll(sums, count - 3, 0), pltpu.roll(sums, 1, 0))
    down = jnp.where(row == 3, pltpu.roll(sums, 3, 0), pltpu.roll(sums, count - 1, 0))
    before = jnp.where(lane == 0, pltpu.roll(up, 1, 1), pltpu.roll(sums, 1, 1))
    after = jnp.where(lane == 127, pltpu.roll(down, 127, 1), pltpu.roll(sums, 127, 1))
    bent = before + after - 2.0 * sums
    return STIFFNESS * (sums + source - BENDING * bent)


def spread_kernel(
    place_ref, table_ref, sums_ref, beyond_far, beyond_near, from_far, from_near, thin_far,
    source_ref, thin_near, moved_ref, ints_ref, row_ref, col_ref, out_ref, edge_far, edge_near, own_ref,
    force_ref, acc_ref,
):
    place = place_ref[0]

    def unfolded(ref, side, c):
        return jnp.concatenate([ref[side, 4 + c, :, :COLS], ref[side, 4 + c, :, COLS:]], axis=0)

    for c in range(2):
        pairs = [turned_round(place, from_far[s, c], from_near[s, c]) for s in range(2)]
        lows, highs = meeting(place, *zip(*pairs))
        pairs = [turned_round(place >> 1, beyond_far[s, c], beyond_near[s, c]) for s in range(2)]
        lows2, highs2 = meeting(place, *zip(*pairs), reach=2)
        pairs = [
            turned_round(place, unfolded(thin_far, s, c), unfolded(thin_near, s, c))
            for s in range(2)
        ]
        source_lows, source_highs = meeting(place, *zip(*pairs))
        for side in range(2):
            sums = sums_ref[c, side] + jnp.concatenate(
                [
                    lows[side][:16] + lows2[side],
                    lows[side][16:] + highs[side][:16],
                    highs[side][16:] + highs2[side],
                ],
                axis=0,
            )
            source = jnp.concatenate(
                [source_lows[side], source_ref[c, side], source_highs[side]], axis=0
            )
            force = force_of(sums, source)
            own_ref[c, side] = force[16:32]
            at = (2 * c + side) * 48
            force_ref[at : at + 48, :] = jnp.concatenate(two_parts(force), axis=1)
    acc_ref[...] = jnp.zeros(acc_ref.shape, F32)

    def blocks(ids, tiles):
        spots = one_hot(joined(ints_ref, ids, 3), COLS)
        picked = lax.dot_general(
            force_ref[...], jnp.concatenate([spots, spots], axis=0), NN,
            preferred_element_type=F32,
        )
        high = lax.broadcasted_iota(I32, (96, len(ids) * SPAN), 0) == joined(ints_ref, ids, 2)
        forces = [
            TIME_STEP
            * jnp.sum(jnp.where(high, picked[96 * c : 96 * c + 96], 0.0), axis=0, keepdims=True)
            for c in range(2)
        ]
        sums = []
        for m, block in enumerate(ids):
            lanes = slice(m * SPAN, (m + 1) * SPAN)
            weighted = jnp.concatenate(
                [row_ref[block] * forces[c][:, lanes] for c in range(2)], axis=0
            )
            sums.append(
                lax.dot_general(
                    jnp.concatenate(two_parts(weighted), axis=1),
                    col_ref[block],
                    NN,
                    preferred_element_type=F32,
                )
            )
        for tile, one in zip(tiles, sums):
            acc_ref[tile] = acc_ref[tile] + one

    over_blocks(table_ref, blocks)
    for c in range(2):
        for side in range(2):
            rows = []
            for a in range(GX):
                total = jnp.zeros((ROWS, COLS), F32)
                for dj in range(4):
                    at = (4 * c + dj) * ROWS
                    one = acc_ref[2 * a + side, at : at + ROWS, :]
                    total = total + (pltpu.roll(one, dj, 1) if dj else one)
                rows.append(total)
            cols = slice(side * COLS, (side + 1) * COLS)
            total = moved_ref[c, cols, :] + jnp.concatenate(rows, axis=0).T
            out_ref[c, cols, :] = total
            far, near = turned_round(place, total[:RIM], total[COLS - RIM :])
            edge_far[side, c] = far.astype(BF16)
            edge_near[side, c] = near.astype(BF16)


def finish_inner_kernel(place_ref, mid_ref, out_ref):
    w = wide_projected(place_ref[0], mid_ref)
    for c in range(2):
        for side in range(2):
            at = side * (COLS + 2 * RIM) + RIM
            block = w[c][at : at + COLS].T
            for a in range(GX):
                out_ref[2 * a + side, c] = block[a * ROWS : (a + 1) * ROWS]


def finish_outer_kernel(place_ref, far_ref, near_ref, inner_ref, out_ref):
    place = place_ref[0]
    w = projected(rim_strips(place, far_ref, near_ref), masked(place))
    blank = jnp.zeros((COLS - 2 * RIM, NROW), F32)
    for c in range(2):
        for side in range(2):
            low, high = outer_columns(w[c], side)
            both = jnp.concatenate([low, blank, high], axis=0).T
            for a in range(GX):
                out_ref[2 * a + side, c] = (
                    inner_ref[2 * a + side, c] + both[a * ROWS : (a + 1) * ROWS]
                )


def on_device(adjoint, base_flow, slot_cell, slot_marker, slot_count, slot_weight, marker_source):
    place = lax.axis_index("zc").astype(I32).reshape(1)
    half = lax.axis_index("xh")
    whole = ("gx", "xh")
    tiles = marker_source.reshape(2, 2, 16, COLS)
    kept = lax.dynamic_index_in_dim(tiles, half, axis=1, keepdims=False)
    other = swapped(lax.dynamic_index_in_dim(tiles, 1 - half, axis=1, keepdims=False))
    source = jnp.where(
        half == 0, jnp.stack([kept, other], axis=1), jnp.stack([other, kept], axis=1)
    )
    packed = call(
        pack_kernel,
        shape(2 * GX, PACK, COLS, dtype=BF16),
        (slot_count, adjoint, base_flow, slot_cell[0, 0], slot_marker[0, 0], slot_weight[0, 0]),
        scratch=(
            pltpu.SMEM((1, 1, 3, GX), I32),
            pltpu.VMEM(adjoint.shape, F32),
            pltpu.VMEM(base_flow.shape, BF16),
            pltpu.VMEM((3, GX, COLS), I32),
            pltpu.VMEM((3, GX, COLS), I32),
            pltpu.VMEM((3, GX, 16, COLS), F32),
            pltpu.SemaphoreType.DMA((6,)),
        ),
        spaces={n: HBM for n in range(6)},
        params=ROOMY,
    )
    got = lax.all_to_all(packed, whole, split_axis=0, concat_axis=0, tiled=True)
    field = shape(2, NCOL, NROW)
    thin = shape(2, 6, THIN, NROW)
    current, base, thin_far, thin_near = call(
        unpack_kernel, (field, field, thin, thin), (place, got, source), spaces={0: SMEM}
    )
    base_far, base_near = exchanged(thin_far, thin_near)
    ints, weights, table = call(
        slots_kernel,
        (
            shape(EMPTY + 1, 8, SPAN, dtype=I32),
            shape(EMPTY + 1, 16, SPAN),
            shape(128, dtype=I32),
        ),
        (got,),
        out_specs=(VMEM, VMEM, SMEM),
    )
    far, near = base_far, base_near
    part = shape(2, 2, 32, COLS)
    beyond = shape(2, 2, 16, COLS)
    rim = shape(2, 2, RIM, NROW, dtype=BF16)
    forces = source
    row_tables = col_tables = None
    for substep in range(SUBSTEPS):
        if substep == 0:
            inner = call(first_inner_kernel, field, (current, base))
        else:
            inner = call(
                inner_kernel,
                field,
                (place, current, base_far, base, base_near),
                spaces={0: SMEM},
            )
        moved, sums, part_far, part_near, next_far, next_near = call(
            functools.partial(outer_kernel, substep == 0),
            (field, shape(2, 2, 48, COLS), part, part, beyond, beyond),
            (place, table, far, current, near, base_far, base, base_near, ints, weights, inner),
            scratch=OUTER_SCRATCH,
            spaces={0: SMEM, 1: SMEM},
        )
        beyond_far, beyond_near = exchanged(next_far, next_near, 2)
        from_far, from_near = exchanged(part_far, part_near)
        if substep == 0:
            row_tables, col_tables = call(
                tables_kernel,
                (
                    shape(EMPTY + 1, 4 * ROWS, SPAN),
                    shape(EMPTY + 1, 2 * SPAN, COLS, dtype=BF16),
                ),
                (table, ints, weights),
                spaces={0: SMEM},
            )
        current, edge_far, edge_near, forces = call(
            spread_kernel,
            (field, rim, rim, shape(2, 2, 16, COLS)),
            (
                place, table, sums, beyond_far, beyond_near, from_far, from_near, base_far,
                source, base_near, moved, ints, row_tables, col_tables,
            ),
            scratch=SPREAD_SCRATCH,
            spaces={0: SMEM, 1: SMEM},
        )
        far, near = exchanged(edge_far, edge_near)
    tiles_out = shape(2 * GX, 2, ROWS, COLS)
    inner = call(finish_inner_kernel, tiles_out, (place, current), spaces={0: SMEM})
    done = call(finish_outer_kernel, tiles_out, (place, far, near, inner), spaces={0: SMEM})
    back = lax.all_to_all(done, whole, split_axis=0, concat_axis=0, tiled=True)
    result = jnp.transpose(back, (1, 0, 2, 3))
    mine = lax.dynamic_index_in_dim(forces, half, axis=1, keepdims=False)
    theirs = swapped(lax.dynamic_index_in_dim(forces, 1 - half, axis=1, keepdims=False))
    planes = jnp.where(
        half == 0, jnp.stack([mine, theirs], axis=1), jnp.stack([theirs, mine], axis=1)
    )
    return (result, planes.reshape(marker_source.shape))


def solution(mesh):
    split = Mesh(mesh.devices.reshape(8, 2, 8), ("gx", "xh", "zc"))
    gy = ("xh", "zc")
    in_specs = (
        P(None, None, "gx", gy),
        P(None, None, "gx", gy),
        P("gx", gy, None, None, None),
        P("gx", gy, None, None, None),
        P("gx", gy, None, None),
        P("gx", gy, None, None, None, None),
        P(None, "gx", gy, None),
    )
    out_specs = (P(None, None, "gx", gy), P(None, "gx", gy, None))
    return jax.shard_map(
        on_device, mesh=split, in_specs=in_specs, out_specs=out_specs, check_vma=False
    )
```

```python
import functools

import jax
import jax.numpy as jnp
from jax import lax
from jax.experimental import pallas as pl
from jax.experimental.pallas import tpu as pltpu
from jax.sharding import Mesh, PartitionSpec as P

SUBSTEPS = 3
SWEEPS = 8

TIME_STEP = 0.5
VISCOSITY = 0.2
STIFFNESS = 2.0
BENDING = 0.25

F32 = jnp.float32
BF16 = jnp.bfloat16
I32 = jnp.int32

GX = 8
ROWS = 32
COLS = 128
NROW = GX * ROWS
NCOL = 2 * COLS
LAST = 7
RIM = 16
STRIP = 2 * RIM
THIN = 8
KEPT = 192
PACK = 304
SPAN = 128
TILES = 2 * GX
DEPTH = 3
EMPTY = TILES * DEPTH
COUNT_AT = 127
GROUP = 12

NT = (((1,), (1,)), ((), ()))
NN = (((1,), (0,)), ((), ()))

PARAMS = pltpu.CompilerParams(vmem_limit_bytes=24 * 1024 * 1024)
ROOMY = pltpu.CompilerParams(vmem_limit_bytes=60 * 1024 * 1024)
VMEM = pl.BlockSpec(memory_space=pltpu.VMEM)
SMEM = pl.BlockSpec(memory_space=pltpu.SMEM)
HBM = pl.BlockSpec(memory_space=pltpu.HBM)


def call(body, outs, ins, scratch=(), spaces=(), out_specs=None, params=PARAMS):
    spaces = dict(spaces)
    return pl.pallas_call(
        body,
        out_shape=outs,
        in_specs=[spaces.get(n, VMEM) for n in range(len(ins))],
        out_specs=out_specs or jax.tree.map(lambda _: VMEM, outs),
        scratch_shapes=list(scratch),
        compiler_params=params,
    )(*ins)


OUTER_SCRATCH = (
    pltpu.VMEM((TILES, 8 * ROWS, 2 * COLS), BF16),
    pltpu.VMEM((COLS, 2 * KEPT), F32),
) + tuple(pltpu.VMEM((8 * ROWS, SPAN), F32) for _ in range(GROUP))
SPREAD_SCRATCH = (
    pltpu.VMEM((KEPT, 2 * COLS), BF16),
    pltpu.VMEM((TILES, 8 * ROWS, COLS), F32),
)


def shape(*dims, dtype=F32):
    return jax.ShapeDtypeStruct(dims, dtype)


def exchanged(far, near, step=1):
    count = lax.axis_size("zc")
    ups = [(n, (n + step) % count) for n in range(count)]
    results = []
    for value, parity in ((far, 1), (near, 0)):
        pairs = [pair for pair in ups if (pair[0] // step) % 2 == parity]
        pairs = pairs + [(target, source) for source, target in pairs]
        results.append(lax.ppermute(value, "zc", pairs))
    return results


def swapped(value):
    return lax.ppermute(value, "xh", [(0, 1), (1, 0)])


def two_parts(value):
    high = value.astype(BF16)
    return high, (value - high.astype(F32)).astype(BF16)


def row_next(x):
    lane = lax.broadcasted_iota(I32, x.shape, 1)
    return jnp.where(lane == NROW - 1, 0.0, pltpu.roll(x, NROW - 1, 1))


def row_prev(x):
    lane = lax.broadcasted_iota(I32, x.shape, 1)
    return jnp.where(lane == 0, 0.0, pltpu.roll(x, 1, 1))


def col_next(x):
    return pltpu.roll(x, x.shape[0] - 1, 0)


def col_prev(x):
    return pltpu.roll(x, 1, 0)


def pack_kernel(
    count_hbm, adj_hbm, base_hbm, cell_hbm, mark_hbm, weight_hbm, out_ref,
    count_ref, adj_ref, base_ref, cell_ref, mark_ref, weight_ref, sems,
):
    copies = [
        pltpu.make_async_copy(src, dst, sems.at[n])
        for n, (src, dst) in enumerate(
            (
                (cell_hbm, cell_ref),
                (mark_hbm, mark_ref),
                (weight_hbm, weight_ref),
                (base_hbm, base_ref),
                (adj_hbm, adj_ref),
                (count_hbm, count_ref),
            )
        )
    ]
    for copy in copies:
        copy.start()
    copies[5].wait()
    copies[0].wait()
    copies[1].wait()
    lane = lax.broadcasted_iota(I32, (1, COLS), 1)
    none = jnp.zeros((4, COLS), F32)
    for e in range(GX):
        for q in range(2):
            rows = []
            for g in range(3):
                cell = cell_ref[g, e : e + 1, :]
                mark = mark_ref[g, e : e + 1, :]
                live = (lane < count_ref[0, 0, g, e]) & ((mark >> 11) == q)
                rows += [cell >> 7, cell & 127, jnp.where(live, (mark >> 7) & 15, -1), mark & 127]
            ints = jnp.concatenate([r.astype(F32) for r in rows] + [none], axis=0)
            out_ref[2 * e + q, 288:304, :] = ints.astype(BF16)
    copies[2].wait()
    for e in range(GX):
        for g in range(3):
            hi, lo = two_parts(weight_ref[g, e])
            for q in range(2):
                out_ref[2 * e + q, 192 + 16 * g : 208 + 16 * g, :] = hi
                out_ref[2 * e + q, 240 + 16 * g : 256 + 16 * g, :] = lo
    copies[3].wait()
    for p in range(2 * GX):
        for c in range(2):
            out_ref[p, 128 + c * ROWS : 128 + (c + 1) * ROWS, :] = base_ref[c, p]
    copies[4].wait()
    for p in range(2 * GX):
        for c in range(2):
            hi, lo = two_parts(adj_ref[c, p])
            out_ref[p, c * ROWS : (c + 1) * ROWS, :] = hi
            out_ref[p, 64 + c * ROWS : 64 + (c + 1) * ROWS, :] = lo


def closed_up(blocks):
    lane = lax.broadcasted_iota(I32, (1, 1, SPAN), 2)
    spot = lax.broadcasted_iota(I32, (1, 24, SPAN), 1)
    blank = jnp.where(spot == 20, -1.0, 0.0)
    for bit in range(9):
        step = 1 << bit
        goes = []
        stays = []
        for x in blocks:
            away = x[:, 20:21, :].astype(I32)
            flag = (away >> bit) & 1
            goes.append(jnp.where((away >= 0) & (flag == 1), 1.0, 0.0))
            stays.append((away >= 0) & (flag == 0))

        def ahead(values, n):
            if step >= SPAN:
                m = n + step // SPAN
                return values[m] if m < len(values) else None
            here = pltpu.roll(values[n], SPAN - step, 2)
            if n + 1 < len(values):
                there = pltpu.roll(values[n + 1], SPAN - step, 2)
            else:
                there = jnp.zeros_like(here)
            return jnp.where(lane < SPAN - step, here, there)

        result = []
        for n, x in enumerate(blocks):
            kept = jnp.where(stays[n], x, blank)
            coming = ahead(goes, n)
            if coming is None:
                result.append(kept)
            else:
                result.append(jnp.where(coming > 0.5, ahead(blocks, n), kept))
        blocks = result
    return blocks


def unpack_kernel(place_ref, got_ref, source_ref, adj_ref, base_ref, far_ref, near_ref):
    place = place_ref[0]
    for n in range(4):
        for side in range(2):
            parts = []
            for a in range(GX):
                d = 2 * a + side
                at = (n % 2) * ROWS
                if n < 2:
                    part = got_ref[d, at : at + ROWS, :].astype(F32)
                    part = part + got_ref[d, 64 + at : 64 + at + ROWS, :].astype(F32)
                else:
                    part = got_ref[d, 128 + at : 128 + at + ROWS, :].astype(F32)
                parts.append(part)
            turned = jnp.concatenate(parts, axis=0).T
            ref = adj_ref if n < 2 else base_ref
            ref[n % 2, side * COLS : (side + 1) * COLS, :] = turned
            far_ref[side, n], near_ref[side, n] = turned_round(
                place, turned[:THIN], turned[COLS - THIN :]
            )
    for c in range(2):
        for side in range(2):
            both = jnp.concatenate(
                [source_ref[c, side, 0:8, :], source_ref[c, side, 8:16, :]], axis=1
            )
            far_ref[side, 4 + c] = both
            near_ref[side, 4 + c] = both


def slots_kernel(got_ref, ints_ref, weight_ref, table_ref):
    ints = got_ref[:, 288:304, :].astype(F32)
    across = lax.broadcasted_iota(I32, (SPAN, SPAN), 0) <= lax.broadcasted_iota(
        I32, (SPAN, SPAN), 1
    )
    across = jnp.where(across, 1.0, 0.0).astype(BF16)
    live = []
    ranks = []
    total = jnp.zeros((TILES, SPAN), F32)
    for g in range(3):
        alive = jnp.where(ints[:, 4 * g + 2, :] >= 0.0, 1.0, 0.0)
        bits = alive.astype(BF16)
        live.append(alive)
        ranks.append(
            total + lax.dot_general(bits, across, NN, preferred_element_type=F32)
        )
        total = total + lax.dot_general(
            bits, jnp.ones((SPAN, SPAN), BF16), NN, preferred_element_type=F32
        )
    filled = jnp.int32(0)
    here = [
        (jnp.max(total[d : d + 1]).astype(I32) + SPAN - 1) // SPAN for d in range(TILES)
    ]
    for d in range(TILES):
        for n in range(DEPTH):

            @pl.when(n < here[d])
            def _():
                table_ref[filled + n] = d * DEPTH + n

        filled = filled + here[d]
    for n in range(GROUP):
        table_ref[filled + n] = EMPTY
    table_ref[COUNT_AT] = filled
    lane = lax.broadcasted_iota(I32, (TILES, SPAN), 1).astype(F32)
    spot = lax.broadcasted_iota(I32, (TILES, 8, SPAN), 1)
    side = (lax.broadcasted_iota(I32, (TILES, 1, SPAN), 0) & 1).astype(F32)
    blocks = []
    for g in range(3):
        away = jnp.where(live[g] > 0.5, lane + float(g * SPAN + 1) - ranks[g], -1.0)
        weights = got_ref[:, 192 + 16 * g : 208 + 16 * g, :].astype(F32)
        weights = weights + got_ref[:, 240 + 16 * g : 256 + 16 * g, :].astype(F32)
        rows = [ints[:, 4 * g + n : 4 * g + n + 1, :] for n in range(4)]
        rows[2] = rows[2] + 48.0 * side + float(16 * g)
        rest = jnp.zeros((TILES, 8, SPAN), F32)
        for n, row in enumerate(rows + [away[:, None, :]]):
            rest = jnp.where(spot == n, row, rest)
        blocks.append(jnp.concatenate([weights, rest], axis=1))
    for n, block in enumerate(closed_up(blocks)):
        for d in range(TILES):
            weight_ref[d * DEPTH + n] = block[d, :16]
            ints_ref[d * DEPTH + n] = block[d, 16:].astype(I32)
    weight_ref[EMPTY] = jnp.zeros((16, SPAN), F32)
    ints_ref[EMPTY] = jnp.zeros((8, SPAN), I32)


def one_hot(index, count):
    spot = lax.broadcasted_iota(I32, (count, index.shape[1]), 0)
    return jnp.where(spot == index, 1.0, 0.0).astype(BF16)


def row_weights(first_row, weights):
    off = lax.broadcasted_iota(I32, (ROWS, SPAN), 0) - first_row
    hits = [off == n for n in range(4)]
    tables = []
    for dj in range(4):
        table = jnp.zeros((ROWS, SPAN), F32)
        for di in (3, 2, 1, 0):
            row = weights[4 * di + dj : 4 * di + dj + 1]
            table = jnp.where(hits[di], row, table)
        tables.append(table)
    return tables


def over_blocks(table_ref, body):
    def run(n, carry):
        ids = [table_ref[GROUP * n + m] for m in range(GROUP)]
        body(ids, [jnp.minimum(block // DEPTH, TILES - 1) for block in ids])
        return carry

    lax.fori_loop(0, (table_ref[COUNT_AT] + GROUP - 1) // GROUP, run, 0)


def joined(ref, ids, row):
    return jnp.concatenate([ref[block, row : row + 1, :] for block in ids], axis=1)


def turned_round(place, one, other):
    odd = (place & 1) == 1
    return jnp.where(odd, other, one), jnp.where(odd, one, other)


def neighbours(place):
    return jnp.where(place == 0, 0.0, 1.0), jnp.where(place == LAST, 0.0, 1.0)


def meeting(place, low, high, reach=1):
    start = place < reach
    end = place > LAST - reach
    has_low = jnp.where(start, 0.0, 1.0)
    has_high = jnp.where(end, 0.0, 1.0)
    lows = (low[0] * has_low, jnp.where(start, low[0], low[1]))
    highs = (jnp.where(end, high[1], high[0]), high[1] * has_high)
    return lows, highs


def masked(place):
    has_low, has_high = neighbours(place)

    def inside(x):
        width = x.shape[0]
        return jnp.concatenate(
            [x[:RIM] * has_low, x[RIM : width - RIM], x[width - RIM :] * has_high], axis=0
        )

    return inside


def projected(wide, inside, looped=False):
    div = 0.5 * (row_next(wide[0]) - row_prev(wide[0])) + 0.5 * (
        col_next(wide[1]) - col_prev(wide[1])
    )
    pressure = inside(-0.25 * div)

    def sweep(_, p):
        return inside(0.25 * (row_next(p) + row_prev(p) + col_next(p) + col_prev(p) - div))

    if looped:
        pressure = lax.fori_loop(0, SWEEPS - 1, sweep, pressure)
    else:
        for n in range(SWEEPS - 1):
            pressure = sweep(n, pressure)
    first = wide[0] - 0.5 * (row_next(pressure) - row_prev(pressure))
    second = wide[1] - 0.5 * (col_next(pressure) - col_prev(pressure))
    return inside(first), inside(second)


def strips(lows, highs, mid_ref, c):
    parts = []
    for side in range(2):
        at = side * COLS
        if mid_ref is None:
            inner = [jnp.zeros((RIM, NROW), F32)] * 2
        else:
            inner = [
                mid_ref[c, at : at + RIM, :],
                mid_ref[c, at + COLS - RIM : at + COLS, :],
            ]
        parts += [lows[side], inner[0], inner[1], highs[side]]
    return jnp.concatenate(parts, axis=0)


def rim_strips(place, far_ref, near_ref):
    result = []
    for c in range(2):
        pairs = [
            turned_round(place, far_ref[side, c].astype(F32), near_ref[side, c].astype(F32))
            for side in range(2)
        ]
        result.append(strips(*meeting(place, *zip(*pairs)), None, c))
    return result


def thin_rims(place, far, near, at):
    pairs = [turned_round(place, far[side, at], near[side, at]) for side in range(2)]
    return meeting(place, *zip(*pairs))


def outer_columns(x, side):
    at = side * 2 * STRIP
    return x[at + RIM : at + 2 * RIM], x[at + STRIP : at + STRIP + RIM]


def widened(mid_ref, c, lows, highs):
    parts = []
    for side in range(2):
        parts += [lows[side], mid_ref[c, side * COLS : (side + 1) * COLS, :], highs[side]]
    return jnp.concatenate(parts, axis=0)


def wide_projected(place, mid_ref):
    blank = (jnp.zeros((RIM, NROW), F32),) * 2
    wide = [widened(mid_ref, c, blank, blank) for c in range(2)]
    return projected(wide, masked(place), looped=True)


def transported(w, base):
    ux = 0.5 * (row_next(base[0]) - row_prev(base[0]))
    vx = 0.5 * (row_next(base[1]) - row_prev(base[1]))
    uy = 0.5 * (col_next(base[0]) - col_prev(base[0]))
    vy = 0.5 * (col_next(base[1]) - col_prev(base[1]))
    mixed = (ux * w[0] + vx * w[1], uy * w[0] + vy * w[1])
    out = []
    for c in range(2):
        east, west = row_next(w[c]), row_prev(w[c])
        north, south = col_next(w[c]), col_prev(w[c])
        laplace = east + west + north + south - 4.0 * w[c]
        value = w[c] + TIME_STEP * (
            base[0] * (0.5 * (east - west))
            + base[1] * (0.5 * (north - south))
            - mixed[c]
            + VISCOSITY * laplace
        )
        out.append(value)
    return out


def interpolate(table_ref, ints_ref, weight_ref, pick_ref, got_refs, sum_ref):
    def blocks(ids, tiles):
        for block, tile, got_ref in zip(ids, tiles, got_refs):
            cols = one_hot(ints_ref[block, 1:2, :], COLS)
            got_ref[...] = lax.dot_general(
                pick_ref[tile],
                jnp.concatenate([cols, cols], axis=0),
                NN,
                preferred_element_type=F32,
            )
        values = []
        for block, got_ref in zip(ids, got_refs):
            tables = row_weights(ints_ref[block, 0:1, :], weight_ref[block])
            both = []
            for c in range(2):
                total = jnp.zeros((ROWS, SPAN), F32)
                for dj in range(4):
                    at = (dj * 2 + c) * ROWS
                    total = total + tables[dj] * got_ref[at : at + ROWS, :]
                both.append(jnp.sum(total, axis=0, keepdims=True))
            values.append(both)
        high = lax.broadcasted_iota(I32, (96, len(ids) * SPAN), 0) == joined(ints_ref, ids, 2)
        parts = [two_parts(jnp.concatenate([v[c] for v in values], axis=1)) for c in range(2)]
        stacked = jnp.concatenate(
            [
                jnp.where(high, parts[c][k].astype(F32), 0.0).astype(BF16)
                for k in range(2)
                for c in range(2)
            ],
            axis=0,
        )
        both = lax.dot_general(
            one_hot(joined(ints_ref, ids, 3), COLS), stacked, NT, preferred_element_type=F32
        )
        sum_ref[...] = sum_ref[...] + both

    sum_ref[...] = jnp.zeros(sum_ref.shape, F32)
    over_blocks(table_ref, blocks)


def pick(field, c, side, pick_ref):
    for dj in range(4):
        shifted = pltpu.roll(field, COLS - dj, 1) if dj else field
        both = jnp.concatenate(two_parts(shifted), axis=1)
        at = (dj * 2 + c) * ROWS
        for a in range(GX):
            pick_ref[2 * a + side, at : at + ROWS, :] = both[a * ROWS : (a + 1) * ROWS]


def first_inner_kernel(mid_ref, base_ref, moved_ref):
    w = [mid_ref[c] for c in range(2)]
    out = transported(w, [base_ref[c] for c in range(2)])
    for c in range(2):
        moved_ref[c] = out[c]


def inner_kernel(place_ref, mid_ref, base_far_ref, base_ref, base_near_ref, moved_ref):
    place = place_ref[0]
    extra = RIM - THIN
    length = COLS + 2 * RIM
    w = [
        jnp.concatenate([x[extra : length - extra], x[length + extra : 2 * length - extra]], axis=0)
        for x in wide_projected(place, mid_ref)
    ]
    base = [
        widened(base_ref, c, *thin_rims(place, base_far_ref, base_near_ref, 2 + c))
        for c in range(2)
    ]
    out = transported(w, base)
    for c in range(2):
        for side in range(2):
            at = side * (COLS + 2 * THIN) + THIN
            moved_ref[c, side * COLS : (side + 1) * COLS, :] = out[c][at : at + COLS]


def outer_kernel(
    first, place_ref, table_ref, far_ref, mid_ref, near_ref, base_far_ref, base_ref,
    base_near_ref, ints_ref, weight_ref, inner_ref, moved_ref, own_ref, part_far, part_near,
    next_far, next_near, pick_ref, sum_ref, *got_refs,
):
    place = place_ref[0]
    blank = jnp.zeros((RIM - THIN, NROW), F32)

    def thin_strips(far, mid, near, c, at):
        lows, highs = thin_rims(place, far, near, at + c)
        return strips(
            [jnp.concatenate([blank, x], axis=0) for x in lows],
            [jnp.concatenate([x, blank], axis=0) for x in highs],
            mid,
            c,
        )

    base = [thin_strips(base_far_ref, base_ref, base_near_ref, c, 2) for c in range(2)]
    if first:
        w = [thin_strips(far_ref, mid_ref, near_ref, c, 0) for c in range(2)]
    else:
        w = projected(rim_strips(place, far_ref, near_ref), masked(place))
    out = transported(w, base)
    spot = lax.broadcasted_iota(I32, (RIM, NROW), 0)
    for c in range(2):
        for side in range(2):
            low, high = outer_columns(out[c], side)
            at = side * COLS
            old_low = inner_ref[c, at : at + RIM, :]
            old_high = inner_ref[c, at + COLS - RIM : at + COLS, :]
            if first:
                low = jnp.where(spot == 0, low, old_low)
                high = jnp.where(spot == RIM - 1, high, old_high)
            else:
                low = old_low + low
                high = old_high + high
            moved = jnp.concatenate(
                [low, inner_ref[c, at + RIM : at + COLS - RIM, :], high], axis=0
            )
            moved_ref[c, at : at + COLS, :] = moved
            pick(moved.T, c, side, pick_ref)
    interpolate(table_ref, ints_ref, weight_ref, pick_ref, got_refs, sum_ref)
    sums = sum_ref[...].T
    sums = sums[:KEPT] + sums[KEPT:]
    for c in range(2):
        for side in range(2):
            at = (2 * c + side) * 48
            one = sums[at : at + 48]
            own_ref[c, side] = one
            part_far[side, c], part_near[side, c] = turned_round(place, one[:32], one[16:])
            next_far[side, c], next_near[side, c] = turned_round(place >> 1, one[:16], one[32:])


def tables_kernel(table_ref, ints_ref, weight_ref, rows_ref, cols_ref):
    def blocks(ids, tiles):
        for block in ids:
            rows_ref[block] = jnp.concatenate(
                row_weights(ints_ref[block, 0:1, :], weight_ref[block]), axis=0
            )
            spot = lax.broadcasted_iota(I32, (COLS, SPAN), 0)
            hits = jnp.where(spot == ints_ref[block, 1:2, :], 1.0, 0.0).T.astype(BF16)
            cols_ref[block] = jnp.concatenate([hits, hits], axis=0)

    rows_ref[EMPTY] = jnp.zeros((4 * ROWS, SPAN), F32)
    cols_ref[EMPTY] = jnp.zeros((2 * SPAN, COLS), BF16)
    over_blocks(table_ref, blocks)


def force_of(sums, source):
    row = lax.broadcasted_iota(I32, sums.shape, 0) & 3
    lane = lax.broadcasted_iota(I32, sums.shape, 1)
    count = sums.shape[0]
    up = jnp.where(row == 0, pltpu.roll(sums, count - 3, 0), pltpu.roll(sums, 1, 0))
    down = jnp.where(row == 3, pltpu.roll(sums, 3, 0), pltpu.roll(sums, count - 1, 0))
    before = jnp.where(lane == 0, pltpu.roll(up, 1, 1), pltpu.roll(sums, 1, 1))
    after = jnp.where(lane == 127, pltpu.roll(down, 127, 1), pltpu.roll(sums, 127, 1))
    bent = before + after - 2.0 * sums
    return STIFFNESS * (sums + source - BENDING * bent)


def spread_kernel(
    place_ref, table_ref, sums_ref, beyond_far, beyond_near, from_far, from_near, thin_far,
    source_ref, thin_near, moved_ref, ints_ref, row_ref, col_ref, out_ref, edge_far, edge_near, own_ref,
    force_ref, acc_ref,
):
    place = place_ref[0]

    def unfolded(ref, side, c):
        return jnp.concatenate([ref[side, 4 + c, :, :COLS], ref[side, 4 + c, :, COLS:]], axis=0)

    for c in range(2):
        pairs = [turned_round(place, from_far[s, c], from_near[s, c]) for s in range(2)]
        lows, highs = meeting(place, *zip(*pairs))
        pairs = [turned_round(place >> 1, beyond_far[s, c], beyond_near[s, c]) for s in range(2)]
        lows2, highs2 = meeting(place, *zip(*pairs), reach=2)
        pairs = [
            turned_round(place, unfolded(thin_far, s, c), unfolded(thin_near, s, c))
            for s in range(2)
        ]
        source_lows, source_highs = meeting(place, *zip(*pairs))
        for side in range(2):
            sums = sums_ref[c, side] + jnp.concatenate(
                [
                    lows[side][:16] + lows2[side],
                    lows[side][16:] + highs[side][:16],
                    highs[side][16:] + highs2[side],
                ],
                axis=0,
            )
            source = jnp.concatenate(
                [source_lows[side], source_ref[c, side], source_highs[side]], axis=0
            )
            force = force_of(sums, source)
            own_ref[c, side] = force[16:32]
            at = (2 * c + side) * 48
            force_ref[at : at + 48, :] = jnp.concatenate(two_parts(force), axis=1)
    acc_ref[...] = jnp.zeros(acc_ref.shape, F32)

    def blocks(ids, tiles):
        spots = one_hot(joined(ints_ref, ids, 3), COLS)
        picked = lax.dot_general(
            force_ref[...], jnp.concatenate([spots, spots], axis=0), NN,
            preferred_element_type=F32,
        )
        high = lax.broadcasted_iota(I32, (96, len(ids) * SPAN), 0) == joined(ints_ref, ids, 2)
        forces = [
            TIME_STEP
            * jnp.sum(jnp.where(high, picked[96 * c : 96 * c + 96], 0.0), axis=0, keepdims=True)
            for c in range(2)
        ]
        sums = []
        for m, block in enumerate(ids):
            lanes = slice(m * SPAN, (m + 1) * SPAN)
            weighted = jnp.concatenate(
                [row_ref[block] * forces[c][:, lanes] for c in range(2)], axis=0
            )
            sums.append(
                lax.dot_general(
                    jnp.concatenate(two_parts(weighted), axis=1),
                    col_ref[block],
                    NN,
                    preferred_element_type=F32,
                )
            )
        for tile, one in zip(tiles, sums):
            acc_ref[tile] = acc_ref[tile] + one

    over_blocks(table_ref, blocks)
    for c in range(2):
        for side in range(2):
            rows = []
            for a in range(GX):
                total = jnp.zeros((ROWS, COLS), F32)
                for dj in range(4):
                    at = (4 * c + dj) * ROWS
                    one = acc_ref[2 * a + side, at : at + ROWS, :]
                    total = total + (pltpu.roll(one, dj, 1) if dj else one)
                rows.append(total)
            cols = slice(side * COLS, (side + 1) * COLS)
            total = moved_ref[c, cols, :] + jnp.concatenate(rows, axis=0).T
            out_ref[c, cols, :] = total
            far, near = turned_round(place, total[:RIM], total[COLS - RIM :])
            edge_far[side, c] = far.astype(BF16)
            edge_near[side, c] = near.astype(BF16)


def finish_inner_kernel(place_ref, mid_ref, out_ref):
    w = wide_projected(place_ref[0], mid_ref)
    for c in range(2):
        for side in range(2):
            at = side * (COLS + 2 * RIM) + RIM
            block = w[c][at : at + COLS].T
            for a in range(GX):
                out_ref[2 * a + side, c] = block[a * ROWS : (a + 1) * ROWS]


def finish_outer_kernel(place_ref, far_ref, near_ref, inner_ref, out_ref):
    place = place_ref[0]
    w = projected(rim_strips(place, far_ref, near_ref), masked(place))
    blank = jnp.zeros((COLS - 2 * RIM, NROW), F32)
    for c in range(2):
        for side in range(2):
            low, high = outer_columns(w[c], side)
            both = jnp.concatenate([low, blank, high], axis=0).T
            for a in range(GX):
                out_ref[2 * a + side, c] = (
                    inner_ref[2 * a + side, c] + both[a * ROWS : (a + 1) * ROWS]
                )


def on_device(adjoint, base_flow, slot_cell, slot_marker, slot_count, slot_weight, marker_source):
    place = lax.axis_index("zc").astype(I32).reshape(1)
    half = lax.axis_index("xh")
    whole = ("gx", "xh")
    tiles = marker_source.reshape(2, 2, 16, COLS)
    kept = lax.dynamic_index_in_dim(tiles, half, axis=1, keepdims=False)
    other = swapped(lax.dynamic_index_in_dim(tiles, 1 - half, axis=1, keepdims=False))
    source = jnp.where(
        half == 0, jnp.stack([kept, other], axis=1), jnp.stack([other, kept], axis=1)
    )
    packed = call(
        pack_kernel,
        shape(2 * GX, PACK, COLS, dtype=BF16),
        (slot_count, adjoint, base_flow, slot_cell[0, 0], slot_marker[0, 0], slot_weight[0, 0]),
        scratch=(
            pltpu.SMEM((1, 1, 3, GX), I32),
            pltpu.VMEM(adjoint.shape, F32),
            pltpu.VMEM(base_flow.shape, BF16),
            pltpu.VMEM((3, GX, COLS), I32),
            pltpu.VMEM((3, GX, COLS), I32),
            pltpu.VMEM((3, GX, 16, COLS), F32),
            pltpu.SemaphoreType.DMA((6,)),
        ),
        spaces={n: HBM for n in range(6)},
        params=ROOMY,
    )
    got = lax.all_to_all(packed, whole, split_axis=0, concat_axis=0, tiled=True)
    field = shape(2, NCOL, NROW)
    thin = shape(2, 6, THIN, NROW)
    current, base, thin_far, thin_near = call(
        unpack_kernel, (field, field, thin, thin), (place, got, source), spaces={0: SMEM}
    )
    base_far, base_near = exchanged(thin_far, thin_near)
    ints, weights, table = call(
        slots_kernel,
        (
            shape(EMPTY + 1, 8, SPAN, dtype=I32),
            shape(EMPTY + 1, 16, SPAN),
            shape(128, dtype=I32),
        ),
        (got,),
        out_specs=(VMEM, VMEM, SMEM),
    )
    far, near = base_far, base_near
    part = shape(2, 2, 32, COLS)
    beyond = shape(2, 2, 16, COLS)
    rim = shape(2, 2, RIM, NROW, dtype=BF16)
    forces = source
    row_tables = col_tables = None
    for substep in range(SUBSTEPS):
        if substep == 0:
            inner = call(first_inner_kernel, field, (current, base))
        else:
            inner = call(
                inner_kernel,
                field,
                (place, current, base_far, base, base_near),
                spaces={0: SMEM},
            )
        moved, sums, part_far, part_near, next_far, next_near = call(
            functools.partial(outer_kernel, substep == 0),
            (field, shape(2, 2, 48, COLS), part, part, beyond, beyond),
            (place, table, far, current, near, base_far, base, base_near, ints, weights, inner),
            scratch=OUTER_SCRATCH,
            spaces={0: SMEM, 1: SMEM},
        )
        beyond_far, beyond_near = exchanged(next_far, next_near, 2)
        from_far, from_near = exchanged(part_far, part_near)
        if substep == 0:
            row_tables, col_tables = call(
                tables_kernel,
                (
                    shape(EMPTY + 1, 4 * ROWS, SPAN),
                    shape(EMPTY + 1, 2 * SPAN, COLS, dtype=BF16),
                ),
                (table, ints, weights),
                spaces={0: SMEM},
            )
        current, edge_far, edge_near, forces = call(
            spread_kernel,
            (field, rim, rim, shape(2, 2, 16, COLS)),
            (
                place, table, sums, beyond_far, beyond_near, from_far, from_near, base_far,
                source, base_near, moved, ints, row_tables, col_tables,
            ),
            scratch=SPREAD_SCRATCH,
            spaces={0: SMEM, 1: SMEM},
        )
        far, near = exchanged(edge_far, edge_near)
    tiles_out = shape(2 * GX, 2, ROWS, COLS)
    inner = call(finish_inner_kernel, tiles_out, (place, current), spaces={0: SMEM})
    done = call(finish_outer_kernel, tiles_out, (place, far, near, inner), spaces={0: SMEM})
    back = lax.all_to_all(done, whole, split_axis=0, concat_axis=0, tiled=True)
    result = jnp.transpose(back, (1, 0, 2, 3))
    mine = lax.dynamic_index_in_dim(forces, half, axis=1, keepdims=False)
    theirs = swapped(lax.dynamic_index_in_dim(forces, 1 - half, axis=1, keepdims=False))
    planes = jnp.where(
        half == 0, jnp.stack([mine, theirs], axis=1), jnp.stack([theirs, mine], axis=1)
    )
    return (result, planes.reshape(marker_source.shape))


def solution(mesh):
    split = Mesh(mesh.devices.reshape(8, 2, 8), ("gx", "xh", "zc"))
    gy = ("xh", "zc")
    in_specs = (
        P(None, None, "gx", gy),
        P(None, None, "gx", gy),
        P("gx", gy, None, None, None),
        P("gx", gy, None, None, None),
        P("gx", gy, None, None),
        P("gx", gy, None, None, None, None),
        P(None, "gx", gy, None),
    )
    out_specs = (P(None, None, "gx", gy), P(None, "gx", gy, None))
    return jax.shard_map(
        on_device, mesh=split, in_specs=in_specs, out_specs=out_specs, check_vma=False
    )
```

```python
import functools

import jax
import jax.numpy as jnp
from jax import lax
from jax.experimental import pallas as pl
from jax.experimental.pallas import tpu as pltpu
from jax.sharding import Mesh, PartitionSpec as P

SUBSTEPS = 3
SWEEPS = 8

TIME_STEP = 0.5
VISCOSITY = 0.2
STIFFNESS = 2.0
BENDING = 0.25

F32 = jnp.float32
BF16 = jnp.bfloat16
I32 = jnp.int32

GX = 8
ROWS = 32
COLS = 128
NROW = GX * ROWS
NCOL = 2 * COLS
LAST = 7
RIM = 16
STRIP = 2 * RIM
THIN = 8
KEPT = 192
PACK = 304
SPAN = 128
TILES = 2 * GX
DEPTH = 3
EMPTY = TILES * DEPTH
COUNT_AT = 127
GROUP = 12

NT = (((1,), (1,)), ((), ()))
NN = (((1,), (0,)), ((), ()))

PARAMS = pltpu.CompilerParams(vmem_limit_bytes=24 * 1024 * 1024)
ROOMY = pltpu.CompilerParams(vmem_limit_bytes=60 * 1024 * 1024)
VMEM = pl.BlockSpec(memory_space=pltpu.VMEM)
SMEM = pl.BlockSpec(memory_space=pltpu.SMEM)
HBM = pl.BlockSpec(memory_space=pltpu.HBM)


def call(body, outs, ins, scratch=(), spaces=(), out_specs=None, params=PARAMS):
    spaces = dict(spaces)
    return pl.pallas_call(
        body,
        out_shape=outs,
        in_specs=[spaces.get(n, VMEM) for n in range(len(ins))],
        out_specs=out_specs or jax.tree.map(lambda _: VMEM, outs),
        scratch_shapes=list(scratch),
        compiler_params=params,
    )(*ins)


OUTER_SCRATCH = (
    pltpu.VMEM((TILES, 8 * ROWS, 2 * COLS), BF16),
    pltpu.VMEM((COLS, 2 * KEPT), F32),
) + tuple(pltpu.VMEM((8 * ROWS, SPAN), F32) for _ in range(GROUP))
SPREAD_SCRATCH = (
    pltpu.VMEM((KEPT, 2 * COLS), BF16),
    pltpu.VMEM((TILES, 8 * ROWS, COLS), F32),
)


def shape(*dims, dtype=F32):
    return jax.ShapeDtypeStruct(dims, dtype)


def exchanged(far, near, step=1):
    count = lax.axis_size("zc")
    ups = [(n, (n + step) % count) for n in range(count)]
    results = []
    for value, parity in ((far, 1), (near, 0)):
        pairs = [pair for pair in ups if (pair[0] // step) % 2 == parity]
        pairs = pairs + [(target, source) for source, target in pairs]
        results.append(lax.ppermute(value, "zc", pairs))
    return results


def swapped(value):
    return lax.ppermute(value, "xh", [(0, 1), (1, 0)])


def two_parts(value):
    high = value.astype(BF16)
    return high, (value - high.astype(F32)).astype(BF16)


def row_next(x):
    lane = lax.broadcasted_iota(I32, x.shape, 1)
    return jnp.where(lane == NROW - 1, 0.0, pltpu.roll(x, NROW - 1, 1))


def row_prev(x):
    lane = lax.broadcasted_iota(I32, x.shape, 1)
    return jnp.where(lane == 0, 0.0, pltpu.roll(x, 1, 1))


def col_next(x):
    return pltpu.roll(x, x.shape[0] - 1, 0)


def col_prev(x):
    return pltpu.roll(x, 1, 0)


def pack_kernel(
    count_hbm, adj_hbm, base_hbm, cell_hbm, mark_hbm, weight_hbm, out_ref,
    count_ref, adj_ref, base_ref, cell_ref, mark_ref, weight_ref, sems,
):
    copies = [
        pltpu.make_async_copy(src, dst, sems.at[n])
        for n, (src, dst) in enumerate(
            (
                (cell_hbm, cell_ref),
                (mark_hbm, mark_ref),
                (weight_hbm, weight_ref),
                (base_hbm, base_ref),
                (adj_hbm, adj_ref),
                (count_hbm, count_ref),
            )
        )
    ]
    for copy in copies:
        copy.start()
    copies[5].wait()
    copies[0].wait()
    copies[1].wait()
    lane = lax.broadcasted_iota(I32, (1, COLS), 1)
    none = jnp.zeros((4, COLS), F32)
    for e in range(GX):
        for q in range(2):
            rows = []
            for g in range(3):
                cell = cell_ref[g, e : e + 1, :]
                mark = mark_ref[g, e : e + 1, :]
                live = (lane < count_ref[0, 0, g, e]) & ((mark >> 11) == q)
                rows += [cell >> 7, cell & 127, jnp.where(live, (mark >> 7) & 15, -1), mark & 127]
            ints = jnp.concatenate([r.astype(F32) for r in rows] + [none], axis=0)
            out_ref[2 * e + q, 288:304, :] = ints.astype(BF16)
    copies[2].wait()
    for e in range(GX):
        for g in range(3):
            hi, lo = two_parts(weight_ref[g, e])
            for q in range(2):
                out_ref[2 * e + q, 192 + 16 * g : 208 + 16 * g, :] = hi
                out_ref[2 * e + q, 240 + 16 * g : 256 + 16 * g, :] = lo
    copies[3].wait()
    for p in range(2 * GX):
        for c in range(2):
            out_ref[p, 128 + c * ROWS : 128 + (c + 1) * ROWS, :] = base_ref[c, p]
    copies[4].wait()
    for p in range(2 * GX):
        for c in range(2):
            hi, lo = two_parts(adj_ref[c, p])
            out_ref[p, c * ROWS : (c + 1) * ROWS, :] = hi
            out_ref[p, 64 + c * ROWS : 64 + (c + 1) * ROWS, :] = lo


def closed_up(blocks):
    lane = lax.broadcasted_iota(I32, (1, 1, SPAN), 2)
    spot = lax.broadcasted_iota(I32, (1, 24, SPAN), 1)
    blank = jnp.where(spot == 20, -1.0, 0.0)
    for bit in range(9):
        step = 1 << bit
        goes = []
        stays = []
        for x in blocks:
            away = x[:, 20:21, :].astype(I32)
            flag = (away >> bit) & 1
            goes.append(jnp.where((away >= 0) & (flag == 1), 1.0, 0.0))
            stays.append((away >= 0) & (flag == 0))

        def ahead(values, n):
            if step >= SPAN:
                m = n + step // SPAN
                return values[m] if m < len(values) else None
            here = pltpu.roll(values[n], SPAN - step, 2)
            if n + 1 < len(values):
                there = pltpu.roll(values[n + 1], SPAN - step, 2)
            else:
                there = jnp.zeros_like(here)
            return jnp.where(lane < SPAN - step, here, there)

        result = []
        for n, x in enumerate(blocks):
            kept = jnp.where(stays[n], x, blank)
            coming = ahead(goes, n)
            if coming is None:
                result.append(kept)
            else:
                result.append(jnp.where(coming > 0.5, ahead(blocks, n), kept))
        blocks = result
    return blocks


def unpack_kernel(place_ref, got_ref, source_ref, adj_ref, base_ref, far_ref, near_ref):
    place = place_ref[0]
    for n in range(4):
        for side in range(2):
            parts = []
            for a in range(GX):
                d = 2 * a + side
                at = (n % 2) * ROWS
                if n < 2:
                    part = got_ref[d, at : at + ROWS, :].astype(F32)
                    part = part + got_ref[d, 64 + at : 64 + at + ROWS, :].astype(F32)
                else:
                    part = got_ref[d, 128 + at : 128 + at + ROWS, :].astype(F32)
                parts.append(part)
            turned = jnp.concatenate(parts, axis=0).T
            ref = adj_ref if n < 2 else base_ref
            ref[n % 2, side * COLS : (side + 1) * COLS, :] = turned
            far_ref[side, n], near_ref[side, n] = turned_round(
                place, turned[:THIN], turned[COLS - THIN :]
            )
    for c in range(2):
        for side in range(2):
            both = jnp.concatenate(
                [source_ref[c, side, 0:8, :], source_ref[c, side, 8:16, :]], axis=1
            )
            far_ref[side, 4 + c] = both
            near_ref[side, 4 + c] = both


def slots_kernel(got_ref, ints_ref, weight_ref, table_ref):
    ints = got_ref[:, 288:304, :].astype(F32)
    across = lax.broadcasted_iota(I32, (SPAN, SPAN), 0) <= lax.broadcasted_iota(
        I32, (SPAN, SPAN), 1
    )
    across = jnp.where(across, 1.0, 0.0).astype(BF16)
    live = []
    ranks = []
    total = jnp.zeros((TILES, SPAN), F32)
    for g in range(3):
        alive = jnp.where(ints[:, 4 * g + 2, :] >= 0.0, 1.0, 0.0)
        bits = alive.astype(BF16)
        live.append(alive)
        ranks.append(
            total + lax.dot_general(bits, across, NN, preferred_element_type=F32)
        )
        total = total + lax.dot_general(
            bits, jnp.ones((SPAN, SPAN), BF16), NN, preferred_element_type=F32
        )
    filled = jnp.int32(0)
    here = [
        (jnp.max(total[d : d + 1]).astype(I32) + SPAN - 1) // SPAN for d in range(TILES)
    ]
    for d in range(TILES):
        for n in range(DEPTH):

            @pl.when(n < here[d])
            def _():
                table_ref[filled + n] = d * DEPTH + n

        filled = filled + here[d]
    for n in range(GROUP):
        table_ref[filled + n] = EMPTY
    table_ref[COUNT_AT] = filled
    lane = lax.broadcasted_iota(I32, (TILES, SPAN), 1).astype(F32)
    spot = lax.broadcasted_iota(I32, (TILES, 8, SPAN), 1)
    side = (lax.broadcasted_iota(I32, (TILES, 1, SPAN), 0) & 1).astype(F32)
    blocks = []
    for g in range(3):
        away = jnp.where(live[g] > 0.5, lane + float(g * SPAN + 1) - ranks[g], -1.0)
        weights = got_ref[:, 192 + 16 * g : 208 + 16 * g, :].astype(F32)
        weights = weights + got_ref[:, 240 + 16 * g : 256 + 16 * g, :].astype(F32)
        rows = [ints[:, 4 * g + n : 4 * g + n + 1, :] for n in range(4)]
        rows[2] = rows[2] + 48.0 * side + float(16 * g)
        rest = jnp.zeros((TILES, 8, SPAN), F32)
        for n, row in enumerate(rows + [away[:, None, :]]):
            rest = jnp.where(spot == n, row, rest)
        blocks.append(jnp.concatenate([weights, rest], axis=1))
    for n, block in enumerate(closed_up(blocks)):
        for d in range(TILES):
            weight_ref[d * DEPTH + n] = block[d, :16]
            ints_ref[d * DEPTH + n] = block[d, 16:].astype(I32)
    weight_ref[EMPTY] = jnp.zeros((16, SPAN), F32)
    ints_ref[EMPTY] = jnp.zeros((8, SPAN), I32)


def one_hot(index, count):
    spot = lax.broadcasted_iota(I32, (count, index.shape[1]), 0)
    return jnp.where(spot == index, 1.0, 0.0).astype(BF16)


def row_weights(first_row, weights):
    off = lax.broadcasted_iota(I32, (ROWS, SPAN), 0) - first_row
    hits = [off == n for n in range(4)]
    tables = []
    for dj in range(4):
        table = jnp.zeros((ROWS, SPAN), F32)
        for di in (3, 2, 1, 0):
            row = weights[4 * di + dj : 4 * di + dj + 1]
            table = jnp.where(hits[di], row, table)
        tables.append(table)
    return tables


def over_blocks(table_ref, body):
    def run(n, carry):
        ids = [table_ref[GROUP * n + m] for m in range(GROUP)]
        body(ids, [jnp.minimum(block // DEPTH, TILES - 1) for block in ids])
        return carry

    lax.fori_loop(0, (table_ref[COUNT_AT] + GROUP - 1) // GROUP, run, 0)


def joined(ref, ids, row):
    return jnp.concatenate([ref[block, row : row + 1, :] for block in ids], axis=1)


def turned_round(place, one, other):
    odd = (place & 1) == 1
    return jnp.where(odd, other, one), jnp.where(odd, one, other)


def neighbours(place):
    return jnp.where(place == 0, 0.0, 1.0), jnp.where(place == LAST, 0.0, 1.0)


def meeting(place, low, high, reach=1):
    start = place < reach
    end = place > LAST - reach
    has_low = jnp.where(start, 0.0, 1.0)
    has_high = jnp.where(end, 0.0, 1.0)
    lows = (low[0] * has_low, jnp.where(start, low[0], low[1]))
    highs = (jnp.where(end, high[1], high[0]), high[1] * has_high)
    return lows, highs


def masked(place):
    has_low, has_high = neighbours(place)

    def inside(x):
        width = x.shape[0]
        return jnp.concatenate(
            [x[:RIM] * has_low, x[RIM : width - RIM], x[width - RIM :] * has_high], axis=0
        )

    return inside


def projected(wide, inside, looped=False):
    div = 0.5 * (row_next(wide[0]) - row_prev(wide[0])) + 0.5 * (
        col_next(wide[1]) - col_prev(wide[1])
    )
    pressure = inside(-0.25 * div)

    def sweep(_, p):
        return inside(0.25 * (row_next(p) + row_prev(p) + col_next(p) + col_prev(p) - div))

    if looped:
        pressure = lax.fori_loop(0, SWEEPS - 1, sweep, pressure)
    else:
        for n in range(SWEEPS - 1):
            pressure = sweep(n, pressure)
    first = wide[0] - 0.5 * (row_next(pressure) - row_prev(pressure))
    second = wide[1] - 0.5 * (col_next(pressure) - col_prev(pressure))
    return inside(first), inside(second)


def strips(lows, highs, mid_ref, c):
    parts = []
    for side in range(2):
        at = side * COLS
        if mid_ref is None:
            inner = [jnp.zeros((RIM, NROW), F32)] * 2
        else:
            inner = [
                mid_ref[c, at : at + RIM, :],
                mid_ref[c, at + COLS - RIM : at + COLS, :],
            ]
        parts += [lows[side], inner[0], inner[1], highs[side]]
    return jnp.concatenate(parts, axis=0)


def rim_strips(place, far_ref, near_ref):
    result = []
    for c in range(2):
        pairs = [
            turned_round(place, far_ref[side, c].astype(F32), near_ref[side, c].astype(F32))
            for side in range(2)
        ]
        result.append(strips(*meeting(place, *zip(*pairs)), None, c))
    return result


def thin_rims(place, far, near, at):
    pairs = [turned_round(place, far[side, at], near[side, at]) for side in range(2)]
    return meeting(place, *zip(*pairs))


def outer_columns(x, side):
    at = side * 2 * STRIP
    return x[at + RIM : at + 2 * RIM], x[at + STRIP : at + STRIP + RIM]


def widened(mid_ref, c, lows, highs):
    parts = []
    for side in range(2):
        parts += [lows[side], mid_ref[c, side * COLS : (side + 1) * COLS, :], highs[side]]
    return jnp.concatenate(parts, axis=0)


def wide_projected(place, mid_ref):
    blank = (jnp.zeros((RIM, NROW), F32),) * 2
    wide = [widened(mid_ref, c, blank, blank) for c in range(2)]
    return projected(wide, masked(place), looped=True)


def transported(w, base):
    ux = 0.5 * (row_next(base[0]) - row_prev(base[0]))
    vx = 0.5 * (row_next(base[1]) - row_prev(base[1]))
    uy = 0.5 * (col_next(base[0]) - col_prev(base[0]))
    vy = 0.5 * (col_next(base[1]) - col_prev(base[1]))
    mixed = (ux * w[0] + vx * w[1], uy * w[0] + vy * w[1])
    out = []
    for c in range(2):
        east, west = row_next(w[c]), row_prev(w[c])
        north, south = col_next(w[c]), col_prev(w[c])
        laplace = east + west + north + south - 4.0 * w[c]
        value = w[c] + TIME_STEP * (
            base[0] * (0.5 * (east - west))
            + base[1] * (0.5 * (north - south))
            - mixed[c]
            + VISCOSITY * laplace
        )
        out.append(value)
    return out


def interpolate(table_ref, ints_ref, weight_ref, pick_ref, got_refs, sum_ref):
    def blocks(ids, tiles):
        for block, tile, got_ref in zip(ids, tiles, got_refs):
            cols = one_hot(ints_ref[block, 1:2, :], COLS)
            got_ref[...] = lax.dot_general(
                pick_ref[tile],
                jnp.concatenate([cols, cols], axis=0),
                NN,
                preferred_element_type=F32,
            )
        values = []
        for block, got_ref in zip(ids, got_refs):
            tables = row_weights(ints_ref[block, 0:1, :], weight_ref[block])
            both = []
            for c in range(2):
                total = jnp.zeros((ROWS, SPAN), F32)
                for dj in range(4):
                    at = (dj * 2 + c) * ROWS
                    total = total + tables[dj] * got_ref[at : at + ROWS, :]
                both.append(jnp.sum(total, axis=0, keepdims=True))
            values.append(both)
        high = lax.broadcasted_iota(I32, (96, len(ids) * SPAN), 0) == joined(ints_ref, ids, 2)
        parts = [two_parts(jnp.concatenate([v[c] for v in values], axis=1)) for c in range(2)]
        stacked = jnp.concatenate(
            [
                jnp.where(high, parts[c][k].astype(F32), 0.0).astype(BF16)
                for k in range(2)
                for c in range(2)
            ],
            axis=0,
        )
        both = lax.dot_general(
            one_hot(joined(ints_ref, ids, 3), COLS), stacked, NT, preferred_element_type=F32
        )
        sum_ref[...] = sum_ref[...] + both

    sum_ref[...] = jnp.zeros(sum_ref.shape, F32)
    over_blocks(table_ref, blocks)


def pick(field, c, side, pick_ref):
    for dj in range(4):
        shifted = pltpu.roll(field, COLS - dj, 1) if dj else field
        both = jnp.concatenate(two_parts(shifted), axis=1)
        at = (dj * 2 + c) * ROWS
        for a in range(GX):
            pick_ref[2 * a + side, at : at + ROWS, :] = both[a * ROWS : (a + 1) * ROWS]


def inner_kernel(place_ref, mid_ref, base_far_ref, base_ref, base_near_ref, moved_ref):
    place = place_ref[0]
    extra = RIM - THIN
    length = COLS + 2 * RIM
    w = [
        jnp.concatenate([x[extra : length - extra], x[length + extra : 2 * length - extra]], axis=0)
        for x in wide_projected(place, mid_ref)
    ]
    base = [
        widened(base_ref, c, *thin_rims(place, base_far_ref, base_near_ref, 2 + c))
        for c in range(2)
    ]
    out = transported(w, base)
    for c in range(2):
        for side in range(2):
            at = side * (COLS + 2 * THIN) + THIN
            moved_ref[c, side * COLS : (side + 1) * COLS, :] = out[c][at : at + COLS]


def first_moved(place, far_ref, mid_ref, near_ref, base_ref):
    w, base = (
        [widened(ref, c, *thin_rims(place, far_ref, near_ref, at + c)) for c in range(2)]
        for ref, at in ((mid_ref, 0), (base_ref, 2))
    )
    length = COLS + 2 * THIN
    return [
        [x[side * length + THIN : side * length + THIN + COLS] for side in range(2)]
        for x in transported(w, base)
    ]


def later_moved(place, far_ref, near_ref, base_far_ref, base_ref, base_near_ref, inner_ref):
    blank = jnp.zeros((RIM - THIN, NROW), F32)
    base = []
    for c in range(2):
        lows, highs = thin_rims(place, base_far_ref, base_near_ref, 2 + c)
        lows = [jnp.concatenate([blank, x], axis=0) for x in lows]
        highs = [jnp.concatenate([x, blank], axis=0) for x in highs]
        base.append(strips(lows, highs, base_ref, c))
    out = transported(projected(rim_strips(place, far_ref, near_ref), masked(place)), base)
    moved = []
    for c in range(2):
        tiles = []
        for side in range(2):
            low, high = outer_columns(out[c], side)
            at = side * COLS
            tiles.append(
                jnp.concatenate(
                    [
                        inner_ref[c, at : at + RIM, :] + low,
                        inner_ref[c, at + RIM : at + COLS - RIM, :],
                        inner_ref[c, at + COLS - RIM : at + COLS, :] + high,
                    ],
                    axis=0,
                )
            )
        moved.append(tiles)
    return moved


def outer_kernel(
    first, place_ref, table_ref, far_ref, near_ref, base_far_ref, base_ref, base_near_ref,
    ints_ref, weight_ref, inner_ref, moved_ref, own_ref, part_far, part_near,
    next_far, next_near, pick_ref, sum_ref, *got_refs,
):
    place = place_ref[0]
    if first:
        moved = first_moved(place, far_ref, inner_ref, near_ref, base_ref)
    else:
        moved = later_moved(
            place, far_ref, near_ref, base_far_ref, base_ref, base_near_ref, inner_ref
        )
    for c in range(2):
        for side in range(2):
            moved_ref[c, side * COLS : (side + 1) * COLS, :] = moved[c][side]
            pick(moved[c][side].T, c, side, pick_ref)
    interpolate(table_ref, ints_ref, weight_ref, pick_ref, got_refs, sum_ref)
    sums = sum_ref[...].T
    sums = sums[:KEPT] + sums[KEPT:]
    for c in range(2):
        for side in range(2):
            at = (2 * c + side) * 48
            one = sums[at : at + 48]
            own_ref[c, side] = one
            part_far[side, c], part_near[side, c] = turned_round(place, one[:32], one[16:])
            next_far[side, c], next_near[side, c] = turned_round(place >> 1, one[:16], one[32:])


def tables_kernel(table_ref, ints_ref, weight_ref, rows_ref, cols_ref):
    def blocks(ids, tiles):
        for block in ids:
            rows_ref[block] = jnp.concatenate(
                row_weights(ints_ref[block, 0:1, :], weight_ref[block]), axis=0
            )
            spot = lax.broadcasted_iota(I32, (COLS, SPAN), 0)
            hits = jnp.where(spot == ints_ref[block, 1:2, :], 1.0, 0.0).T.astype(BF16)
            cols_ref[block] = jnp.concatenate([hits, hits], axis=0)

    rows_ref[EMPTY] = jnp.zeros((4 * ROWS, SPAN), F32)
    cols_ref[EMPTY] = jnp.zeros((2 * SPAN, COLS), BF16)
    over_blocks(table_ref, blocks)


def force_of(sums, source):
    row = lax.broadcasted_iota(I32, sums.shape, 0) & 3
    lane = lax.broadcasted_iota(I32, sums.shape, 1)
    count = sums.shape[0]
    up = jnp.where(row == 0, pltpu.roll(sums, count - 3, 0), pltpu.roll(sums, 1, 0))
    down = jnp.where(row == 3, pltpu.roll(sums, 3, 0), pltpu.roll(sums, count - 1, 0))
    before = jnp.where(lane == 0, pltpu.roll(up, 1, 1), pltpu.roll(sums, 1, 1))
    after = jnp.where(lane == 127, pltpu.roll(down, 127, 1), pltpu.roll(sums, 127, 1))
    bent = before + after - 2.0 * sums
    return STIFFNESS * (sums + source - BENDING * bent)


def spread_kernel(
    place_ref, table_ref, sums_ref, beyond_far, beyond_near, from_far, from_near, thin_far,
    source_ref, thin_near, moved_ref, ints_ref, row_ref, col_ref, out_ref, edge_far, edge_near, own_ref,
    force_ref, acc_ref,
):
    place = place_ref[0]

    def unfolded(ref, side, c):
        return jnp.concatenate([ref[side, 4 + c, :, :COLS], ref[side, 4 + c, :, COLS:]], axis=0)

    for c in range(2):
        pairs = [turned_round(place, from_far[s, c], from_near[s, c]) for s in range(2)]
        lows, highs = meeting(place, *zip(*pairs))
        pairs = [turned_round(place >> 1, beyond_far[s, c], beyond_near[s, c]) for s in range(2)]
        lows2, highs2 = meeting(place, *zip(*pairs), reach=2)
        pairs = [
            turned_round(place, unfolded(thin_far, s, c), unfolded(thin_near, s, c))
            for s in range(2)
        ]
        source_lows, source_highs = meeting(place, *zip(*pairs))
        for side in range(2):
            sums = sums_ref[c, side] + jnp.concatenate(
                [
                    lows[side][:16] + lows2[side],
                    lows[side][16:] + highs[side][:16],
                    highs[side][16:] + highs2[side],
                ],
                axis=0,
            )
            source = jnp.concatenate(
                [source_lows[side], source_ref[c, side], source_highs[side]], axis=0
            )
            force = force_of(sums, source)
            own_ref[c, side] = force[16:32]
            at = (2 * c + side) * 48
            force_ref[at : at + 48, :] = jnp.concatenate(two_parts(force), axis=1)
    acc_ref[...] = jnp.zeros(acc_ref.shape, F32)

    def blocks(ids, tiles):
        spots = one_hot(joined(ints_ref, ids, 3), COLS)
        picked = lax.dot_general(
            force_ref[...], jnp.concatenate([spots, spots], axis=0), NN,
            preferred_element_type=F32,
        )
        high = lax.broadcasted_iota(I32, (96, len(ids) * SPAN), 0) == joined(ints_ref, ids, 2)
        forces = [
            TIME_STEP
            * jnp.sum(jnp.where(high, picked[96 * c : 96 * c + 96], 0.0), axis=0, keepdims=True)
            for c in range(2)
        ]
        sums = []
        for m, block in enumerate(ids):
            lanes = slice(m * SPAN, (m + 1) * SPAN)
            weighted = jnp.concatenate(
                [row_ref[block] * forces[c][:, lanes] for c in range(2)], axis=0
            )
            sums.append(
                lax.dot_general(
                    jnp.concatenate(two_parts(weighted), axis=1),
                    col_ref[block],
                    NN,
                    preferred_element_type=F32,
                )
            )
        for tile, one in zip(tiles, sums):
            acc_ref[tile] = acc_ref[tile] + one

    over_blocks(table_ref, blocks)
    for c in range(2):
        for side in range(2):
            rows = []
            for a in range(GX):
                total = jnp.zeros((ROWS, COLS), F32)
                for dj in range(4):
                    at = (4 * c + dj) * ROWS
                    one = acc_ref[2 * a + side, at : at + ROWS, :]
                    total = total + (pltpu.roll(one, dj, 1) if dj else one)
                rows.append(total)
            cols = slice(side * COLS, (side + 1) * COLS)
            total = moved_ref[c, cols, :] + jnp.concatenate(rows, axis=0).T
            out_ref[c, cols, :] = total
            far, near = turned_round(place, total[:RIM], total[COLS - RIM :])
            edge_far[side, c] = far.astype(BF16)
            edge_near[side, c] = near.astype(BF16)


def finish_inner_kernel(place_ref, mid_ref, out_ref):
    w = wide_projected(place_ref[0], mid_ref)
    for c in range(2):
        for side in range(2):
            at = side * (COLS + 2 * RIM) + RIM
            block = w[c][at : at + COLS].T
            for a in range(GX):
                out_ref[2 * a + side, c] = block[a * ROWS : (a + 1) * ROWS]


def finish_outer_kernel(place_ref, far_ref, near_ref, inner_ref, out_ref):
    place = place_ref[0]
    w = projected(rim_strips(place, far_ref, near_ref), masked(place))
    blank = jnp.zeros((COLS - 2 * RIM, NROW), F32)
    for c in range(2):
        for side in range(2):
            low, high = outer_columns(w[c], side)
            both = jnp.concatenate([low, blank, high], axis=0).T
            for a in range(GX):
                out_ref[2 * a + side, c] = (
                    inner_ref[2 * a + side, c] + both[a * ROWS : (a + 1) * ROWS]
                )


def on_device(adjoint, base_flow, slot_cell, slot_marker, slot_count, slot_weight, marker_source):
    place = lax.axis_index("zc").astype(I32).reshape(1)
    half = lax.axis_index("xh")
    whole = ("gx", "xh")
    tiles = marker_source.reshape(2, 2, 16, COLS)
    kept = lax.dynamic_index_in_dim(tiles, half, axis=1, keepdims=False)
    other = swapped(lax.dynamic_index_in_dim(tiles, 1 - half, axis=1, keepdims=False))
    source = jnp.where(
        half == 0, jnp.stack([kept, other], axis=1), jnp.stack([other, kept], axis=1)
    )
    packed = call(
        pack_kernel,
        shape(2 * GX, PACK, COLS, dtype=BF16),
        (slot_count, adjoint, base_flow, slot_cell[0, 0], slot_marker[0, 0], slot_weight[0, 0]),
        scratch=(
            pltpu.SMEM((1, 1, 3, GX), I32),
            pltpu.VMEM(adjoint.shape, F32),
            pltpu.VMEM(base_flow.shape, BF16),
            pltpu.VMEM((3, GX, COLS), I32),
            pltpu.VMEM((3, GX, COLS), I32),
            pltpu.VMEM((3, GX, 16, COLS), F32),
            pltpu.SemaphoreType.DMA((6,)),
        ),
        spaces={n: HBM for n in range(6)},
        params=ROOMY,
    )
    got = lax.all_to_all(packed, whole, split_axis=0, concat_axis=0, tiled=True)
    field = shape(2, NCOL, NROW)
    thin = shape(2, 6, THIN, NROW)
    current, base, thin_far, thin_near = call(
        unpack_kernel, (field, field, thin, thin), (place, got, source), spaces={0: SMEM}
    )
    base_far, base_near = exchanged(thin_far, thin_near)
    ints, weights, table = call(
        slots_kernel,
        (
            shape(EMPTY + 1, 8, SPAN, dtype=I32),
            shape(EMPTY + 1, 16, SPAN),
            shape(128, dtype=I32),
        ),
        (got,),
        out_specs=(VMEM, VMEM, SMEM),
    )
    far, near = base_far, base_near
    part = shape(2, 2, 32, COLS)
    beyond = shape(2, 2, 16, COLS)
    rim = shape(2, 2, RIM, NROW, dtype=BF16)
    forces = source
    row_tables = col_tables = None
    for substep in range(SUBSTEPS):
        if substep == 0:
            inner = current
        else:
            inner = call(
                inner_kernel,
                field,
                (place, current, base_far, base, base_near),
                spaces={0: SMEM},
            )
        moved, sums, part_far, part_near, next_far, next_near = call(
            functools.partial(outer_kernel, substep == 0),
            (field, shape(2, 2, 48, COLS), part, part, beyond, beyond),
            (place, table, far, near, base_far, base, base_near, ints, weights, inner),
            scratch=OUTER_SCRATCH,
            spaces={0: SMEM, 1: SMEM},
        )
        beyond_far, beyond_near = exchanged(next_far, next_near, 2)
        from_far, from_near = exchanged(part_far, part_near)
        if substep == 0:
            row_tables, col_tables = call(
                tables_kernel,
                (
                    shape(EMPTY + 1, 4 * ROWS, SPAN),
                    shape(EMPTY + 1, 2 * SPAN, COLS, dtype=BF16),
                ),
                (table, ints, weights),
                spaces={0: SMEM},
            )
        current, edge_far, edge_near, forces = call(
            spread_kernel,
            (field, rim, rim, shape(2, 2, 16, COLS)),
            (
                place, table, sums, beyond_far, beyond_near, from_far, from_near, base_far,
                source, base_near, moved, ints, row_tables, col_tables,
            ),
            scratch=SPREAD_SCRATCH,
            spaces={0: SMEM, 1: SMEM},
        )
        far, near = exchanged(edge_far, edge_near)
    tiles_out = shape(2 * GX, 2, ROWS, COLS)
    inner = call(finish_inner_kernel, tiles_out, (place, current), spaces={0: SMEM})
    done = call(finish_outer_kernel, tiles_out, (place, far, near, inner), spaces={0: SMEM})
    back = lax.all_to_all(done, whole, split_axis=0, concat_axis=0, tiled=True)
    result = jnp.transpose(back, (1, 0, 2, 3))
    mine = lax.dynamic_index_in_dim(forces, half, axis=1, keepdims=False)
    theirs = swapped(lax.dynamic_index_in_dim(forces, 1 - half, axis=1, keepdims=False))
    planes = jnp.where(
        half == 0, jnp.stack([mine, theirs], axis=1), jnp.stack([theirs, mine], axis=1)
    )
    return (result, planes.reshape(marker_source.shape))


def solution(mesh):
    split = Mesh(mesh.devices.reshape(8, 2, 8), ("gx", "xh", "zc"))
    gy = ("xh", "zc")
    in_specs = (
        P(None, None, "gx", gy),
        P(None, None, "gx", gy),
        P("gx", gy, None, None, None),
        P("gx", gy, None, None, None),
        P("gx", gy, None, None),
        P("gx", gy, None, None, None, None),
        P(None, "gx", gy, None),
    )
    out_specs = (P(None, None, "gx", gy), P(None, "gx", gy, None))
    return jax.shard_map(
        on_device, mesh=split, in_specs=in_specs, out_specs=out_specs, check_vma=False
    )
```

```python
import functools

import jax
import jax.numpy as jnp
from jax import lax
from jax.experimental import pallas as pl
from jax.experimental.pallas import tpu as pltpu
from jax.sharding import Mesh, PartitionSpec as P

SUBSTEPS = 3
SWEEPS = 8

TIME_STEP = 0.5
VISCOSITY = 0.2
STIFFNESS = 2.0
BENDING = 0.25

F32 = jnp.float32
BF16 = jnp.bfloat16
I32 = jnp.int32

GX = 8
ROWS = 32
COLS = 128
NROW = GX * ROWS
NCOL = 2 * COLS
LAST = 7
RIM = 16
STRIP = 2 * RIM
THIN = 8
KEPT = 192
PACK = 304
SPAN = 128
TILES = 2 * GX
DEPTH = 3
EMPTY = TILES * DEPTH
COUNT_AT = 127
GROUP = 12

NT = (((1,), (1,)), ((), ()))
NN = (((1,), (0,)), ((), ()))

PARAMS = pltpu.CompilerParams(vmem_limit_bytes=24 * 1024 * 1024)
ROOMY = pltpu.CompilerParams(vmem_limit_bytes=60 * 1024 * 1024)
VMEM = pl.BlockSpec(memory_space=pltpu.VMEM)
SMEM = pl.BlockSpec(memory_space=pltpu.SMEM)
HBM = pl.BlockSpec(memory_space=pltpu.HBM)


def call(body, outs, ins, scratch=(), spaces=(), out_specs=None, params=PARAMS):
    spaces = dict(spaces)
    return pl.pallas_call(
        body,
        out_shape=outs,
        in_specs=[spaces.get(n, VMEM) for n in range(len(ins))],
        out_specs=out_specs or jax.tree.map(lambda _: VMEM, outs),
        scratch_shapes=list(scratch),
        compiler_params=params,
    )(*ins)


OUTER_SCRATCH = (
    pltpu.VMEM((TILES, 8 * ROWS, 2 * COLS), BF16),
    pltpu.VMEM((COLS, 2 * KEPT), F32),
) + tuple(pltpu.VMEM((8 * ROWS, SPAN), F32) for _ in range(GROUP))
SPREAD_SCRATCH = (
    pltpu.VMEM((KEPT, 2 * COLS), BF16),
    pltpu.VMEM((TILES, 8 * ROWS, COLS), F32),
)


def shape(*dims, dtype=F32):
    return jax.ShapeDtypeStruct(dims, dtype)


def exchanged(far, near, step=1):
    count = lax.axis_size("zc")
    ups = [(n, (n + step) % count) for n in range(count)]
    results = []
    for value, parity in ((far, 1), (near, 0)):
        pairs = [pair for pair in ups if (pair[0] // step) % 2 == parity]
        pairs = pairs + [(target, source) for source, target in pairs]
        results.append(lax.ppermute(value, "zc", pairs))
    return results


def swapped(value):
    return lax.ppermute(value, "xh", [(0, 1), (1, 0)])


def two_parts(value):
    high = value.astype(BF16)
    return high, (value - high.astype(F32)).astype(BF16)


def row_next(x):
    low, high = (pltpu.roll(half, COLS - 1, 1) for half in (x[:, :COLS], x[:, COLS:]))
    inner = lax.broadcasted_iota(I32, low.shape, 1) < COLS - 1
    return jnp.concatenate([jnp.where(inner, low, high), jnp.where(inner, high, 0.0)], axis=1)


def row_prev(x):
    low, high = (pltpu.roll(half, 1, 1) for half in (x[:, :COLS], x[:, COLS:]))
    inner = lax.broadcasted_iota(I32, low.shape, 1) > 0
    return jnp.concatenate([jnp.where(inner, low, 0.0), jnp.where(inner, high, low)], axis=1)


def col_next(x):
    return pltpu.roll(x, x.shape[0] - 1, 0)


def col_prev(x):
    return pltpu.roll(x, 1, 0)


def pack_kernel(
    count_hbm, adj_hbm, base_hbm, cell_hbm, mark_hbm, weight_hbm, out_ref,
    count_ref, adj_ref, base_ref, cell_ref, mark_ref, weight_ref, sems,
):
    copies = [
        pltpu.make_async_copy(src, dst, sems.at[n])
        for n, (src, dst) in enumerate(
            (
                (cell_hbm, cell_ref),
                (mark_hbm, mark_ref),
                (weight_hbm, weight_ref),
                (base_hbm, base_ref),
                (adj_hbm, adj_ref),
                (count_hbm, count_ref),
            )
        )
    ]
    for copy in copies:
        copy.start()
    copies[5].wait()
    copies[0].wait()
    copies[1].wait()
    lane = lax.broadcasted_iota(I32, (1, COLS), 1)
    none = jnp.zeros((4, COLS), F32)
    for e in range(GX):
        for q in range(2):
            rows = []
            for g in range(3):
                cell = cell_ref[g, e : e + 1, :]
                mark = mark_ref[g, e : e + 1, :]
                live = (lane < count_ref[0, 0, g, e]) & ((mark >> 11) == q)
                rows += [cell >> 7, cell & 127, jnp.where(live, (mark >> 7) & 15, -1), mark & 127]
            ints = jnp.concatenate([r.astype(F32) for r in rows] + [none], axis=0)
            out_ref[2 * e + q, 288:304, :] = ints.astype(BF16)
    copies[2].wait()
    for e in range(GX):
        for g in range(3):
            hi, lo = two_parts(weight_ref[g, e])
            for q in range(2):
                out_ref[2 * e + q, 192 + 16 * g : 208 + 16 * g, :] = hi
                out_ref[2 * e + q, 240 + 16 * g : 256 + 16 * g, :] = lo
    copies[3].wait()
    for p in range(2 * GX):
        for c in range(2):
            out_ref[p, 128 + c * ROWS : 128 + (c + 1) * ROWS, :] = base_ref[c, p]
    copies[4].wait()
    for p in range(2 * GX):
        for c in range(2):
            hi, lo = two_parts(adj_ref[c, p])
            out_ref[p, c * ROWS : (c + 1) * ROWS, :] = hi
            out_ref[p, 64 + c * ROWS : 64 + (c + 1) * ROWS, :] = lo


def closed_up(blocks):
    lane = lax.broadcasted_iota(I32, (1, 1, SPAN), 2)
    spot = lax.broadcasted_iota(I32, (1, 24, SPAN), 1)
    blank = jnp.where(spot == 20, -1.0, 0.0)
    for bit in range(9):
        step = 1 << bit
        goes = []
        stays = []
        for x in blocks:
            away = x[:, 20:21, :].astype(I32)
            flag = (away >> bit) & 1
            goes.append(jnp.where((away >= 0) & (flag == 1), 1.0, 0.0))
            stays.append((away >= 0) & (flag == 0))

        def ahead(values, n):
            if step >= SPAN:
                m = n + step // SPAN
                return values[m] if m < len(values) else None
            here = pltpu.roll(values[n], SPAN - step, 2)
            if n + 1 < len(values):
                there = pltpu.roll(values[n + 1], SPAN - step, 2)
            else:
                there = jnp.zeros_like(here)
            return jnp.where(lane < SPAN - step, here, there)

        result = []
        for n, x in enumerate(blocks):
            kept = jnp.where(stays[n], x, blank)
            coming = ahead(goes, n)
            if coming is None:
                result.append(kept)
            else:
                result.append(jnp.where(coming > 0.5, ahead(blocks, n), kept))
        blocks = result
    return blocks


def unpack_kernel(place_ref, got_ref, source_ref, adj_ref, base_ref, far_ref, near_ref):
    place = place_ref[0]
    for n in range(4):
        for side in range(2):
            parts = []
            for a in range(GX):
                d = 2 * a + side
                at = (n % 2) * ROWS
                if n < 2:
                    part = got_ref[d, at : at + ROWS, :].astype(F32)
                    part = part + got_ref[d, 64 + at : 64 + at + ROWS, :].astype(F32)
                else:
                    part = got_ref[d, 128 + at : 128 + at + ROWS, :].astype(F32)
                parts.append(part)
            turned = jnp.concatenate(parts, axis=0).T
            ref = adj_ref if n < 2 else base_ref
            ref[n % 2, side * COLS : (side + 1) * COLS, :] = turned
            far_ref[side, n], near_ref[side, n] = turned_round(
                place, turned[:THIN], turned[COLS - THIN :]
            )
    for c in range(2):
        for side in range(2):
            both = jnp.concatenate(
                [source_ref[c, side, 0:8, :], source_ref[c, side, 8:16, :]], axis=1
            )
            far_ref[side, 4 + c] = both
            near_ref[side, 4 + c] = both


def slots_kernel(got_ref, ints_ref, weight_ref, table_ref):
    ints = got_ref[:, 288:304, :].astype(F32)
    across = lax.broadcasted_iota(I32, (SPAN, SPAN), 0) <= lax.broadcasted_iota(
        I32, (SPAN, SPAN), 1
    )
    across = jnp.where(across, 1.0, 0.0).astype(BF16)
    live = []
    ranks = []
    total = jnp.zeros((TILES, SPAN), F32)
    for g in range(3):
        alive = jnp.where(ints[:, 4 * g + 2, :] >= 0.0, 1.0, 0.0)
        bits = alive.astype(BF16)
        live.append(alive)
        ranks.append(
            total + lax.dot_general(bits, across, NN, preferred_element_type=F32)
        )
        total = total + lax.dot_general(
            bits, jnp.ones((SPAN, SPAN), BF16), NN, preferred_element_type=F32
        )
    filled = jnp.int32(0)
    here = [
        (jnp.max(total[d : d + 1]).astype(I32) + SPAN - 1) // SPAN for d in range(TILES)
    ]
    for d in range(TILES):
        for n in range(DEPTH):

            @pl.when(n < here[d])
            def _():
                table_ref[filled + n] = d * DEPTH + n

        filled = filled + here[d]
    for n in range(GROUP):
        table_ref[filled + n] = EMPTY
    table_ref[COUNT_AT] = filled
    lane = lax.broadcasted_iota(I32, (TILES, SPAN), 1).astype(F32)
    spot = lax.broadcasted_iota(I32, (TILES, 8, SPAN), 1)
    side = (lax.broadcasted_iota(I32, (TILES, 1, SPAN), 0) & 1).astype(F32)
    blocks = []
    for g in range(3):
        away = jnp.where(live[g] > 0.5, lane + float(g * SPAN + 1) - ranks[g], -1.0)
        weights = got_ref[:, 192 + 16 * g : 208 + 16 * g, :].astype(F32)
        weights = weights + got_ref[:, 240 + 16 * g : 256 + 16 * g, :].astype(F32)
        rows = [ints[:, 4 * g + n : 4 * g + n + 1, :] for n in range(4)]
        rows[2] = rows[2] + 48.0 * side + float(16 * g)
        rest = jnp.zeros((TILES, 8, SPAN), F32)
        for n, row in enumerate(rows + [away[:, None, :]]):
            rest = jnp.where(spot == n, row, rest)
        blocks.append(jnp.concatenate([weights, rest], axis=1))
    for n, block in enumerate(closed_up(blocks)):
        for d in range(TILES):
            weight_ref[d * DEPTH + n] = block[d, :16]
            ints_ref[d * DEPTH + n] = block[d, 16:].astype(I32)
    weight_ref[EMPTY] = jnp.zeros((16, SPAN), F32)
    ints_ref[EMPTY] = jnp.zeros((8, SPAN), I32)


def one_hot(index, count):
    spot = lax.broadcasted_iota(I32, (count, index.shape[1]), 0)
    return jnp.where(spot == index, 1.0, 0.0).astype(BF16)


def row_weights(first_row, weights):
    off = lax.broadcasted_iota(I32, (ROWS, SPAN), 0) - first_row
    hits = [off == n for n in range(4)]
    tables = []
    for dj in range(4):
        table = jnp.zeros((ROWS, SPAN), F32)
        for di in (3, 2, 1, 0):
            row = weights[4 * di + dj : 4 * di + dj + 1]
            table = jnp.where(hits[di], row, table)
        tables.append(table)
    return tables


def over_blocks(table_ref, body):
    def run(n, carry):
        ids = [table_ref[GROUP * n + m] for m in range(GROUP)]
        body(ids, [jnp.minimum(block // DEPTH, TILES - 1) for block in ids])
        return carry

    lax.fori_loop(0, (table_ref[COUNT_AT] + GROUP - 1) // GROUP, run, 0)


def joined(ref, ids, row):
    return jnp.concatenate([ref[block, row : row + 1, :] for block in ids], axis=1)


def turned_round(place, one, other):
    odd = (place & 1) == 1
    return jnp.where(odd, other, one), jnp.where(odd, one, other)


def neighbours(place):
    return jnp.where(place == 0, 0.0, 1.0), jnp.where(place == LAST, 0.0, 1.0)


def meeting(place, low, high, reach=1):
    start = place < reach
    end = place > LAST - reach
    has_low = jnp.where(start, 0.0, 1.0)
    has_high = jnp.where(end, 0.0, 1.0)
    lows = (low[0] * has_low, jnp.where(start, low[0], low[1]))
    highs = (jnp.where(end, high[1], high[0]), high[1] * has_high)
    return lows, highs


def masked(place):
    has_low, has_high = neighbours(place)

    def inside(x):
        width = x.shape[0]
        return jnp.concatenate(
            [x[:RIM] * has_low, x[RIM : width - RIM], x[width - RIM :] * has_high], axis=0
        )

    return inside


def projected(wide, inside, looped=False):
    div = 0.5 * (row_next(wide[0]) - row_prev(wide[0])) + 0.5 * (
        col_next(wide[1]) - col_prev(wide[1])
    )
    pressure = inside(-0.25 * div)

    def sweep(_, p):
        return inside(0.25 * (row_next(p) + row_prev(p) + col_next(p) + col_prev(p) - div))

    if looped:
        pressure = lax.fori_loop(0, SWEEPS - 1, sweep, pressure)
    else:
        for n in range(SWEEPS - 1):
            pressure = sweep(n, pressure)
    first = wide[0] - 0.5 * (row_next(pressure) - row_prev(pressure))
    second = wide[1] - 0.5 * (col_next(pressure) - col_prev(pressure))
    return inside(first), inside(second)


def strips(lows, highs, mid_ref, c):
    parts = []
    for side in range(2):
        at = side * COLS
        if mid_ref is None:
            inner = [jnp.zeros((RIM, NROW), F32)] * 2
        else:
            inner = [
                mid_ref[c, at : at + RIM, :],
                mid_ref[c, at + COLS - RIM : at + COLS, :],
            ]
        parts += [lows[side], inner[0], inner[1], highs[side]]
    return jnp.concatenate(parts, axis=0)


def rim_strips(place, far_ref, near_ref):
    result = []
    for c in range(2):
        pairs = [
            turned_round(place, far_ref[side, c].astype(F32), near_ref[side, c].astype(F32))
            for side in range(2)
        ]
        result.append(strips(*meeting(place, *zip(*pairs)), None, c))
    return result


def thin_rims(place, far, near, at):
    pairs = [turned_round(place, far[side, at], near[side, at]) for side in range(2)]
    return meeting(place, *zip(*pairs))


def outer_columns(x, side):
    at = side * 2 * STRIP
    return x[at + RIM : at + 2 * RIM], x[at + STRIP : at + STRIP + RIM]


def widened(mid_ref, c, lows, highs):
    parts = []
    for side in range(2):
        parts += [lows[side], mid_ref[c, side * COLS : (side + 1) * COLS, :], highs[side]]
    return jnp.concatenate(parts, axis=0)


def wide_projected(place, mid_ref):
    blank = (jnp.zeros((RIM, NROW), F32),) * 2
    wide = [widened(mid_ref, c, blank, blank) for c in range(2)]
    return projected(wide, masked(place), looped=True)


def transported(w, base):
    ux = 0.5 * (row_next(base[0]) - row_prev(base[0]))
    vx = 0.5 * (row_next(base[1]) - row_prev(base[1]))
    uy = 0.5 * (col_next(base[0]) - col_prev(base[0]))
    vy = 0.5 * (col_next(base[1]) - col_prev(base[1]))
    mixed = (ux * w[0] + vx * w[1], uy * w[0] + vy * w[1])
    out = []
    for c in range(2):
        east, west = row_next(w[c]), row_prev(w[c])
        north, south = col_next(w[c]), col_prev(w[c])
        laplace = east + west + north + south - 4.0 * w[c]
        value = w[c] + TIME_STEP * (
            base[0] * (0.5 * (east - west))
            + base[1] * (0.5 * (north - south))
            - mixed[c]
            + VISCOSITY * laplace
        )
        out.append(value)
    return out


def interpolate(table_ref, ints_ref, weight_ref, pick_ref, got_refs, sum_ref):
    def blocks(ids, tiles):
        for block, tile, got_ref in zip(ids, tiles, got_refs):
            cols = one_hot(ints_ref[block, 1:2, :], COLS)
            got_ref[...] = lax.dot_general(
                pick_ref[tile],
                jnp.concatenate([cols, cols], axis=0),
                NN,
                preferred_element_type=F32,
            )
        values = []
        for block, got_ref in zip(ids, got_refs):
            tables = row_weights(ints_ref[block, 0:1, :], weight_ref[block])
            both = []
            for c in range(2):
                total = jnp.zeros((ROWS, SPAN), F32)
                for dj in range(4):
                    at = (dj * 2 + c) * ROWS
                    total = total + tables[dj] * got_ref[at : at + ROWS, :]
                both.append(jnp.sum(total, axis=0, keepdims=True))
            values.append(both)
        high = lax.broadcasted_iota(I32, (96, len(ids) * SPAN), 0) == joined(ints_ref, ids, 2)
        parts = [two_parts(jnp.concatenate([v[c] for v in values], axis=1)) for c in range(2)]
        stacked = jnp.concatenate(
            [
                jnp.where(high, parts[c][k].astype(F32), 0.0).astype(BF16)
                for k in range(2)
                for c in range(2)
            ],
            axis=0,
        )
        both = lax.dot_general(
            one_hot(joined(ints_ref, ids, 3), COLS), stacked, NT, preferred_element_type=F32
        )
        sum_ref[...] = sum_ref[...] + both

    sum_ref[...] = jnp.zeros(sum_ref.shape, F32)
    over_blocks(table_ref, blocks)


def pick(field, c, side, pick_ref):
    for dj in range(4):
        shifted = pltpu.roll(field, COLS - dj, 1) if dj else field
        both = jnp.concatenate(two_parts(shifted), axis=1)
        at = (dj * 2 + c) * ROWS
        for a in range(GX):
            pick_ref[2 * a + side, at : at + ROWS, :] = both[a * ROWS : (a + 1) * ROWS]


def first_inner_kernel(mid_ref, base_ref, moved_ref):
    w = [mid_ref[c] for c in range(2)]
    out = transported(w, [base_ref[c] for c in range(2)])
    for c in range(2):
        moved_ref[c] = out[c]


def inner_kernel(place_ref, mid_ref, base_far_ref, base_ref, base_near_ref, moved_ref):
    place = place_ref[0]
    extra = RIM - THIN
    length = COLS + 2 * RIM
    w = [
        jnp.concatenate([x[extra : length - extra], x[length + extra : 2 * length - extra]], axis=0)
        for x in wide_projected(place, mid_ref)
    ]
    base = [
        widened(base_ref, c, *thin_rims(place, base_far_ref, base_near_ref, 2 + c))
        for c in range(2)
    ]
    out = transported(w, base)
    for c in range(2):
        for side in range(2):
            at = side * (COLS + 2 * THIN) + THIN
            moved_ref[c, side * COLS : (side + 1) * COLS, :] = out[c][at : at + COLS]


def outer_kernel(
    first, place_ref, table_ref, far_ref, mid_ref, near_ref, base_far_ref, base_ref,
    base_near_ref, ints_ref, weight_ref, inner_ref, moved_ref, own_ref, part_far, part_near,
    next_far, next_near, pick_ref, sum_ref, *got_refs,
):
    place = place_ref[0]
    blank = jnp.zeros((RIM - THIN, NROW), F32)

    def thin_strips(far, mid, near, c, at):
        lows, highs = thin_rims(place, far, near, at + c)
        return strips(
            [jnp.concatenate([blank, x], axis=0) for x in lows],
            [jnp.concatenate([x, blank], axis=0) for x in highs],
            mid,
            c,
        )

    base = [thin_strips(base_far_ref, base_ref, base_near_ref, c, 2) for c in range(2)]
    if first:
        w = [thin_strips(far_ref, mid_ref, near_ref, c, 0) for c in range(2)]
    else:
        w = projected(rim_strips(place, far_ref, near_ref), masked(place))
    out = transported(w, base)
    spot = lax.broadcasted_iota(I32, (RIM, NROW), 0)
    for c in range(2):
        for side in range(2):
            low, high = outer_columns(out[c], side)
            at = side * COLS
            old_low = inner_ref[c, at : at + RIM, :]
            old_high = inner_ref[c, at + COLS - RIM : at + COLS, :]
            if first:
                low = jnp.where(spot == 0, low, old_low)
                high = jnp.where(spot == RIM - 1, high, old_high)
            else:
                low = old_low + low
                high = old_high + high
            moved = jnp.concatenate(
                [low, inner_ref[c, at + RIM : at + COLS - RIM, :], high], axis=0
            )
            moved_ref[c, at : at + COLS, :] = moved
            pick(moved.T, c, side, pick_ref)
    interpolate(table_ref, ints_ref, weight_ref, pick_ref, got_refs, sum_ref)
    sums = sum_ref[...].T
    sums = sums[:KEPT] + sums[KEPT:]
    for c in range(2):
        for side in range(2):
            at = (2 * c + side) * 48
            one = sums[at : at + 48]
            own_ref[c, side] = one
            part_far[side, c], part_near[side, c] = turned_round(place, one[:32], one[16:])
            next_far[side, c], next_near[side, c] = turned_round(place >> 1, one[:16], one[32:])


def tables_kernel(table_ref, ints_ref, weight_ref, rows_ref, cols_ref):
    def blocks(ids, tiles):
        for block in ids:
            rows_ref[block] = jnp.concatenate(
                row_weights(ints_ref[block, 0:1, :], weight_ref[block]), axis=0
            )
            spot = lax.broadcasted_iota(I32, (COLS, SPAN), 0)
            hits = jnp.where(spot == ints_ref[block, 1:2, :], 1.0, 0.0).T.astype(BF16)
            cols_ref[block] = jnp.concatenate([hits, hits], axis=0)

    rows_ref[EMPTY] = jnp.zeros((4 * ROWS, SPAN), F32)
    cols_ref[EMPTY] = jnp.zeros((2 * SPAN, COLS), BF16)
    over_blocks(table_ref, blocks)


def force_of(sums, source):
    row = lax.broadcasted_iota(I32, sums.shape, 0) & 3
    lane = lax.broadcasted_iota(I32, sums.shape, 1)
    count = sums.shape[0]
    up = jnp.where(row == 0, pltpu.roll(sums, count - 3, 0), pltpu.roll(sums, 1, 0))
    down = jnp.where(row == 3, pltpu.roll(sums, 3, 0), pltpu.roll(sums, count - 1, 0))
    before = jnp.where(lane == 0, pltpu.roll(up, 1, 1), pltpu.roll(sums, 1, 1))
    after = jnp.where(lane == 127, pltpu.roll(down, 127, 1), pltpu.roll(sums, 127, 1))
    bent = before + after - 2.0 * sums
    return STIFFNESS * (sums + source - BENDING * bent)


def spread_kernel(
    place_ref, table_ref, sums_ref, beyond_far, beyond_near, from_far, from_near, thin_far,
    source_ref, thin_near, moved_ref, ints_ref, row_ref, col_ref, out_ref, edge_far, edge_near, own_ref,
    force_ref, acc_ref,
):
    place = place_ref[0]

    def unfolded(ref, side, c):
        return jnp.concatenate([ref[side, 4 + c, :, :COLS], ref[side, 4 + c, :, COLS:]], axis=0)

    for c in range(2):
        pairs = [turned_round(place, from_far[s, c], from_near[s, c]) for s in range(2)]
        lows, highs = meeting(place, *zip(*pairs))
        pairs = [turned_round(place >> 1, beyond_far[s, c], beyond_near[s, c]) for s in range(2)]
        lows2, highs2 = meeting(place, *zip(*pairs), reach=2)
        pairs = [
            turned_round(place, unfolded(thin_far, s, c), unfolded(thin_near, s, c))
            for s in range(2)
        ]
        source_lows, source_highs = meeting(place, *zip(*pairs))
        for side in range(2):
            sums = sums_ref[c, side] + jnp.concatenate(
                [
                    lows[side][:16] + lows2[side],
                    lows[side][16:] + highs[side][:16],
                    highs[side][16:] + highs2[side],
                ],
                axis=0,
            )
            source = jnp.concatenate(
                [source_lows[side], source_ref[c, side], source_highs[side]], axis=0
            )
            force = force_of(sums, source)
            own_ref[c, side] = force[16:32]
            at = (2 * c + side) * 48
            force_ref[at : at + 48, :] = jnp.concatenate(two_parts(force), axis=1)
    acc_ref[...] = jnp.zeros(acc_ref.shape, F32)

    def blocks(ids, tiles):
        spots = one_hot(joined(ints_ref, ids, 3), COLS)
        picked = lax.dot_general(
            force_ref[...], jnp.concatenate([spots, spots], axis=0), NN,
            preferred_element_type=F32,
        )
        high = lax.broadcasted_iota(I32, (96, len(ids) * SPAN), 0) == joined(ints_ref, ids, 2)
        forces = [
            TIME_STEP
            * jnp.sum(jnp.where(high, picked[96 * c : 96 * c + 96], 0.0), axis=0, keepdims=True)
            for c in range(2)
        ]
        sums = []
        for m, block in enumerate(ids):
            lanes = slice(m * SPAN, (m + 1) * SPAN)
            weighted = jnp.concatenate(
                [row_ref[block] * forces[c][:, lanes] for c in range(2)], axis=0
            )
            sums.append(
                lax.dot_general(
                    jnp.concatenate(two_parts(weighted), axis=1),
                    col_ref[block],
                    NN,
                    preferred_element_type=F32,
                )
            )
        for tile, one in zip(tiles, sums):
            acc_ref[tile] = acc_ref[tile] + one

    over_blocks(table_ref, blocks)
    for c in range(2):
        for side in range(2):
            rows = []
            for a in range(GX):
                total = jnp.zeros((ROWS, COLS), F32)
                for dj in range(4):
                    at = (4 * c + dj) * ROWS
                    one = acc_ref[2 * a + side, at : at + ROWS, :]
                    total = total + (pltpu.roll(one, dj, 1) if dj else one)
                rows.append(total)
            cols = slice(side * COLS, (side + 1) * COLS)
            total = moved_ref[c, cols, :] + jnp.concatenate(rows, axis=0).T
            out_ref[c, cols, :] = total
            far, near = turned_round(place, total[:RIM], total[COLS - RIM :])
            edge_far[side, c] = far.astype(BF16)
            edge_near[side, c] = near.astype(BF16)


def finish_inner_kernel(place_ref, mid_ref, out_ref):
    w = wide_projected(place_ref[0], mid_ref)
    for c in range(2):
        for side in range(2):
            at = side * (COLS + 2 * RIM) + RIM
            block = w[c][at : at + COLS].T
            for a in range(GX):
                out_ref[2 * a + side, c] = block[a * ROWS : (a + 1) * ROWS]


def finish_outer_kernel(place_ref, far_ref, near_ref, inner_ref, out_ref):
    place = place_ref[0]
    w = projected(rim_strips(place, far_ref, near_ref), masked(place))
    blank = jnp.zeros((COLS - 2 * RIM, NROW), F32)
    for c in range(2):
        for side in range(2):
            low, high = outer_columns(w[c], side)
            both = jnp.concatenate([low, blank, high], axis=0).T
            for a in range(GX):
                out_ref[2 * a + side, c] = (
                    inner_ref[2 * a + side, c] + both[a * ROWS : (a + 1) * ROWS]
                )


def on_device(adjoint, base_flow, slot_cell, slot_marker, slot_count, slot_weight, marker_source):
    place = lax.axis_index("zc").astype(I32).reshape(1)
    half = lax.axis_index("xh")
    whole = ("gx", "xh")
    tiles = marker_source.reshape(2, 2, 16, COLS)
    kept = lax.dynamic_index_in_dim(tiles, half, axis=1, keepdims=False)
    other = swapped(lax.dynamic_index_in_dim(tiles, 1 - half, axis=1, keepdims=False))
    source = jnp.where(
        half == 0, jnp.stack([kept, other], axis=1), jnp.stack([other, kept], axis=1)
    )
    packed = call(
        pack_kernel,
        shape(2 * GX, PACK, COLS, dtype=BF16),
        (slot_count, adjoint, base_flow, slot_cell[0, 0], slot_marker[0, 0], slot_weight[0, 0]),
        scratch=(
            pltpu.SMEM((1, 1, 3, GX), I32),
            pltpu.VMEM(adjoint.shape, F32),
            pltpu.VMEM(base_flow.shape, BF16),
            pltpu.VMEM((3, GX, COLS), I32),
            pltpu.VMEM((3, GX, COLS), I32),
            pltpu.VMEM((3, GX, 16, COLS), F32),
            pltpu.SemaphoreType.DMA((6,)),
        ),
        spaces={n: HBM for n in range(6)},
        params=ROOMY,
    )
    got = lax.all_to_all(packed, whole, split_axis=0, concat_axis=0, tiled=True)
    field = shape(2, NCOL, NROW)
    thin = shape(2, 6, THIN, NROW)
    current, base, thin_far, thin_near = call(
        unpack_kernel, (field, field, thin, thin), (place, got, source), spaces={0: SMEM}
    )
    base_far, base_near = exchanged(thin_far, thin_near)
    ints, weights, table = call(
        slots_kernel,
        (
            shape(EMPTY + 1, 8, SPAN, dtype=I32),
            shape(EMPTY + 1, 16, SPAN),
            shape(128, dtype=I32),
        ),
        (got,),
        out_specs=(VMEM, VMEM, SMEM),
    )
    far, near = base_far, base_near
    part = shape(2, 2, 32, COLS)
    beyond = shape(2, 2, 16, COLS)
    rim = shape(2, 2, RIM, NROW, dtype=BF16)
    forces = source
    row_tables = col_tables = None
    for substep in range(SUBSTEPS):
        if substep == 0:
            inner = call(first_inner_kernel, field, (current, base))
        else:
            inner = call(
                inner_kernel,
                field,
                (place, current, base_far, base, base_near),
                spaces={0: SMEM},
            )
        moved, sums, part_far, part_near, next_far, next_near = call(
            functools.partial(outer_kernel, substep == 0),
            (field, shape(2, 2, 48, COLS), part, part, beyond, beyond),
            (place, table, far, current, near, base_far, base, base_near, ints, weights, inner),
            scratch=OUTER_SCRATCH,
            spaces={0: SMEM, 1: SMEM},
        )
        beyond_far, beyond_near = exchanged(next_far, next_near, 2)
        from_far, from_near = exchanged(part_far, part_near)
        if substep == 0:
            row_tables, col_tables = call(
                tables_kernel,
                (
                    shape(EMPTY + 1, 4 * ROWS, SPAN),
                    shape(EMPTY + 1, 2 * SPAN, COLS, dtype=BF16),
                ),
                (table, ints, weights),
                spaces={0: SMEM},
            )
        current, edge_far, edge_near, forces = call(
            spread_kernel,
            (field, rim, rim, shape(2, 2, 16, COLS)),
            (
                place, table, sums, beyond_far, beyond_near, from_far, from_near, base_far,
                source, base_near, moved, ints, row_tables, col_tables,
            ),
            scratch=SPREAD_SCRATCH,
            spaces={0: SMEM, 1: SMEM},
        )
        far, near = exchanged(edge_far, edge_near)
    tiles_out = shape(2 * GX, 2, ROWS, COLS)
    inner = call(finish_inner_kernel, tiles_out, (place, current), spaces={0: SMEM})
    done = call(finish_outer_kernel, tiles_out, (place, far, near, inner), spaces={0: SMEM})
    back = lax.all_to_all(done, whole, split_axis=0, concat_axis=0, tiled=True)
    result = jnp.transpose(back, (1, 0, 2, 3))
    mine = lax.dynamic_index_in_dim(forces, half, axis=1, keepdims=False)
    theirs = swapped(lax.dynamic_index_in_dim(forces, 1 - half, axis=1, keepdims=False))
    planes = jnp.where(
        half == 0, jnp.stack([mine, theirs], axis=1), jnp.stack([theirs, mine], axis=1)
    )
    return (result, planes.reshape(marker_source.shape))


def solution(mesh):
    split = Mesh(mesh.devices.reshape(8, 2, 8), ("gx", "xh", "zc"))
    gy = ("xh", "zc")
    in_specs = (
        P(None, None, "gx", gy),
        P(None, None, "gx", gy),
        P("gx", gy, None, None, None),
        P("gx", gy, None, None, None),
        P("gx", gy, None, None),
        P("gx", gy, None, None, None, None),
        P(None, "gx", gy, None),
    )
    out_specs = (P(None, None, "gx", gy), P(None, "gx", gy, None))
    return jax.shard_map(
        on_device, mesh=split, in_specs=in_specs, out_specs=out_specs, check_vma=False
    )
```
